128 devices in a mesh: gx: 16 (over z, x), gy: 8 (over y, core).
Axes of the slice: x: 4, y: 4, z: 4, core: 2. Of those that a mesh axis runs over, the one named last changes fastest.
Arguments:
- fine_feats: bfloat16 [24576, 8, 512], P(('gx', 'gy')), may hold values from -6 to 6
- owner_of: int32 [24576], P(('gx', 'gy')), may hold values from 0 to 127, as said below
- arrival_slot: int32 [98304], P(('gx', 'gy')), may hold values from -1 to 383, as said below
- w_stride: bfloat16 [512, 128], replicated, may hold values from -0.25 to 0.25
- w_conv: bfloat16 [27, 128, 128], replicated, may hold values from -0.109375 to 0.109375
- w_head: bfloat16 [128, 8], replicated, may hold values from -4 to 4
- labels: int32 [128, 64, 48], P('gx', 'gy'), may hold values from 0 to 7
Outputs:
- grad_fine: bfloat16 [24576, 8, 512], P(('gx', 'gy'))
- grad_stride: float32 [512, 128], replicated
- grad_conv: float32 [27, 128, 128], replicated
The draws below stay inside these ranges and needn't reach their ends.
Inputs may be any that keep to these rules, and one draw needn't show every extreme that they name: `owner_of`: one device's rows name one owner at most 6 times, and some device reaches 6. `arrival_slot`: entry d * 128 * 6 + s * 6 + p is the slot (0 to 383) of the p-th fine brick that device s sends to owner d, in row order, and -1 where s sends fewer; one owner's slots are distinct, and some owner fills all of its slots.
All inputs are finite; a program needn't handle non-finite values.
Results may differ from the reference program's by a relative error of at most 0.012.
Values may be sent and summed in bfloat16 or wider, within the bound.
No kernel may reach another device: no remote copies, remote signals or barrier semaphores. Data moves between devices by JAX's collectives and lax.ppermute only.
A program may use at most 128 MiB of HBM per device.

```python
import math
import jax
import jax.numpy as jnp
from jax import lax

CF = 64
CC = 128
BR = 4
NCLS = 8
BX = 2
BY = 2
F_DEV = 192
CAP = 6
BZ = 12
HB = 2
FINE = 24576
NXC = 128
NYC = 64
NZC = 48
N_GX = 16
N_GY = 8
DEVICES = 128


def plan_layout(key):
    dev_count = DEVICES
    per_dev = F_DEV
    pair_cap = CAP
    full_count = per_dev // (2 * pair_cap)
    half_count = per_dev // pair_cap
    shift_by = full_count + half_count
    key_order, key_group, key_shuffle, key_slots = jax.random.split(key, 4)
    owner_order = jax.random.permutation(key_order, dev_count)
    places = jnp.arange(dev_count, dtype=jnp.int32)
    levels = jnp.where(places < full_count, pair_cap, jnp.where(places < shift_by, pair_cap // 2, 0)).astype(jnp.int32)
    level_first = jnp.zeros((dev_count,), jnp.int32).at[owner_order].set(levels)
    level_second = jnp.zeros((dev_count,), jnp.int32).at[owner_order].set(levels[(places + shift_by) % dev_count])
    in_first = jax.random.permutation(key_group, dev_count) < dev_count // 2
    counts = jnp.where(in_first[:, None], level_first[None, :], level_second[None, :])
    bounds = jnp.cumsum(counts, axis=1)
    records = jnp.arange(per_dev, dtype=jnp.int32)
    sorted_dest = jnp.sum((bounds[:, None, :] <= records[None, :, None]).astype(jnp.int32), axis=2)
    shuffles = jax.vmap(lambda subkey: jax.random.permutation(subkey, per_dev))(jax.random.split(key_shuffle, dev_count))
    destination = jnp.take_along_axis(sorted_dest, shuffles, axis=1)
    matches = (destination[:, :, None] == places[None, None, :]).astype(jnp.int32)
    position = jnp.sum(jnp.cumsum(matches, axis=1) * matches, axis=2) - 1
    offsets = jnp.cumsum(counts, axis=0) - counts
    arrive_rank = jnp.take_along_axis(offsets, destination, axis=1) + position
    slot_count = dev_count * pair_cap // 2
    slot_perms = jax.vmap(lambda subkey: jax.random.permutation(subkey, slot_count))(jax.random.split(key_slots, dev_count))
    chosen_slot = slot_perms[destination, arrive_rank].astype(jnp.int32)
    sources = jnp.broadcast_to(places[:, None], (dev_count, per_dev))
    landing = destination * (dev_count * pair_cap) + sources * pair_cap + position
    arrival = jnp.full((dev_count * dev_count * pair_cap,), -1, jnp.int32).at[landing.reshape(-1)].set(chosen_slot.reshape(-1))
    return (destination.reshape(-1).astype(jnp.int32), arrival)


def draw_owner_of(key, part):
    return plan_layout(key)[0]


def draw_arrival_slot(key, part):
    return plan_layout(key)[1]


def set_ends(result, own_key, smallest, high):
    longest = result.shape.index(max(result.shape))
    spots = []
    for shift in (0, 1):
        where = [jax.random.randint(jax.random.fold_in(own_key, axis), (), 0, length) for axis, length in enumerate(result.shape)]
        where[longest] = (where[longest] + shift) % result.shape[longest]
        spots.append(tuple(where))
    return result.at[spots[0]].set(smallest).at[spots[1]].set(high)


def shard_levels(rng, extent, shards, smallest, largest):
    loudness, own = 1.0, jax.random.fold_in(rng, 6)
    for dim, shards_of in shards:
        heights = jnp.exp(jax.random.uniform(jax.random.fold_in(own, dim), (shards_of,), jnp.float32, smallest / len(shards), largest / len(shards)))
        loudness = loudness * jnp.repeat(heights, extent[dim] // shards_of).reshape([-1 if axis == dim else 1 for axis in range(len(extent))])
    return loudness


def gaussian(own_key, dims, width, most, cuts=(), kind=jnp.bfloat16):
    gain = shard_levels(own_key, dims, cuts, -0.22, 0.18) if cuts else 1.0
    result = jax.random.normal(own_key, dims, jnp.float32) * width * gain
    return jnp.minimum(jnp.maximum(result, -most), most).astype(kind)


def setup_inputs(seed: int = 0) -> dict:
    seeds = jax.random.split(jax.random.key(seed), 8)
    fine_feats = gaussian(seeds[0], (FINE, HB**3, 8 * CF), 1.0, 6.0, ((0, 128),))
    owner_of = draw_owner_of(jax.random.fold_in(seeds[7], 71), 0)
    arrival_slot = draw_arrival_slot(jax.random.fold_in(seeds[7], 71), 0)
    w_stride = gaussian(seeds[3], (8 * CF, CC), (8 * CF) ** -0.5, 0.25)
    w_conv = gaussian(seeds[4], (27, CC, CC), (27 * CC) ** -0.5, 0.109375)
    w_head = gaussian(seeds[5], (CC, NCLS), 1.0, 4.0)
    labels = set_ends(jax.random.randint(seeds[6], (NXC, NYC, NZC), 0, NCLS), jax.random.fold_in(seeds[6], 1), 0, NCLS - 1).astype(jnp.int32)
    return dict(fine_feats=fine_feats, owner_of=owner_of, arrival_slot=arrival_slot, w_stride=w_stride, w_conv=w_conv, w_head=w_head, labels=labels)


def conv_block(padded, kernel):
    size_x = padded.shape[0] - 2
    size_y = padded.shape[1] - 2
    depth = padded.shape[2]
    chans = padded.shape[3]
    deep_pad = jnp.pad(padded, ((0, 0), (0, 0), (1, 1), (0, 0)))
    total = jnp.zeros((size_x * size_y * depth, kernel.shape[2]), jnp.float32)
    for along_x in range(3):
        for along_y in range(3):
            window = deep_pad[along_x:along_x + size_x, along_y:along_y + size_y]
            stacked = jnp.concatenate([window[:, :, shift_z:shift_z + depth] for shift_z in range(3)], axis=3)
            total = total + jnp.dot(stacked.reshape(-1, 3 * chans), kernel[along_x * 3 + along_y], preferred_element_type=jnp.float32)
    return total.reshape(size_x, size_y, depth, kernel.shape[2])

def weight_grad(padded, grad_pre):
    size_x = padded.shape[0] - 2
    size_y = padded.shape[1] - 2
    depth = padded.shape[2]
    chans = padded.shape[3]
    deep_pad = jnp.pad(padded, ((0, 0), (0, 0), (1, 1), (0, 0)))
    flat_grad = grad_pre.reshape(-1, grad_pre.shape[3])
    pieces = []
    for along_x in range(3):
        for along_y in range(3):
            window = deep_pad[along_x:along_x + size_x, along_y:along_y + size_y]
            stacked = jnp.concatenate([window[:, :, shift_z:shift_z + depth] for shift_z in range(3)], axis=3)
            pieces.append(lax.dot_general(stacked.reshape(-1, 3 * chans), flat_grad, (((0,), (0,)), ((), ())), preferred_element_type=jnp.float32))
    return jnp.stack(pieces)

def flip_kernel(w_conv):
    chans = w_conv.shape[1]
    return w_conv.reshape(3, 3, 3, chans, chans)[::-1, ::-1, ::-1].transpose(0, 1, 2, 4, 3).reshape(9, 3 * chans, chans)

def block_backward(padded, cell_mask, labels, kernel, w_head):
    chans = padded.shape[3]
    pre_act = conv_block(padded, kernel) * cell_mask[..., None]
    activated = jax.nn.silu(pre_act).astype(jnp.bfloat16)
    logits = jnp.dot(activated.reshape(-1, chans), w_head, preferred_element_type=jnp.float32)
    target = (labels.reshape(-1)[:, None] == jnp.arange(w_head.shape[1], dtype=jnp.int32)[None, :]).astype(jnp.float32)
    grad_logits = (jax.nn.sigmoid(logits) - target) * cell_mask.reshape(-1)[:, None]
    grad_act = jnp.dot(grad_logits, w_head.astype(jnp.float32).T, precision=lax.Precision.HIGHEST)
    flat_pre = pre_act.reshape(-1, chans)
    sigmoid_pre = jax.nn.sigmoid(flat_pre)
    grad_pre = (grad_act * sigmoid_pre * (1.0 + flat_pre * (1.0 - sigmoid_pre))).astype(jnp.bfloat16).reshape(pre_act.shape)
    return (grad_pre, weight_grad(padded, grad_pre))

def slots_to_grid(slots, count_x, count_y, bricks_z, half_edge):
    chans = slots.shape[2]
    shaped = slots.reshape(count_x, count_y, BX, BY, bricks_z, 2, 2, 2, half_edge, half_edge, half_edge, chans)
    ordered = shaped.transpose(0, 2, 5, 8, 1, 3, 6, 9, 4, 7, 10, 11)
    return ordered.reshape(count_x * BX * 2 * half_edge, count_y * BY * 2 * half_edge, bricks_z * 2 * half_edge, chans)

def grid_to_slots(grid_vals, count_x, count_y, bricks_z, half_edge):
    chans = grid_vals.shape[3]
    shaped = grid_vals.reshape(count_x, BX, 2, half_edge, count_y, BY, 2, half_edge, bricks_z, 2, half_edge, chans)
    ordered = shaped.transpose(0, 4, 1, 5, 8, 2, 6, 9, 3, 7, 10, 11)
    return ordered.reshape(-1, half_edge ** 3, chans)

def brick_mask(filled, count_x, count_y, bricks_z):
    bricks = lax.optimization_barrier(jnp.max(filled.reshape(count_x, count_y, BX, BY, bricks_z, 8), axis=5))
    bricks = bricks.transpose(0, 2, 1, 3, 4).reshape(count_x * BX, count_y * BY, bricks_z)
    return jnp.repeat(jnp.repeat(jnp.repeat(bricks, BR, axis=0), BR, axis=1), BR, axis=2)

def reference(fine_feats, owner_of, arrival_slot, w_stride, w_conv, w_head, labels):
    dev_count = N_GX * N_GY
    half_edge = BR // 2
    cells = half_edge ** 3
    n_slot = 8 * BX * BY * BZ
    size_x = BX * BR
    size_y = BY * BR
    partial_value = jnp.dot(fine_feats.reshape(-1, 8 * CF), w_stride, preferred_element_type=jnp.float32).astype(jnp.bfloat16).reshape(FINE, cells, CC)
    owners = owner_of.reshape(dev_count, F_DEV)
    matches = (owners[:, :, None] == jnp.arange(dev_count, dtype=jnp.int32)[None, None, :]).astype(jnp.int32)
    position = lax.optimization_barrier(jnp.sum(jnp.cumsum(matches, axis=1) * matches, axis=2)) - 1
    sources = jnp.arange(dev_count, dtype=jnp.int32)[:, None]
    lookup = (owners * (dev_count * CAP) + sources * CAP + position).reshape(-1).astype(jnp.int32)
    global_slot = (owner_of * n_slot + arrival_slot[lookup]).astype(jnp.int32)
    slots = jnp.zeros((dev_count * n_slot, cells, CC), jnp.bfloat16).at[global_slot].set(partial_value)
    filled = jnp.zeros((dev_count * n_slot,), jnp.float32).at[global_slot].set(1.0)
    coarse = slots_to_grid(slots, N_GX, N_GY, BZ, half_edge)
    cell_mask = brick_mask(filled, N_GX, N_GY, BZ)
    kernel = w_conv.reshape(9, 3 * CC, CC)
    coarse_pad = jnp.pad(coarse, ((1, 1), (1, 1), (0, 0), (0, 0)))
    zero_index = jnp.zeros((), jnp.int32)

    def forward_one(index):
        start_x = (index // N_GY * size_x).astype(jnp.int32)
        start_y = (index % N_GY * size_y).astype(jnp.int32)
        padded = lax.dynamic_slice(coarse_pad, (start_x, start_y, zero_index, zero_index), (size_x + 2, size_y + 2, NZC, CC))
        local_mask = lax.dynamic_slice(cell_mask, (start_x, start_y, zero_index), (size_x, size_y, NZC))
        local_labels = lax.dynamic_slice(labels, (start_x, start_y, zero_index), (size_x, size_y, NZC))
        return block_backward(padded, local_mask, local_labels, kernel, w_head)
    block_ids = jnp.arange(dev_count, dtype=jnp.int32)
    grad_blocks, conv_blocks = lax.map(forward_one, block_ids)
    grad_pre = grad_blocks.reshape(N_GX, N_GY, size_x, size_y, NZC, CC).transpose(0, 2, 1, 3, 4, 5).reshape(NXC, NYC, NZC, CC)
    grad_pad = jnp.pad(grad_pre, ((1, 1), (1, 1), (0, 0), (0, 0)))
    flipped = flip_kernel(w_conv)

    def backward_one(index):
        start_x = (index // N_GY * size_x).astype(jnp.int32)
        start_y = (index % N_GY * size_y).astype(jnp.int32)
        padded = lax.dynamic_slice(grad_pad, (start_x, start_y, zero_index, zero_index), (size_x + 2, size_y + 2, NZC, CC))
        return conv_block(padded, flipped).astype(jnp.bfloat16)
    coarse_grads = lax.map(backward_one, block_ids)
    grad_coarse = coarse_grads.reshape(N_GX, N_GY, size_x, size_y, NZC, CC).transpose(0, 2, 1, 3, 4, 5).reshape(NXC, NYC, NZC, CC)
    grad_slots = grid_to_slots(grad_coarse, N_GX, N_GY, BZ, half_edge)
    grad_partial = grad_slots[global_slot]
    flat_grad = grad_partial.reshape(-1, CC)
    grad_fine = lax.dot_general(flat_grad, w_stride, (((1,), (1,)), ((), ())), preferred_element_type=jnp.float32).astype(jnp.bfloat16).reshape(FINE, cells, 8 * CF)
    scale = 1.0 / math.sqrt(FINE * cells)
    grad_stride = lax.dot_general(fine_feats.reshape(-1, 8 * CF), flat_grad, (((0,), (0,)), ((), ())), preferred_element_type=jnp.float32) * scale
    grad_conv = (lax.optimization_barrier(jnp.sum(conv_blocks, axis=0)) * scale).reshape(27, CC, CC)
    return (grad_fine, grad_stride, grad_conv)
```

```python
import functools
import math

import jax
import jax.numpy as jnp
from jax import lax
from jax.experimental import pallas as pl
from jax.experimental.pallas import tpu as pltpu
from jax.sharding import PartitionSpec as P

BX = 2
BY = 2
BR = 4
SX = 8
SY = 8
SZ = 48
CH = 128
CELLS = 8
FX = SX + 4
FY = SY + 4
ROWS = SY * SZ
CODE = 16
SIDE = 2 * SZ
BRICKS = 384
BACK = 80
VMEM = pltpu.CompilerParams(vmem_limit_bytes=48 * 1024 * 1024)
BF = jnp.bfloat16
F32 = jnp.float32


def whole(shape):
    return pl.BlockSpec(shape, lambda: (0,) * len(shape))


def smem():
    return pl.BlockSpec(memory_space=pltpu.SMEM)


def matmul(a, b):
    return jnp.dot(a, b, preferred_element_type=F32)


def iota(shape, dim):
    return lax.broadcasted_iota(jnp.int32, shape, dim)


def send_kernel(cap, owner, feats, w_stride, buf, place, rows, count):
    per_dev = owner.shape[0]
    devs = count.shape[0]

    def clear(i, c):
        count[i] = 0
        return c

    lax.fori_loop(0, devs, clear, 0, unroll=8)
    buf[...] = jnp.zeros_like(buf)
    rows[...] = matmul(feats[...], w_stride[...]).reshape(rows.shape)

    def put(i, c):
        who = owner[i]
        pos = count[who]
        count[who] = pos + 1
        place[i] = (who * (BACK // 16) + pos // 2) * 2 + pos % 2
        buf[who * cap + pos] = rows[i].astype(BF)
        return c

    lax.fori_loop(0, per_dev, put, 0, unroll=4)


def send(feats, owner, w_stride, devs, cap):
    per_dev = owner.shape[0]
    return pl.pallas_call(
        functools.partial(send_kernel, cap),
        out_shape=(
            jax.ShapeDtypeStruct((devs * cap, CELLS, CH), BF),
            jax.ShapeDtypeStruct((per_dev,), jnp.int32),
        ),
        in_specs=[smem(), whole(feats.shape), whole(w_stride.shape)],
        out_specs=(whole((devs * cap, CELLS, CH)), smem()),
        scratch_shapes=[pltpu.VMEM((per_dev, CELLS, CH), F32), pltpu.SMEM((devs,), jnp.int32)],
        compiler_params=VMEM,
        name="send_bricks",
    )(owner, feats, w_stride)


def brick_order():
    row = iota((4 * SZ, 4 * SZ), 0)
    col = iota((4 * SZ, 4 * SZ), 1)
    z = row % SZ
    return (col == (z // 2) * 8 + (row // SZ) * 2 + z % 2).astype(BF)


def land_kernel(index, arrived, order, code, slab, first, last, held):
    held[...] = jnp.zeros_like(held)

    def put(j, c):
        held[index[j]] = arrived[j].astype(F32)
        return c

    lax.fori_loop(0, index.shape[0], put, 0, unroll=8)
    for big_x in range(SX // 2):
        for big_y in range(SY // 2):
            start = (big_x * (SY // 2) + big_y) * (SZ // 2)
            block = held[start : start + SZ // 2].reshape(4 * SZ, CH).astype(BF)
            moved = matmul(order[...], block).astype(BF)
            for i in range(2):
                for l in range(2):
                    piece = moved[(2 * i + l) * SZ : (2 * i + l + 1) * SZ]
                    row = (2 * big_y + l) * SZ
                    slab[2 * big_x + i, row : row + SZ, :] = piece
    slab[:, ROWS:, :] = code[...]
    first[...] = slab[:2]
    last[...] = slab[SX - 2 :]


def land(arrived, index, order, code):
    shapes = ((SX, ROWS + CODE, CH), (2, ROWS + CODE, CH), (2, ROWS + CODE, CH))
    return pl.pallas_call(
        land_kernel,
        out_shape=tuple(jax.ShapeDtypeStruct(s, BF) for s in shapes),
        in_specs=[smem(), whole(arrived.shape), whole(order.shape), whole(code.shape)],
        out_specs=tuple(whole(s) for s in shapes),
        scratch_shapes=[pltpu.VMEM((BRICKS + 8, CELLS, CH), F32)],
        compiler_params=VMEM,
        name="land_bricks",
    )(index, arrived, order, code)


def sides_kernel(slab, before, after, up, down):
    row = iota((CODE // 2, CH), 0)
    none = jnp.zeros((CODE // 2, CH), F32)
    for x in range(FX):
        if x < 2:
            ref, at = before, x
        elif x < 2 + SX:
            ref, at = slab, x - 2
        else:
            ref, at = after, x - 2 - SX
        up[x, :SIDE, :] = ref[at, ROWS - SIDE : ROWS, :]
        down[x, :SIDE, :] = ref[at, :SIDE, :]
        codes = ref[at, ROWS:, :].astype(F32)
        upper = jnp.where(row < 2, codes[8:], 0.0)
        lower = jnp.where((row == 2) | (row == 3), codes[:8], 0.0)
        up[x, SIDE:, :] = jnp.concatenate([upper, none], axis=0).astype(BF)
        down[x, SIDE:, :] = jnp.concatenate([none, lower], axis=0).astype(BF)


def sides(slab, before, after):
    shape = (FX, SIDE + CODE, CH)
    return pl.pallas_call(
        sides_kernel,
        out_shape=(jax.ShapeDtypeStruct(shape, BF),) * 2,
        in_specs=[whole(slab.shape), whole(before.shape), whole(after.shape)],
        out_specs=(whole(shape),) * 2,
        compiler_params=VMEM,
        name="y_sides",
    )(slab, before, after)


def shifted(vals, z, by):
    rows = vals.shape[0]
    turned = pltpu.roll(vals, by % rows, 0)
    return jnp.where(z == (0 if by == 1 else SZ - 1), 0.0, turned)


def core_kernel(
    index, slab, before, after, left, right, w_fwd, w_bwd, head, head_t, order_t, back,
    grid, codes, grad, grad3, total, coarse, held,
):
    grid[:2, SIDE : SIDE + ROWS, :] = before[:, :ROWS, :]
    grid[2 : 2 + SX, SIDE : SIDE + ROWS, :] = slab[:, :ROWS, :]
    grid[2 + SX :, SIDE : SIDE + ROWS, :] = after[:, :ROWS, :]
    grid[:, :SIDE, :] = left[:, :SIDE, :]
    grid[:, SIDE + ROWS :, :] = right[:, :SIDE, :]
    codes[:2] = before[:, ROWS:, :].astype(F32)
    codes[2 : 2 + SX] = slab[:, ROWS:, :].astype(F32)
    codes[2 + SX :] = after[:, ROWS:, :].astype(F32)
    codes[...] += left[:, SIDE:, :].astype(F32) + right[:, SIDE:, :].astype(F32)

    wide = ROWS + SIDE
    lane = iota((wide, CH), 1)
    z_wide = iota((wide // SZ, SZ, CH), 1).reshape(wide, CH)
    z_own = iota((SY, SZ, CH), 1).reshape(ROWS, CH)
    eye = (iota((SZ, CH), 0) == iota((SZ, CH), 1)).astype(F32)
    ones = jnp.ones((CH, CH), BF)

    def forward(x, carry):
        taps = jnp.concatenate(
            [grid[x + e, f * SZ : f * SZ + wide, :] for e in range(3) for f in range(3)], axis=1
        )
        parts = matmul(taps, w_fwd[...])
        pre = (
            shifted(parts[:, :CH], z_wide, 1)
            + parts[:, CH : 2 * CH]
            + shifted(parts[:, 2 * CH :], z_wide, -1)
        )
        here = codes[x + 1]
        spread = jnp.concatenate([eye * here[y + 1 : y + 2, :] for y in range(SY + 2)], axis=0)
        code = matmul(spread.astype(BF), ones)
        mask = code > 0.5
        pre = jnp.where(mask, pre, 0.0)
        gate = jax.nn.sigmoid(pre)
        logits = matmul((pre * gate).astype(BF), head[...])
        target = (code - 1.0 == (lane % 8).astype(F32)).astype(F32)
        grad_logits = jnp.where(mask, jax.nn.sigmoid(logits) - target, 0.0)
        high = grad_logits.astype(BF).astype(F32)
        terms = jnp.where(lane < 8, high, jnp.where(lane < 16, grad_logits - high, 0.0))
        grad_act = matmul(terms.astype(BF), head_t[...])
        grad_pre = (grad_act * gate * (1.0 + pre * (1.0 - gate))).astype(BF)
        grad[x] = grad_pre
        own = grad_pre[SZ : SZ + ROWS].astype(F32)
        grad3[x, :, :CH] = shifted(own, z_own, -1).astype(BF)
        grad3[x, :, CH : 2 * CH] = grad_pre[SZ : SZ + ROWS]
        grad3[x, :, 2 * CH :] = shifted(own, z_own, 1).astype(BF)
        return carry

    lax.fori_loop(0, SX + 2, forward, 0)

    total[...] = jnp.zeros_like(total)

    def weights(x, carry):
        for e in range(3):
            taps = jnp.concatenate(
                [grid[x + 1 + e, (1 + f) * SZ : (1 + f) * SZ + ROWS, :] for f in range(3)], axis=1
            )
            total[e] += lax.dot_general(
                taps, grad3[x + 1], (((0,), (0,)), ((), ())), preferred_element_type=F32
            )
        return carry

    lax.fori_loop(0, SX, weights, 0)

    def backward(x, carry):
        taps = jnp.concatenate(
            [
                grad[x + 2 - e, (2 - f) * SZ : (2 - f) * SZ + ROWS, :]
                for e in range(3)
                for f in range(3)
            ],
            axis=1,
        )
        parts = matmul(taps, w_bwd[...])
        coarse[x] = (
            shifted(parts[:, :CH], z_own, -1)
            + parts[:, CH : 2 * CH]
            + shifted(parts[:, 2 * CH :], z_own, 1)
        ).astype(BF)
        return carry

    lax.fori_loop(0, SX, backward, 0)

    for big_x in range(SX // 2):
        for big_y in range(SY // 2):
            block = jnp.concatenate(
                [
                    coarse[2 * big_x + i, (2 * big_y + l) * SZ : (2 * big_y + l + 1) * SZ, :]
                    for i in range(2)
                    for l in range(2)
                ],
                axis=0,
            )
            start = (big_x * (SY // 2) + big_y) * (SZ // 2)
            held[start : start + SZ // 2] = matmul(order_t[...], block).reshape(SZ // 2, CELLS, CH)

    def put(d, carry):
        for pair in range(3):
            j = d * 6 + 2 * pair
            both = jnp.concatenate([held[index[j]], held[index[j + 1]]], axis=0)
            back[d, 16 * pair : 16 * pair + 16, :] = both.astype(BF)
        return carry

    lax.fori_loop(0, back.shape[0], put, 0, unroll=2)

    for tap in range(27):
        e, f, g = tap // 9, tap // 3 % 3, tap % 3
        block = total[e, f * CH : (f + 1) * CH, g * CH : (g + 1) * CH].astype(BF)
        back[4 * tap : 4 * tap + 4, 48:, :] = block.reshape(4, 32, CH)
    back[108:, 48:, :] = jnp.zeros((back.shape[0] - 108, 32, CH), BF)


def core(index, slab, before, after, left, right, w_fwd, w_bwd, head, head_t, order_t, devs):
    wide = ROWS + SIDE
    arrays = (slab, before, after, left, right, w_fwd, w_bwd, head, head_t, order_t)
    return pl.pallas_call(
        core_kernel,
        out_shape=jax.ShapeDtypeStruct((devs, BACK, CH), BF),
        in_specs=[smem()] + [whole(a.shape) for a in arrays],
        out_specs=whole((devs, BACK, CH)),
        scratch_shapes=[
            pltpu.VMEM((FX, FY * SZ, CH), BF),
            pltpu.VMEM((FX, CODE, CH), F32),
            pltpu.VMEM((SX + 2, wide, CH), BF),
            pltpu.VMEM((SX + 2, ROWS, 3 * CH), BF),
            pltpu.VMEM((3, 3 * CH, 3 * CH), F32),
            pltpu.VMEM((SX, ROWS, CH), BF),
            pltpu.VMEM((BRICKS, CELLS, CH), F32),
        ],
        compiler_params=VMEM,
        name="conv_both_ways",
    )(index, *arrays)


def last_kernel(place, came, feats, w_stride, grad_fine, stride, conv, mine):
    per_dev = place.shape[0]

    def take(i, carry):
        at = place[i]
        both = came[at // 2].astype(F32)
        mine[i] = jnp.where(at % 2 == 0, both[:8], both[8:])
        return carry

    lax.fori_loop(0, per_dev, take, 0, unroll=4)
    vals = mine[...].reshape(per_dev * CELLS, CH).astype(BF)
    grad_fine[...] = lax.dot_general(
        vals, w_stride[...], (((1,), (1,)), ((), ())), preferred_element_type=F32
    ).astype(BF)
    stride[...] = lax.dot_general(
        feats[...], vals, (((0,), (0,)), ((), ())), preferred_element_type=F32
    ).astype(BF)
    per = BACK // 16

    def add(d, sums):
        return (sums[0] + came[d * per + 3].astype(F32), sums[1] + came[d * per + 4].astype(F32))

    none = jnp.zeros((16, CH), F32)
    low, high = lax.fori_loop(0, came.shape[0] // per, add, (none, none), unroll=4)
    conv[:16, :] = low
    conv[16:, :] = high


def last(came, place, feats, w_stride):
    per_dev = place.shape[0]
    return pl.pallas_call(
        last_kernel,
        out_shape=(
            jax.ShapeDtypeStruct(feats.shape, BF),
            jax.ShapeDtypeStruct(w_stride.shape, BF),
            jax.ShapeDtypeStruct((32, CH), F32),
        ),
        in_specs=[smem(), whole(came.shape), whole(feats.shape), whole(w_stride.shape)],
        out_specs=(whole(feats.shape), whole(w_stride.shape), whole((32, CH))),
        scratch_shapes=[pltpu.VMEM((per_dev, CELLS, CH), F32)],
        compiler_params=VMEM,
        name="grad_fine_and_terms",
    )(place, came, feats, w_stride)


def to_all(buffer):
    return lax.all_to_all(buffer, ("gx", "gy"), split_axis=0, concat_axis=0, tiled=True)


def both_ways(first, last_part, axis):
    peers = lax.axis_size(axis)
    up = [(i, i + 1) for i in range(peers - 1)]
    down = [(i + 1, i) for i in range(peers - 1)]
    return lax.ppermute(last_part, axis, up), lax.ppermute(first, axis, down)


def label_codes(arrival_slot, labels):
    bricks = BX * BY * SZ // BR
    filled = jnp.any(
        (arrival_slot >> 3)[None, :] == jnp.arange(bricks, dtype=jnp.int32)[:, None], axis=1
    ).reshape(BX, 1, BY, 1, SZ // BR, 1)
    cells = labels.reshape(BX, BR, BY, BR, SZ // BR, BR)
    codes = jnp.where(filled, cells + 1, 0).reshape(SX, SY, SZ).astype(BF)
    return jnp.pad(codes, ((0, 0), (2, CODE - 2 - SY), (0, CH - SZ)))


def per_device(fine_feats, owner_of, arrival_slot, w_stride, w_conv, w_head, labels):
    devs = lax.axis_size("gx") * lax.axis_size("gy")
    per_dev, cells, in_width = fine_feats.shape
    cap = arrival_slot.shape[0] // devs
    feats = fine_feats.reshape(per_dev * cells, in_width)
    buffer, place = send(feats, owner_of, w_stride, devs, cap)

    brick, octant = arrival_slot >> 3, arrival_slot & 7
    deep = SZ // BR
    big_x = 2 * (brick // (BY * deep)) + (octant >> 2)
    big_y = 2 * (brick // deep % BY) + ((octant >> 1) & 1)
    big_z = 2 * (brick % deep) + (octant & 1)
    index = jnp.where(arrival_slot >= 0, (big_x * (SY // 2) + big_y) * (SZ // 2) + big_z, BRICKS)
    code = label_codes(arrival_slot, labels)
    order = brick_order()
    taps = w_conv.reshape(9, 3, CH, CH)
    w_fwd = taps.transpose(0, 2, 1, 3).reshape(9 * CH, 3 * CH)
    w_bwd = taps.transpose(0, 3, 1, 2).reshape(9 * CH, 3 * CH)
    head = jnp.pad(jnp.concatenate([w_head, w_head], axis=1), ((0, 0), (0, CH - 16)))

    arrived = to_all(buffer)
    slab, first, last_part = land(arrived, index, order, code)
    before, after = both_ways(first, last_part, "gx")
    up, down = sides(slab, before, after)
    left, right = both_ways(down, up, "gy")
    returned = core(
        jnp.minimum(index, BRICKS - 1),
        slab,
        before,
        after,
        left,
        right,
        w_fwd,
        w_bwd,
        head,
        head.T,
        order.T,
        devs,
    )
    came = to_all(returned)
    grad_fine, stride, conv = last(
        came.reshape(devs * BACK // 16, 16, CH), place, feats, w_stride
    )
    share = in_width // devs
    terms = to_all(stride.reshape(devs, share, CH))
    stride_sum = jnp.sum(terms.astype(F32), axis=0)
    block = jnp.concatenate([conv, stride_sum], axis=0).astype(BF)
    sums = to_all(jnp.broadcast_to(block[None], (devs,) + block.shape))
    scale = 1.0 / math.sqrt(per_dev * devs * cells)
    grad_conv = sums[:, :32].reshape(devs * 32, CH)[: 27 * CH].astype(F32) * scale
    grad_stride = sums[:, 32:].reshape(in_width, CH).astype(F32) * scale
    return (
        grad_fine.reshape(per_dev, cells, in_width),
        grad_stride,
        grad_conv.reshape(27, CH, CH),
    )


def solution(mesh):
    return jax.shard_map(
        per_device,
        mesh=mesh,
        in_specs=(
            P(("gx", "gy"), None, None),
            P(("gx", "gy")),
            P(("gx", "gy")),
            P(),
            P(),
            P(),
            P("gx", "gy", None),
        ),
        out_specs=(P(("gx", "gy"), None, None), P(), P()),
        check_vma=False,
    )
```

```python
import functools
import math

import jax
import jax.numpy as jnp
from jax import lax
from jax.experimental import pallas as pl
from jax.experimental.pallas import tpu as pltpu
from jax.sharding import PartitionSpec as P

BX = 2
BY = 2
BR = 4
SX = 8
SY = 8
SZ = 48
CH = 128
CELLS = 8
FX = SX + 4
FY = SY + 4
ROWS = SY * SZ
CODE = 16
SIDE = 2 * SZ
BRICKS = 384
PARTS = 4
VMEM = pltpu.CompilerParams(vmem_limit_bytes=24 * 1024 * 1024)
ALL_VMEM = pltpu.CompilerParams(vmem_limit_bytes=63 * 1024 * 1024)
BF = jnp.bfloat16
F32 = jnp.float32


def whole(shape):
    return pl.BlockSpec(shape, lambda: (0,) * len(shape))


def anywhere():
    return pl.BlockSpec(memory_space=pl.ANY)


def smem():
    return pl.BlockSpec(memory_space=pltpu.SMEM)


def matmul(a, b):
    return jnp.dot(a, b, preferred_element_type=F32)


def iota(shape, dim):
    return lax.broadcasted_iota(jnp.int32, shape, dim)


def send_kernel(
    cap, owner_hbm, feats_hbm, w_hbm, buf_hbm, place, owner, feats, w_stride, rows, buf, count, sems
):
    per_dev = owner.shape[0]
    devs = count.shape[0]
    part = feats.shape[0] // PARTS
    copies = [
        pltpu.make_async_copy(owner_hbm, owner, sems.at[0]),
        pltpu.make_async_copy(w_hbm, w_stride, sems.at[1]),
    ] + [
        pltpu.make_async_copy(
            feats_hbm.at[pl.ds(i * part, part)], feats.at[pl.ds(i * part, part)], sems.at[2 + i]
        )
        for i in range(PARTS)
    ]
    for copy in copies:
        copy.start()

    def clear(i, c):
        count[i] = 0
        return c

    lax.fori_loop(0, devs, clear, 0, unroll=8)
    buf[...] = jnp.zeros_like(buf)
    copies[0].wait()

    def find(i, c):
        who = owner[i]
        pos = count[who]
        count[who] = pos + 1
        place[i] = who * cap + pos
        return c

    lax.fori_loop(0, per_dev, find, 0, unroll=8)
    copies[1].wait()
    bricks = per_dev // PARTS
    for i in range(PARTS):
        copies[2 + i].wait()
        vals = matmul(feats[i * part : (i + 1) * part, :], w_stride[...])
        rows[i * bricks : (i + 1) * bricks] = vals.reshape(bricks, CELLS, CH)

    def put(i, c):
        buf[place[i]] = rows[i].astype(BF)
        return c

    lax.fori_loop(0, per_dev, put, 0, unroll=8)
    out = pltpu.make_async_copy(buf, buf_hbm, sems.at[0])
    out.start()
    out.wait()


def hbm():
    return pl.BlockSpec(memory_space=pltpu.HBM)


def send(feats, owner, w_stride, devs, cap):
    per_dev = owner.shape[0]
    return pl.pallas_call(
        functools.partial(send_kernel, cap),
        out_shape=(
            jax.ShapeDtypeStruct((devs * cap, CELLS, CH), BF),
            jax.ShapeDtypeStruct((per_dev,), jnp.int32),
        ),
        in_specs=[hbm(), hbm(), hbm()],
        out_specs=(hbm(), smem()),
        scratch_shapes=[
            pltpu.SMEM((per_dev,), jnp.int32),
            pltpu.VMEM(feats.shape, BF),
            pltpu.VMEM(w_stride.shape, BF),
            pltpu.VMEM((per_dev, CELLS, CH), F32),
            pltpu.VMEM((devs * cap, CELLS, CH), BF),
            pltpu.SMEM((devs,), jnp.int32),
            pltpu.SemaphoreType.DMA((2 + PARTS,)),
        ],
        compiler_params=ALL_VMEM,
        name="send_bricks",
    )(owner, feats, w_stride)


def brick_order():
    row = iota((4 * SZ, 4 * SZ), 0)
    col = iota((4 * SZ, 4 * SZ), 1)
    z = row % SZ
    return (col == (z // 2) * 8 + (row // SZ) * 2 + z % 2).astype(BF)


def land_kernel(index, arrived, order, code, slab, first, last, held):
    held[...] = jnp.zeros_like(held)

    def put(j, c):
        held[index[j]] = arrived[j].astype(F32)
        return c

    lax.fori_loop(0, index.shape[0], put, 0, unroll=8)
    for big_x in range(SX // 2):
        for big_y in range(SY // 2):
            start = (big_x * (SY // 2) + big_y) * (SZ // 2)
            block = held[start : start + SZ // 2].reshape(4 * SZ, CH).astype(BF)
            moved = matmul(order[...], block).astype(BF)
            for i in range(2):
                for l in range(2):
                    piece = moved[(2 * i + l) * SZ : (2 * i + l + 1) * SZ]
                    row = (2 * big_y + l) * SZ
                    slab[2 * big_x + i, row : row + SZ, :] = piece
    slab[:, ROWS:, :] = code[...]
    first[...] = slab[:2]
    last[...] = slab[SX - 2 :]


def land(arrived, index, order, code):
    shapes = ((SX, ROWS + CODE, CH), (2, ROWS + CODE, CH), (2, ROWS + CODE, CH))
    return pl.pallas_call(
        land_kernel,
        out_shape=tuple(jax.ShapeDtypeStruct(s, BF) for s in shapes),
        in_specs=[smem(), whole(arrived.shape), whole(order.shape), whole(code.shape)],
        out_specs=tuple(whole(s) for s in shapes),
        scratch_shapes=[pltpu.VMEM((BRICKS + 8, CELLS, CH), F32)],
        compiler_params=VMEM,
        name="land_bricks",
    )(index, arrived, order, code)


def sides_kernel(slab, before, after, inside, up, down):
    row = iota((CODE // 2, CH), 0)
    none = jnp.zeros((CODE // 2, CH), F32)
    for x in range(FX):
        if x < 2:
            ref, at = before, x
        elif x < 2 + SX:
            ref, at = slab, x - 2
        else:
            ref, at = after, x - 2 - SX
        up[x, :SIDE, :] = ref[at, ROWS - SIDE : ROWS, :]
        down[x, :SIDE, :] = ref[at, :SIDE, :]
        codes = ref[at, ROWS:, :].astype(F32)
        upper = jnp.where(row < 2, codes[8:], 0.0)
        lower = jnp.where((row == 2) | (row == 3), codes[:8], 0.0)
        up[x, SIDE:, :] = jnp.concatenate([upper, none], axis=0).astype(BF)
        down[x, SIDE:, :] = jnp.concatenate([none, lower], axis=0).astype(BF)


def sides(slab, before, after, inside):
    shape = (FX, SIDE + CODE, CH)
    return pl.pallas_call(
        sides_kernel,
        out_shape=(jax.ShapeDtypeStruct(shape, BF),) * 2,
        in_specs=[whole(slab.shape), whole(before.shape), whole(after.shape), anywhere()],
        out_specs=(whole(shape),) * 2,
        compiler_params=VMEM,
        name="y_sides",
    )(slab, before, after, inside)


def shifted(vals, z, by):
    rows = vals.shape[0]
    turned = pltpu.roll(vals, by % rows, 0)
    return jnp.where(z == (0 if by == 1 else SZ - 1), 0.0, turned)


def spread_codes(blocks):
    eye = (iota((SZ, CH), 0) == iota((SZ, CH), 1)).astype(F32)
    return jnp.concatenate([eye * block for block in blocks], axis=0).astype(BF)


def front(taps, spread, w_fwd, head, head_t):
    rows = spread.shape[0]
    lane = iota((rows, CH), 1)
    z = iota((rows // SZ, SZ, CH), 1).reshape(rows, CH)
    parts = matmul(jnp.concatenate(taps, axis=1), w_fwd)
    pre = (
        shifted(parts[:, :CH], z, 1)
        + parts[:, CH : 2 * CH]
        + shifted(parts[:, 2 * CH :], z, -1)
    )
    code = matmul(spread, jnp.ones((CH, CH), BF))
    mask = code > 0.5
    pre = jnp.where(mask, pre, 0.0)
    gate = jax.nn.sigmoid(pre)
    logits = matmul((pre * gate).astype(BF), head)
    target = (code - 1.0 == (lane % 8).astype(F32)).astype(F32)
    grad_logits = jnp.where(mask, jax.nn.sigmoid(logits) - target, 0.0)
    high = grad_logits.astype(BF).astype(F32)
    terms = jnp.where(lane < 8, high, jnp.where(lane < 16, grad_logits - high, 0.0))
    grad_act = matmul(terms.astype(BF), head_t)
    return (grad_act * gate * (1.0 + pre * (1.0 - gate))).astype(BF)


INNER = (SY - 2) * SZ


def front_cost(slabs):
    flops = 2 * 9 * 3 * CH * CH * INNER * slabs
    return pl.CostEstimate(flops=flops, bytes_accessed=4 * 2**20, transcendentals=0)


def inner_kernel(slab, w_fwd, head, head_t, grad):
    def step(x, carry):
        taps = [slab[x + e, f * SZ : f * SZ + INNER, :] for e in range(3) for f in range(3)]
        codes = slab[x + 1, ROWS:, :].astype(F32)
        spread = spread_codes([codes[y : y + 1] for y in range(3, SY + 1)])
        grad[x] = front(taps, spread, w_fwd[...], head[...], head_t[...])
        return carry

    lax.fori_loop(0, SX - 2, step, 0, unroll=2)


def inner(slab, w_fwd, head, head_t):
    arrays = (slab, w_fwd, head, head_t)
    shape = (SX - 2, INNER, CH)
    return pl.pallas_call(
        inner_kernel,
        out_shape=jax.ShapeDtypeStruct(shape, BF),
        in_specs=[whole(a.shape) for a in arrays],
        out_specs=whole(shape),
        compiler_params=VMEM,
        cost_estimate=front_cost(SX - 2),
        name="grad_pre_inside",
    )(*arrays)


def x_sides_kernel(slab, before, after, w_fwd, head, head_t, grad):
    def source(x):
        if x < 2:
            return before, x
        return (slab, x - 2) if x < SX + 2 else (after, x - SX - 2)

    for i, x in enumerate((0, 1, SX, SX + 1)):
        taps = []
        for e in range(3):
            ref, at = source(x + e)
            taps += [ref[at, f * SZ : f * SZ + INNER, :] for f in range(3)]
        ref, at = source(x + 1)
        codes = ref[at, ROWS:, :].astype(F32)
        spread = spread_codes([codes[y : y + 1] for y in range(3, SY + 1)])
        grad[i] = front(taps, spread, w_fwd[...], head[...], head_t[...])


def x_sides(slab, before, after, w_fwd, head, head_t):
    arrays = (slab, before, after, w_fwd, head, head_t)
    shape = (4, INNER, CH)
    return pl.pallas_call(
        x_sides_kernel,
        out_shape=jax.ShapeDtypeStruct(shape, BF),
        in_specs=[whole(a.shape) for a in arrays],
        out_specs=whole(shape),
        compiler_params=VMEM,
        cost_estimate=front_cost(4),
        name="grad_pre_x_sides",
    )(*arrays)


def core_kernel(
    index, slab, before, after, left, right, inside, at_x, w_fwd, w_bwd, head, head_t, order_t,
    back_hbm, grid_hbm, own_hbm, low, high, codes, grad, coarse, held, back, sems,
):
    middle = pl.ds(SIDE, ROWS)
    pairs = (
        (slab.at[:, pl.ds(0, ROWS)], grid_hbm.at[pl.ds(2, SX), middle]),
        (before.at[:, pl.ds(0, ROWS)], grid_hbm.at[pl.ds(0, 2), middle]),
        (after.at[:, pl.ds(0, ROWS)], grid_hbm.at[pl.ds(2 + SX, 2), middle]),
        (left.at[:, pl.ds(0, SIDE)], grid_hbm.at[:, pl.ds(0, SIDE)]),
        (right.at[:, pl.ds(0, SIDE)], grid_hbm.at[:, pl.ds(SIDE + ROWS, SIDE)]),
    )
    copies = [pltpu.make_async_copy(a, b, sems.at[i]) for i, (a, b) in enumerate(pairs)]
    for copy in copies:
        copy.start()
    for at, ref in ((0, before), (2, slab), (2 + SX, after)):
        many = ref.shape[0]
        low[at : at + many, SIDE:, :] = ref[:, :SIDE, :]
        high[at : at + many, :SIDE, :] = ref[:, ROWS - SIDE : ROWS, :]
        codes[at : at + many] = ref[:, ROWS:, :].astype(F32)
    low[:, :SIDE, :] = left[:, :SIDE, :]
    high[:, SIDE:, :] = right[:, :SIDE, :]
    codes[...] += left[:, SIDE:, :].astype(F32) + right[:, SIDE:, :].astype(F32)
    grad[:2, SIDE : SIDE + INNER, :] = at_x[:2]
    grad[2:SX, SIDE : SIDE + INNER, :] = inside[...]
    grad[SX:, SIDE : SIDE + INNER, :] = at_x[2:]

    z_own = iota((SY, SZ, CH), 1).reshape(ROWS, CH)

    def forward(pair, carry):
        x = 2 * pair
        taps = [
            jnp.concatenate(
                [
                    ref[x + i + e, f * SZ : f * SZ + SIDE, :]
                    for i in range(2)
                    for ref in (low, high)
                ],
                axis=0,
            )
            for e in range(3)
            for f in range(3)
        ]
        blocks = []
        for i in range(2):
            here = codes[x + i + 1]
            blocks += [here[y : y + 1] for y in (1, 2, SY + 1, SY + 2)]
        vals = front(taps, spread_codes(blocks), w_fwd[...], head[...], head_t[...])
        for i in range(2):
            grad[x + i, :SIDE, :] = vals[2 * i * SIDE : (2 * i + 1) * SIDE]
            grad[x + i, SIDE + INNER :, :] = vals[(2 * i + 1) * SIDE : (2 * i + 2) * SIDE]
        return carry

    lax.fori_loop(0, SX // 2 + 1, forward, 0, unroll=5)
    out = pltpu.make_async_copy(
        grad.at[pl.ds(1, SX), pl.ds(SZ, ROWS)], own_hbm, sems.at[len(pairs)]
    )
    out.start()
    copies.append(out)

    def backward(x, carry):
        taps = jnp.concatenate(
            [
                grad[x + 2 - e, (2 - f) * SZ : (2 - f) * SZ + ROWS, :]
                for e in range(3)
                for f in range(3)
            ],
            axis=1,
        )
        parts = matmul(taps, w_bwd[...])
        coarse[x] = (
            shifted(parts[:, :CH], z_own, -1)
            + parts[:, CH : 2 * CH]
            + shifted(parts[:, 2 * CH :], z_own, 1)
        ).astype(BF)
        return carry

    lax.fori_loop(0, SX, backward, 0, unroll=2)

    for big_x in range(SX // 2):
        for big_y in range(SY // 2):
            block = jnp.concatenate(
                [
                    coarse[2 * big_x + i, (2 * big_y + l) * SZ : (2 * big_y + l + 1) * SZ, :]
                    for i in range(2)
                    for l in range(2)
                ],
                axis=0,
            )
            start = (big_x * (SY // 2) + big_y) * (SZ // 2)
            held[start : start + SZ // 2] = matmul(order_t[...], block).reshape(SZ // 2, CELLS, CH)

    def put(j, carry):
        back[j] = held[index[j]].astype(BF)
        return carry

    part = index.shape[0] // PARTS
    for i in range(PARTS):
        lax.fori_loop(i * part, (i + 1) * part, put, 0, unroll=8)
        rows = pl.ds(i * part, part)
        copy = pltpu.make_async_copy(back.at[rows], back_hbm.at[rows], sems.at[6 + i])
        copy.start()
        copies.append(copy)
    for copy in copies:
        copy.wait()


def core(
    index, slab, before, after, left, right, inside, at_x, w_fwd, w_bwd, head, head_t, order_t
):
    arrays = (
        slab, before, after, left, right, inside, at_x, w_fwd, w_bwd, head, head_t, order_t
    )
    shapes = ((index.shape[0], CELLS, CH), (FX, FY * SZ, CH), (SX, ROWS, CH))
    return pl.pallas_call(
        core_kernel,
        out_shape=tuple(jax.ShapeDtypeStruct(s, BF) for s in shapes),
        in_specs=[smem()] + [whole(a.shape) for a in arrays],
        out_specs=(hbm(),) * 3,
        scratch_shapes=[
            pltpu.VMEM((FX, 2 * SIDE, CH), BF),
            pltpu.VMEM((FX, 2 * SIDE, CH), BF),
            pltpu.VMEM((FX, CODE, CH), F32),
            pltpu.VMEM((SX + 2, ROWS + SIDE, CH), BF),
            pltpu.VMEM((SX, ROWS, CH), BF),
            pltpu.VMEM((BRICKS, CELLS, CH), F32),
            pltpu.VMEM((index.shape[0], CELLS, CH), BF),
            pltpu.SemaphoreType.DMA((6 + PARTS,)),
        ],
        compiler_params=VMEM,
        name="conv_both_ways",
    )(index, *arrays)


def weights_kernel(half, grid, grad, keep, give, total, taps_out):
    z_own = iota((SY, SZ, CH), 1).reshape(ROWS, CH)
    total[...] = jnp.zeros_like(total)

    def add(x, carry):
        mid = grad[x].astype(F32)
        grads = jnp.concatenate(
            [shifted(mid, z_own, -1).astype(BF), grad[x], shifted(mid, z_own, 1).astype(BF)],
            axis=1,
        )
        for e in range(3):
            taps = jnp.concatenate(
                [grid[x + 1 + e, (1 + f) * SZ : (1 + f) * SZ + ROWS, :] for f in range(3)], axis=1
            )
            total[e] += lax.dot_general(
                taps, grads, (((0,), (0,)), ((), ())), preferred_element_type=F32
            )
        return carry

    lax.fori_loop(0, SX, add, 0, unroll=2)
    for tap in range(27):
        e, f, g = tap // 9, tap // 3 % 3, tap % 3
        taps_out[tap] = total[e, f * CH : (f + 1) * CH, g * CH : (g + 1) * CH]
    taps_out[27:] = jnp.zeros((5, CH, CH), F32)
    mine = half[0]
    keep[...] = taps_out[pl.ds(16 * mine, 16)]
    give[...] = taps_out[pl.ds(16 * (1 - mine), 16)].astype(BF)


def weights(half, grid, grad):
    shape = (16, CH, CH)
    return pl.pallas_call(
        weights_kernel,
        out_shape=(jax.ShapeDtypeStruct(shape, F32), jax.ShapeDtypeStruct(shape, BF)),
        in_specs=[smem(), whole(grid.shape), whole(grad.shape)],
        out_specs=(whole(shape),) * 2,
        scratch_shapes=[pltpu.VMEM((3, 3 * CH, 3 * CH), F32), pltpu.VMEM((32, CH, CH), F32)],
        compiler_params=ALL_VMEM,
        cost_estimate=pl.CostEstimate(
            flops=2 * 27 * CH * CH * SX * ROWS, bytes_accessed=6 * 2**20, transcendentals=0
        ),
        name="conv_weight_grad",
    )(half, grid, grad)


def pair_kernel(me, keep, got, mine, *others):
    share = mine.shape[0]
    for by, out in enumerate((mine,) + others):
        at = pl.ds(share * lax.rem(me[0] + by, len(others) + 1), share)
        out[...] = (keep[at] + got[at].astype(F32)).astype(out.dtype)


def add_pair(y, keep, got, ring):
    shape = (keep.shape[0] // ring, CH, CH)
    kinds = (F32,) + (BF,) * (ring - 1)
    return pl.pallas_call(
        pair_kernel,
        out_shape=tuple(jax.ShapeDtypeStruct(shape, kind) for kind in kinds),
        in_specs=[smem(), whole(keep.shape), whole(got.shape)],
        out_specs=(whole(shape),) * ring,
        compiler_params=ALL_VMEM,
        name="add_pair",
    )(y, keep, got)


def sum_over_gy(keep, give):
    me = lax.axis_index("gy")
    y = me // 2
    peers = lax.axis_size("gy")
    ring = peers // 2
    got = lax.ppermute(give, "gy", [(i, i ^ 1) for i in range(peers)])
    total, *others = add_pair(y.astype(jnp.int32).reshape(1), keep, got, ring)
    for by, part in enumerate(others, 1):
        perm = [(i, (i + 2 * by) % peers) for i in range(peers)]
        total = total + lax.ppermute(part, "gy", perm).astype(F32)
    return total.transpose(1, 0, 2).astype(BF)


def last_kernel(place, came, feats, mine, stride, rows):
    per_dev = place.shape[0]

    def take(i, carry):
        rows[i] = came[place[i]].astype(F32)
        return carry

    lax.fori_loop(0, per_dev, take, 0, unroll=8)
    vals = rows[...].reshape(per_dev * CELLS, CH).astype(BF)
    mine[...] = vals
    stride[...] = lax.dot_general(
        feats[...], vals, (((0,), (0,)), ((), ())), preferred_element_type=F32
    ).astype(BF)


def last(came, place, feats):
    shapes = ((feats.shape[0], CH), (feats.shape[1], CH))
    return pl.pallas_call(
        last_kernel,
        out_shape=tuple(jax.ShapeDtypeStruct(s, BF) for s in shapes),
        in_specs=[smem(), whole(came.shape), whole(feats.shape)],
        out_specs=tuple(whole(s) for s in shapes),
        scratch_shapes=[pltpu.VMEM((place.shape[0], CELLS, CH), F32)],
        compiler_params=VMEM,
        name="stride_term",
    )(place, came, feats)


def to_all(buffer):
    return lax.all_to_all(buffer, ("gx", "gy"), split_axis=0, concat_axis=0, tiled=True)


def both_ways(first, last_part, axis):
    peers = lax.axis_size(axis)
    up = [(i, i + 1) for i in range(peers - 1)]
    down = [(i + 1, i) for i in range(peers - 1)]
    return lax.ppermute(last_part, axis, up), lax.ppermute(first, axis, down)


def label_codes(arrival_slot, labels):
    bricks = BX * BY * SZ // BR
    filled = jnp.any(
        (arrival_slot >> 3)[None, :] == jnp.arange(bricks, dtype=jnp.int32)[:, None], axis=1
    ).reshape(BX, 1, BY, 1, SZ // BR, 1)
    cells = labels.reshape(BX, BR, BY, BR, SZ // BR, BR)
    codes = jnp.where(filled, cells + 1, 0).reshape(SX, SY, SZ).astype(BF)
    return jnp.pad(codes, ((0, 0), (2, CODE - 2 - SY), (0, CH - SZ)))


def per_device(fine_feats, owner_of, arrival_slot, w_stride, w_conv, w_head, labels):
    devs = lax.axis_size("gx") * lax.axis_size("gy")
    per_dev, cells, in_width = fine_feats.shape
    cap = arrival_slot.shape[0] // devs
    feats = fine_feats.reshape(per_dev * cells, in_width)
    buffer, place = send(feats, owner_of, w_stride, devs, cap)

    brick, octant = arrival_slot >> 3, arrival_slot & 7
    deep = SZ // BR
    big_x = 2 * (brick // (BY * deep)) + (octant >> 2)
    big_y = 2 * (brick // deep % BY) + ((octant >> 1) & 1)
    big_z = 2 * (brick % deep) + (octant & 1)
    index = jnp.where(arrival_slot >= 0, (big_x * (SY // 2) + big_y) * (SZ // 2) + big_z, BRICKS)
    code = label_codes(arrival_slot, labels)
    order = brick_order()
    place, w_conv = lax.optimization_barrier((place, w_conv))
    taps = w_conv.reshape(9, 3, CH, CH)
    w_fwd = taps.transpose(0, 2, 1, 3).reshape(9 * CH, 3 * CH)
    w_bwd = taps.transpose(0, 3, 1, 2).reshape(9 * CH, 3 * CH)
    head = jnp.pad(jnp.concatenate([w_head, w_head], axis=1), ((0, 0), (0, CH - 16)))

    arrived, w_fwd, w_bwd = lax.optimization_barrier((to_all(buffer), w_fwd, w_bwd))
    slab, first, last_part = land(arrived, index, order, code)
    before, after = both_ways(first, last_part, "gx")
    inside = inner(slab, w_fwd, head, head.T)
    up, down = sides(slab, before, after, inside)
    left, right = both_ways(down, up, "gy")
    at_x = x_sides(slab, before, after, w_fwd, head, head.T)
    returned, grid, grad = core(
        jnp.minimum(index, BRICKS - 1),
        slab,
        before,
        after,
        left,
        right,
        inside,
        at_x,
        w_fwd,
        w_bwd,
        head,
        head.T,
        order.T,
    )
    came = to_all(returned)
    half = (lax.axis_index("gy") % 2).astype(jnp.int32).reshape(1)
    conv = sum_over_gy(*weights(half, grid, grad))
    mine, stride = last(came, place, feats)
    share = in_width // devs
    terms = to_all(jnp.concatenate([conv, stride.reshape(devs, share, CH)], axis=1))
    grad_fine = lax.dot_general(
        mine, w_stride, (((1,), (1,)), ((), ())), preferred_element_type=F32
    ).astype(BF)
    terms = terms.astype(F32).reshape(lax.axis_size("gx"), lax.axis_size("gy"), 4 + share, CH)
    by_part = jnp.sum(terms, axis=0)
    conv_sum = by_part[:, :4].reshape(-1, 2, 4, CH).transpose(1, 0, 2, 3).reshape(32, CH)
    block = jnp.concatenate([conv_sum, jnp.sum(by_part[:, 4:], axis=0)], axis=0).astype(BF)
    sums = to_all(jnp.broadcast_to(block[None], (devs,) + block.shape))
    scale = 1.0 / math.sqrt(per_dev * devs * cells)
    grad_conv = sums[:, :27].transpose(1, 0, 2).astype(F32) * scale
    grad_stride = sums[:, 32:].reshape(in_width, CH).astype(F32) * scale
    return (
        grad_fine.reshape(per_dev, cells, in_width),
        grad_stride,
        grad_conv,
    )


def solution(mesh):
    return jax.shard_map(
        per_device,
        mesh=mesh,
        in_specs=(
            P(("gx", "gy"), None, None),
            P(("gx", "gy")),
            P(("gx", "gy")),
            P(),
            P(),
            P(),
            P("gx", "gy", None),
        ),
        out_specs=(P(("gx", "gy"), None, None), P(), P()),
        check_vma=False,
    )
```

```python
import functools
import math

import jax
import jax.numpy as jnp
from jax import lax
from jax.experimental import pallas as pl
from jax.experimental.pallas import tpu as pltpu
from jax.sharding import PartitionSpec as P

BX = 2
BY = 2
BR = 4
SX = 8
SY = 8
SZ = 48
CH = 128
CELLS = 8
FX = SX + 4
FY = SY + 4
ROWS = SY * SZ
CODE = 16
SIDE = 2 * SZ
BRICKS = 384
PARTS = 4
VMEM = pltpu.CompilerParams(vmem_limit_bytes=24 * 1024 * 1024)
ALL_VMEM = pltpu.CompilerParams(vmem_limit_bytes=63 * 1024 * 1024)
BF = jnp.bfloat16
F32 = jnp.float32


def whole(shape):
    return pl.BlockSpec(shape, lambda: (0,) * len(shape))


def anywhere():
    return pl.BlockSpec(memory_space=pl.ANY)


def smem():
    return pl.BlockSpec(memory_space=pltpu.SMEM)


def matmul(a, b):
    return jnp.dot(a, b, preferred_element_type=F32)


def iota(shape, dim):
    return lax.broadcasted_iota(jnp.int32, shape, dim)


def send_kernel(
    cap, owner_hbm, feats_hbm, w_hbm, buf_hbm, place, owner, feats, w_stride, rows, buf, count, sems
):
    per_dev = owner.shape[0]
    devs = count.shape[0]
    part = feats.shape[0] // PARTS
    copies = [
        pltpu.make_async_copy(owner_hbm, owner, sems.at[0]),
        pltpu.make_async_copy(w_hbm, w_stride, sems.at[1]),
    ] + [
        pltpu.make_async_copy(
            feats_hbm.at[pl.ds(i * part, part)], feats.at[pl.ds(i * part, part)], sems.at[2 + i]
        )
        for i in range(PARTS)
    ]
    for copy in copies:
        copy.start()

    def clear(i, c):
        count[i] = 0
        return c

    lax.fori_loop(0, devs, clear, 0, unroll=8)
    buf[...] = jnp.zeros_like(buf)
    copies[0].wait()

    def find(i, c):
        who = owner[i]
        pos = count[who]
        count[who] = pos + 1
        place[i] = who * cap + pos
        return c

    lax.fori_loop(0, per_dev, find, 0, unroll=8)
    copies[1].wait()
    bricks = per_dev // PARTS
    for i in range(PARTS):
        copies[2 + i].wait()
        vals = matmul(feats[i * part : (i + 1) * part, :], w_stride[...])
        rows[i * bricks : (i + 1) * bricks] = vals.reshape(bricks, CELLS, CH)

    def put(i, c):
        buf[place[i]] = rows[i].astype(BF)
        return c

    lax.fori_loop(0, per_dev, put, 0, unroll=8)
    out = pltpu.make_async_copy(buf, buf_hbm, sems.at[0])
    out.start()
    out.wait()


def hbm():
    return pl.BlockSpec(memory_space=pltpu.HBM)


def send(feats, owner, w_stride, devs, cap):
    per_dev = owner.shape[0]
    return pl.pallas_call(
        functools.partial(send_kernel, cap),
        out_shape=(
            jax.ShapeDtypeStruct((devs * cap, CELLS, CH), BF),
            jax.ShapeDtypeStruct((per_dev,), jnp.int32),
        ),
        in_specs=[hbm(), hbm(), hbm()],
        out_specs=(hbm(), smem()),
        scratch_shapes=[
            pltpu.SMEM((per_dev,), jnp.int32),
            pltpu.VMEM(feats.shape, BF),
            pltpu.VMEM(w_stride.shape, BF),
            pltpu.VMEM((per_dev, CELLS, CH), F32),
            pltpu.VMEM((devs * cap, CELLS, CH), BF),
            pltpu.SMEM((devs,), jnp.int32),
            pltpu.SemaphoreType.DMA((2 + PARTS,)),
        ],
        compiler_params=ALL_VMEM,
        name="send_bricks",
    )(owner, feats, w_stride)


def brick_order():
    row = iota((4 * SZ, 4 * SZ), 0)
    col = iota((4 * SZ, 4 * SZ), 1)
    z = row % SZ
    return (col == (z // 2) * 8 + (row // SZ) * 2 + z % 2).astype(BF)


def land_kernel(index, arrived, order, code, slab, first, last, held):
    held[...] = jnp.zeros_like(held)

    def put(j, c):
        held[index[j]] = arrived[j].astype(F32)
        return c

    lax.fori_loop(0, index.shape[0], put, 0, unroll=8)
    for big_x in range(SX // 2):
        for big_y in range(SY // 2):
            start = (big_x * (SY // 2) + big_y) * (SZ // 2)
            block = held[start : start + SZ // 2].reshape(4 * SZ, CH).astype(BF)
            moved = matmul(order[...], block).astype(BF)
            for i in range(2):
                for l in range(2):
                    piece = moved[(2 * i + l) * SZ : (2 * i + l + 1) * SZ]
                    row = (2 * big_y + l) * SZ
                    slab[2 * big_x + i, row : row + SZ, :] = piece
    slab[:, ROWS:, :] = code[...]
    first[...] = slab[:2]
    last[...] = slab[SX - 2 :]


def land(arrived, index, order, code):
    shapes = ((SX, ROWS + CODE, CH), (2, ROWS + CODE, CH), (2, ROWS + CODE, CH))
    return pl.pallas_call(
        land_kernel,
        out_shape=tuple(jax.ShapeDtypeStruct(s, BF) for s in shapes),
        in_specs=[smem(), whole(arrived.shape), whole(order.shape), whole(code.shape)],
        out_specs=tuple(whole(s) for s in shapes),
        scratch_shapes=[pltpu.VMEM((BRICKS + 8, CELLS, CH), F32)],
        compiler_params=ALL_VMEM,
        name="land_bricks",
    )(index, arrived, order, code)


def sides_kernel(slab, before, after, inside, up, down):
    row = iota((CODE // 2, CH), 0)
    none = jnp.zeros((CODE // 2, CH), F32)
    for x in range(FX):
        if x < 2:
            ref, at = before, x
        elif x < 2 + SX:
            ref, at = slab, x - 2
        else:
            ref, at = after, x - 2 - SX
        up[x, :SIDE, :] = ref[at, ROWS - SIDE : ROWS, :]
        down[x, :SIDE, :] = ref[at, :SIDE, :]
        codes = ref[at, ROWS:, :].astype(F32)
        upper = jnp.where(row < 2, codes[8:], 0.0)
        lower = jnp.where((row == 2) | (row == 3), codes[:8], 0.0)
        up[x, SIDE:, :] = jnp.concatenate([upper, none], axis=0).astype(BF)
        down[x, SIDE:, :] = jnp.concatenate([none, lower], axis=0).astype(BF)


def sides(slab, before, after, inside):
    shape = (FX, SIDE + CODE, CH)
    return pl.pallas_call(
        sides_kernel,
        out_shape=(jax.ShapeDtypeStruct(shape, BF),) * 2,
        in_specs=[whole(slab.shape), whole(before.shape), whole(after.shape), anywhere()],
        out_specs=(whole(shape),) * 2,
        compiler_params=VMEM,
        name="y_sides",
    )(slab, before, after, inside)


def shifted(vals, z, by):
    rows = vals.shape[0]
    turned = pltpu.roll(vals, by % rows, 0)
    return jnp.where(z == (0 if by == 1 else SZ - 1), 0.0, turned)


def spread_codes(blocks):
    eye = (iota((SZ, CH), 0) == iota((SZ, CH), 1)).astype(F32)
    return jnp.concatenate([eye * block for block in blocks], axis=0).astype(BF)


def front(taps, spread, w_fwd, head, head_t):
    rows = spread.shape[0]
    lane = iota((rows, CH), 1)
    z = iota((rows // SZ, SZ, CH), 1).reshape(rows, CH)
    parts = matmul(jnp.concatenate(taps, axis=1), w_fwd)
    pre = (
        shifted(parts[:, :CH], z, 1)
        + parts[:, CH : 2 * CH]
        + shifted(parts[:, 2 * CH :], z, -1)
    )
    code = matmul(spread, jnp.ones((CH, CH), BF))
    mask = code > 0.5
    pre = jnp.where(mask, pre, 0.0)
    gate = jax.nn.sigmoid(pre)
    logits = matmul((pre * gate).astype(BF), head)
    target = (code - 1.0 == (lane % 8).astype(F32)).astype(F32)
    grad_logits = jnp.where(mask, jax.nn.sigmoid(logits) - target, 0.0)
    high = grad_logits.astype(BF).astype(F32)
    terms = jnp.where(lane < 8, high, jnp.where(lane < 16, grad_logits - high, 0.0))
    grad_act = matmul(terms.astype(BF), head_t)
    return (grad_act * gate * (1.0 + pre * (1.0 - gate))).astype(BF)


INNER = (SY - 2) * SZ


def front_cost(slabs):
    flops = 2 * 9 * 3 * CH * CH * INNER * slabs
    return pl.CostEstimate(flops=flops, bytes_accessed=4 * 2**20, transcendentals=0)


def inner_kernel(slab, w_fwd, head, head_t, grad):
    def step(x, carry):
        taps = [slab[x + e, f * SZ : f * SZ + INNER, :] for e in range(3) for f in range(3)]
        codes = slab[x + 1, ROWS:, :].astype(F32)
        spread = spread_codes([codes[y : y + 1] for y in range(3, SY + 1)])
        grad[x] = front(taps, spread, w_fwd[...], head[...], head_t[...])
        return carry

    lax.fori_loop(0, SX - 2, step, 0, unroll=2)


def inner(slab, w_fwd, head, head_t):
    arrays = (slab, w_fwd, head, head_t)
    shape = (SX - 2, INNER, CH)
    return pl.pallas_call(
        inner_kernel,
        out_shape=jax.ShapeDtypeStruct(shape, BF),
        in_specs=[whole(a.shape) for a in arrays],
        out_specs=whole(shape),
        compiler_params=VMEM,
        cost_estimate=front_cost(SX - 2),
        name="grad_pre_inside",
    )(*arrays)


def x_sides_kernel(slab, before, after, w_fwd, head, head_t, grad):
    def source(x):
        if x < 2:
            return before, x
        return (slab, x - 2) if x < SX + 2 else (after, x - SX - 2)

    for i, x in enumerate((0, 1, SX, SX + 1)):
        taps = []
        for e in range(3):
            ref, at = source(x + e)
            taps += [ref[at, f * SZ : f * SZ + INNER, :] for f in range(3)]
        ref, at = source(x + 1)
        codes = ref[at, ROWS:, :].astype(F32)
        spread = spread_codes([codes[y : y + 1] for y in range(3, SY + 1)])
        grad[i] = front(taps, spread, w_fwd[...], head[...], head_t[...])


def x_sides(slab, before, after, w_fwd, head, head_t):
    arrays = (slab, before, after, w_fwd, head, head_t)
    shape = (4, INNER, CH)
    return pl.pallas_call(
        x_sides_kernel,
        out_shape=jax.ShapeDtypeStruct(shape, BF),
        in_specs=[whole(a.shape) for a in arrays],
        out_specs=whole(shape),
        compiler_params=VMEM,
        cost_estimate=front_cost(4),
        name="grad_pre_x_sides",
    )(*arrays)


def core_kernel(
    index, slab, before, after, left, right, inside, at_x, w_fwd, w_bwd, head, head_t, order_t,
    back_hbm, kept_hbm, low, high, codes, grad, coarse, held, back, sems,
):
    middle = pl.ds(SIDE, ROWS)
    pairs = (
        (slab.at[:, pl.ds(0, ROWS)], kept_hbm.at[pl.ds(2, SX), middle]),
        (before.at[:, pl.ds(0, ROWS)], kept_hbm.at[pl.ds(0, 2), middle]),
        (after.at[:, pl.ds(0, ROWS)], kept_hbm.at[pl.ds(2 + SX, 2), middle]),
        (left.at[:, pl.ds(0, SIDE)], kept_hbm.at[pl.ds(0, FX), pl.ds(0, SIDE)]),
        (right.at[:, pl.ds(0, SIDE)], kept_hbm.at[pl.ds(0, FX), pl.ds(SIDE + ROWS, SIDE)]),
    )
    copies = [pltpu.make_async_copy(a, b, sems.at[i]) for i, (a, b) in enumerate(pairs)]
    for copy in copies:
        copy.start()
    for at, ref in ((0, before), (2, slab), (2 + SX, after)):
        many = ref.shape[0]
        low[at : at + many, SIDE:, :] = ref[:, :SIDE, :]
        high[at : at + many, :SIDE, :] = ref[:, ROWS - SIDE : ROWS, :]
        codes[at : at + many] = ref[:, ROWS:, :].astype(F32)
    low[:, :SIDE, :] = left[:, :SIDE, :]
    high[:, SIDE:, :] = right[:, :SIDE, :]
    codes[...] += left[:, SIDE:, :].astype(F32) + right[:, SIDE:, :].astype(F32)
    grad[:2, SIDE : SIDE + INNER, :] = at_x[:2]
    grad[2:SX, SIDE : SIDE + INNER, :] = inside[...]
    grad[SX:, SIDE : SIDE + INNER, :] = at_x[2:]

    z_own = iota((SY, SZ, CH), 1).reshape(ROWS, CH)

    def forward(pair, carry):
        x = 2 * pair
        taps = [
            jnp.concatenate(
                [
                    ref[x + i + e, f * SZ : f * SZ + SIDE, :]
                    for i in range(2)
                    for ref in (low, high)
                ],
                axis=0,
            )
            for e in range(3)
            for f in range(3)
        ]
        blocks = []
        for i in range(2):
            here = codes[x + i + 1]
            blocks += [here[y : y + 1] for y in (1, 2, SY + 1, SY + 2)]
        vals = front(taps, spread_codes(blocks), w_fwd[...], head[...], head_t[...])
        for i in range(2):
            grad[x + i, :SIDE, :] = vals[2 * i * SIDE : (2 * i + 1) * SIDE]
            grad[x + i, SIDE + INNER :, :] = vals[(2 * i + 1) * SIDE : (2 * i + 2) * SIDE]
        return carry

    lax.fori_loop(0, SX // 2 + 1, forward, 0, unroll=5)
    out = pltpu.make_async_copy(
        grad.at[pl.ds(1, SX), pl.ds(SZ, ROWS)],
        kept_hbm.at[pl.ds(FX, SX), pl.ds(0, ROWS)],
        sems.at[len(pairs)],
    )
    out.start()
    copies.append(out)

    def backward(x, carry):
        taps = jnp.concatenate(
            [
                grad[x + 2 - e, (2 - f) * SZ : (2 - f) * SZ + ROWS, :]
                for e in range(3)
                for f in range(3)
            ],
            axis=1,
        )
        parts = matmul(taps, w_bwd[...])
        coarse[x] = (
            shifted(parts[:, :CH], z_own, -1)
            + parts[:, CH : 2 * CH]
            + shifted(parts[:, 2 * CH :], z_own, 1)
        ).astype(BF)
        return carry

    lax.fori_loop(0, SX, backward, 0, unroll=2)

    for big_x in range(SX // 2):
        for big_y in range(SY // 2):
            block = jnp.concatenate(
                [
                    coarse[2 * big_x + i, (2 * big_y + l) * SZ : (2 * big_y + l + 1) * SZ, :]
                    for i in range(2)
                    for l in range(2)
                ],
                axis=0,
            )
            start = (big_x * (SY // 2) + big_y) * (SZ // 2)
            held[start : start + SZ // 2] = matmul(order_t[...], block).reshape(SZ // 2, CELLS, CH)

    def put(j, carry):
        back[j] = held[index[j]].astype(BF)
        return carry

    part = index.shape[0] // PARTS
    for i in range(PARTS):
        lax.fori_loop(i * part, (i + 1) * part, put, 0, unroll=8)
        rows = pl.ds(i * part, part)
        copy = pltpu.make_async_copy(back.at[rows], back_hbm.at[rows], sems.at[6 + i])
        copy.start()
        copies.append(copy)
    for copy in copies:
        copy.wait()


def core(
    index, slab, before, after, left, right, inside, at_x, w_fwd, w_bwd, head, head_t, order_t
):
    arrays = (
        slab, before, after, left, right, inside, at_x, w_fwd, w_bwd, head, head_t, order_t
    )
    shapes = ((index.shape[0], CELLS, CH), (FX + SX, FY * SZ, CH))
    return pl.pallas_call(
        core_kernel,
        out_shape=tuple(jax.ShapeDtypeStruct(s, BF) for s in shapes),
        in_specs=[smem()] + [whole(a.shape) for a in arrays],
        out_specs=(hbm(),) * 2,
        scratch_shapes=[
            pltpu.VMEM((FX, 2 * SIDE, CH), BF),
            pltpu.VMEM((FX, 2 * SIDE, CH), BF),
            pltpu.VMEM((FX, CODE, CH), F32),
            pltpu.VMEM((SX + 2, ROWS + SIDE, CH), BF),
            pltpu.VMEM((SX, ROWS, CH), BF),
            pltpu.VMEM((BRICKS, CELLS, CH), F32),
            pltpu.VMEM((index.shape[0], CELLS, CH), BF),
            pltpu.SemaphoreType.DMA((6 + PARTS,)),
        ],
        compiler_params=VMEM,
        name="conv_both_ways",
    )(index, *arrays)


def weights_kernel(half, kept, keep, give, total, taps_out):
    z_own = iota((SY, SZ, CH), 1).reshape(ROWS, CH)
    total[...] = jnp.zeros_like(total)

    def add(x, carry):
        here = kept[FX + x, :ROWS, :]
        mid = here.astype(F32)
        grads = jnp.concatenate(
            [shifted(mid, z_own, -1).astype(BF), here, shifted(mid, z_own, 1).astype(BF)],
            axis=1,
        )
        for e in range(3):
            taps = jnp.concatenate(
                [kept[x + 1 + e, (1 + f) * SZ : (1 + f) * SZ + ROWS, :] for f in range(3)], axis=1
            )
            total[e] += lax.dot_general(
                taps, grads, (((0,), (0,)), ((), ())), preferred_element_type=F32
            )
        return carry

    lax.fori_loop(0, SX, add, 0, unroll=2)
    for tap in range(27):
        e, f, g = tap // 9, tap // 3 % 3, tap % 3
        taps_out[tap] = total[e, f * CH : (f + 1) * CH, g * CH : (g + 1) * CH]
    taps_out[27:] = jnp.zeros((5, CH, CH), F32)
    mine = half[0]
    keep[...] = taps_out[pl.ds(16 * mine, 16)]
    give[...] = taps_out[pl.ds(16 * (1 - mine), 16)].astype(BF)


def weights(half, kept):
    shape = (16, CH, CH)
    return pl.pallas_call(
        weights_kernel,
        out_shape=(jax.ShapeDtypeStruct(shape, F32), jax.ShapeDtypeStruct(shape, BF)),
        in_specs=[smem(), whole(kept.shape)],
        out_specs=(whole(shape),) * 2,
        scratch_shapes=[pltpu.VMEM((3, 3 * CH, 3 * CH), F32), pltpu.VMEM((32, CH, CH), F32)],
        compiler_params=VMEM,
        cost_estimate=pl.CostEstimate(
            flops=2 * 27 * CH * CH * SX * ROWS, bytes_accessed=6 * 2**20, transcendentals=0
        ),
        name="conv_weight_grad",
    )(half, kept)


def pair_kernel(me, keep, got, *outs):
    both = keep[...] + got[...].astype(F32).reshape(keep.shape)
    turned = jnp.concatenate([both[:, :, 4:], both[:, :, :4]], axis=2)
    for by, out in enumerate(outs):
        y = lax.rem(me[0] + by, len(outs))
        part = jnp.where(y % 2 == 0, both, turned)
        part = jnp.where(y < 2, part[:, 0], part[:, 1])
        out[...] = part[:, :4].astype(out.dtype)


def add_pair(y, keep, got, ring, devs):
    shape = (devs, 4, CH)
    kinds = (F32,) + (BF,) * (ring - 1)
    keep = keep.reshape(devs, 2, 8, CH)
    got = got.reshape(devs, 16, CH)
    return pl.pallas_call(
        pair_kernel,
        out_shape=tuple(jax.ShapeDtypeStruct(shape, kind) for kind in kinds),
        in_specs=[smem(), whole(keep.shape), whole(got.shape)],
        out_specs=(whole(shape),) * ring,
        compiler_params=ALL_VMEM,
        name="add_pair",
    )(y, keep, got)


def sum_over_gy(keep, give, devs):
    me = lax.axis_index("gy")
    y = me // 2
    peers = lax.axis_size("gy")
    ring = peers // 2
    got = lax.ppermute(give, "gy", [(i, i ^ 1) for i in range(peers)])
    parts = add_pair(y.astype(jnp.int32).reshape(1), keep, got, ring, devs)
    perms = [[(i, (i + 2 * by) % peers) for i in range(peers)] for by in range(ring)]
    return parts[:1] + tuple(
        lax.ppermute(part, "gy", perm) for part, perm in zip(parts[1:], perms[1:])
    )


def last_kernel(place, came, feats, mine, stride, rows):
    per_dev = place.shape[0]

    def take(i, carry):
        rows[i] = came[place[i]].astype(F32)
        return carry

    lax.fori_loop(0, per_dev, take, 0, unroll=8)
    vals = rows[...].reshape(per_dev * CELLS, CH).astype(BF)
    mine[...] = vals
    stride[...] = lax.dot_general(
        feats[...], vals, (((0,), (0,)), ((), ())), preferred_element_type=F32
    ).astype(BF)


def last(came, place, feats):
    shapes = ((feats.shape[0], CH), (feats.shape[1], CH))
    return pl.pallas_call(
        last_kernel,
        out_shape=tuple(jax.ShapeDtypeStruct(s, BF) for s in shapes),
        in_specs=[smem(), whole(came.shape), whole(feats.shape)],
        out_specs=tuple(whole(s) for s in shapes),
        scratch_shapes=[pltpu.VMEM((place.shape[0], CELLS, CH), F32)],
        compiler_params=ALL_VMEM,
        name="stride_term",
    )(place, came, feats)


def to_all(buffer):
    return lax.all_to_all(buffer, ("gx", "gy"), split_axis=0, concat_axis=0, tiled=True)


def both_ways(first, last_part, axis):
    peers = lax.axis_size(axis)
    up = [(i, i + 1) for i in range(peers - 1)]
    down = [(i + 1, i) for i in range(peers - 1)]
    return lax.ppermute(last_part, axis, up), lax.ppermute(first, axis, down)


def label_codes(arrival_slot, labels):
    bricks = BX * BY * SZ // BR
    filled = jnp.any(
        (arrival_slot >> 3)[None, :] == jnp.arange(bricks, dtype=jnp.int32)[:, None], axis=1
    ).reshape(BX, 1, BY, 1, SZ // BR, 1)
    cells = labels.reshape(BX, BR, BY, BR, SZ // BR, BR)
    codes = jnp.where(filled, cells + 1, 0).reshape(SX, SY, SZ).astype(BF)
    return jnp.pad(codes, ((0, 0), (2, CODE - 2 - SY), (0, CH - SZ)))


def per_device(fine_feats, owner_of, arrival_slot, w_stride, w_conv, w_head, labels):
    devs = lax.axis_size("gx") * lax.axis_size("gy")
    per_dev, cells, in_width = fine_feats.shape
    cap = arrival_slot.shape[0] // devs
    feats = fine_feats.reshape(per_dev * cells, in_width)
    buffer, place = send(feats, owner_of, w_stride, devs, cap)

    brick, octant = arrival_slot >> 3, arrival_slot & 7
    deep = SZ // BR
    big_x = 2 * (brick // (BY * deep)) + (octant >> 2)
    big_y = 2 * (brick // deep % BY) + ((octant >> 1) & 1)
    big_z = 2 * (brick % deep) + (octant & 1)
    index = jnp.where(arrival_slot >= 0, (big_x * (SY // 2) + big_y) * (SZ // 2) + big_z, BRICKS)
    code = label_codes(arrival_slot, labels)
    order = brick_order()
    place, w_conv = lax.optimization_barrier((place, w_conv))
    taps = w_conv.reshape(9, 3, CH, CH)
    w_fwd = taps.transpose(0, 2, 1, 3).reshape(9 * CH, 3 * CH)
    w_bwd = taps.transpose(0, 3, 1, 2).reshape(9 * CH, 3 * CH)
    head = jnp.pad(jnp.concatenate([w_head, w_head], axis=1), ((0, 0), (0, CH - 16)))

    arrived, w_fwd, w_bwd = lax.optimization_barrier((to_all(buffer), w_fwd, w_bwd))
    slab, first, last_part = land(arrived, index, order, code)
    before, after = both_ways(first, last_part, "gx")
    inside = inner(slab, w_fwd, head, head.T)
    up, down = sides(slab, before, after, inside)
    left, right = both_ways(down, up, "gy")
    at_x = x_sides(slab, before, after, w_fwd, head, head.T)
    returned, kept = core(
        jnp.minimum(index, BRICKS - 1),
        slab,
        before,
        after,
        left,
        right,
        inside,
        at_x,
        w_fwd,
        w_bwd,
        head,
        head.T,
        order.T,
    )
    came = to_all(returned)
    half = (lax.axis_index("gy") % 2).astype(jnp.int32).reshape(1)
    terms = sum_over_gy(*weights(half, kept), devs)
    mine, stride = last(came, place, feats)
    terms, stride = lax.optimization_barrier((terms, stride))
    conv = sum(term.astype(F32) for term in terms).astype(BF)
    share = in_width // devs
    rows = conv.shape[1]
    terms = to_all(jnp.concatenate([conv, stride.reshape(devs, share, CH)], axis=1))
    grad_fine = lax.dot_general(
        mine, w_stride, (((1,), (1,)), ((), ())), preferred_element_type=F32
    ).astype(BF)
    terms = terms.astype(F32).reshape(lax.axis_size("gx"), -1, 2, rows + share, CH)
    by_part = jnp.sum(terms, axis=0)
    conv_sum = by_part[:, :, :rows].transpose(1, 0, 2, 3).reshape(2, -1, CH)
    stride_sum = jnp.sum(by_part[:, :, rows:], axis=(0, 1))
    block = jnp.concatenate(
        [conv_sum, jnp.broadcast_to(stride_sum, (2,) + stride_sum.shape)], axis=1
    ).astype(BF)
    block, grad_fine = lax.optimization_barrier((block, grad_fine))
    sums = to_all(jnp.broadcast_to(block, (devs // 2,) + block.shape).reshape(devs, -1, CH))
    scale = 1.0 / math.sqrt(per_dev * devs * cells)
    mine = sums[:, :-share].reshape(-1, CH)
    swap = [(i, i ^ 1) for i in range(lax.axis_size("gy"))]
    other = lax.ppermute(mine, "gy", swap)
    first_core = half[0] == 0
    grad_conv = jnp.concatenate(
        [
            jnp.where(first_core, mine, other),
            jnp.where(first_core, other, mine)[: 27 * CH - mine.shape[0]],
        ],
        axis=0,
    ).astype(F32).reshape(27, CH, CH) * scale
    grad_stride = sums[:, -share:].reshape(in_width, CH).astype(F32) * scale
    return (
        grad_fine.reshape(per_dev, cells, in_width),
        grad_stride,
        grad_conv,
    )


def solution(mesh):
    return jax.shard_map(
        per_device,
        mesh=mesh,
        in_specs=(
            P(("gx", "gy"), None, None),
            P(("gx", "gy")),
            P(("gx", "gy")),
            P(),
            P(),
            P(),
            P("gx", "gy", None),
        ),
        out_specs=(P(("gx", "gy"), None, None), P(), P()),
        check_vma=False,
    )
```

```python
import functools
import math

import jax
import jax.numpy as jnp
from jax import lax
from jax.experimental import pallas as pl
from jax.experimental.pallas import tpu as pltpu
from jax.sharding import PartitionSpec as P

BX = 2
BY = 2
BR = 4
SX = 8
SY = 8
SZ = 48
CH = 128
CELLS = 8
FX = SX + 4
FY = SY + 4
ROWS = SY * SZ
CODE = 16
SIDE = 2 * SZ
BRICKS = 384
KEPT = 84
PARTS = 4
VMEM = pltpu.CompilerParams(vmem_limit_bytes=24 * 1024 * 1024)
MOST_VMEM = pltpu.CompilerParams(vmem_limit_bytes=48 * 1024 * 1024)
ALL_VMEM = pltpu.CompilerParams(vmem_limit_bytes=63 * 1024 * 1024)
BF = jnp.bfloat16
F32 = jnp.float32


def whole(shape):
    return pl.BlockSpec(shape, lambda: (0,) * len(shape))


def anywhere():
    return pl.BlockSpec(memory_space=pl.ANY)


def smem():
    return pl.BlockSpec(memory_space=pltpu.SMEM)


def matmul(a, b):
    return jnp.dot(a, b, preferred_element_type=F32)


def iota(shape, dim):
    return lax.broadcasted_iota(jnp.int32, shape, dim)


def send_kernel(
    cap, owner_hbm, feats_hbm, w_hbm, buf_hbm, place, owner, feats, w_stride, rows, buf, count, sems
):
    per_dev = owner.shape[0]
    devs = count.shape[0]
    part = feats.shape[0] // PARTS
    copies = [
        pltpu.make_async_copy(owner_hbm, owner, sems.at[0]),
        pltpu.make_async_copy(w_hbm, w_stride, sems.at[1]),
    ] + [
        pltpu.make_async_copy(
            feats_hbm.at[pl.ds(i * part, part)], feats.at[pl.ds(i * part, part)], sems.at[2 + i]
        )
        for i in range(PARTS)
    ]
    for copy in copies:
        copy.start()

    def clear(i, c):
        count[i] = 0
        return c

    lax.fori_loop(0, devs, clear, 0, unroll=8)
    buf[...] = jnp.zeros_like(buf)
    copies[0].wait()

    def find(i, c):
        who = owner[i]
        pos = count[who]
        count[who] = pos + 1
        place[i] = who * cap + pos
        return c

    lax.fori_loop(0, per_dev, find, 0, unroll=8)
    copies[1].wait()
    bricks = per_dev // PARTS
    for i in range(PARTS):
        copies[2 + i].wait()
        vals = matmul(feats[i * part : (i + 1) * part, :], w_stride[...])
        rows[i * bricks : (i + 1) * bricks] = vals.reshape(bricks, CELLS, CH).astype(BF)

    def put(i, c):
        buf[place[i]] = rows[i]
        return c

    lax.fori_loop(0, per_dev, put, 0, unroll=8)
    out = pltpu.make_async_copy(buf, buf_hbm, sems.at[0])
    out.start()
    out.wait()


def hbm():
    return pl.BlockSpec(memory_space=pltpu.HBM)


def send(feats, owner, w_stride, devs, cap):
    per_dev = owner.shape[0]
    return pl.pallas_call(
        functools.partial(send_kernel, cap),
        out_shape=(
            jax.ShapeDtypeStruct((devs * cap, CELLS, CH), BF),
            jax.ShapeDtypeStruct((per_dev,), jnp.int32),
        ),
        in_specs=[hbm(), hbm(), hbm()],
        out_specs=(hbm(), smem()),
        scratch_shapes=[
            pltpu.SMEM((per_dev,), jnp.int32),
            pltpu.VMEM(feats.shape, BF),
            pltpu.VMEM(w_stride.shape, BF),
            pltpu.VMEM((per_dev, CELLS, CH), BF),
            pltpu.VMEM((devs * cap, CELLS, CH), BF),
            pltpu.SMEM((devs,), jnp.int32),
            pltpu.SemaphoreType.DMA((2 + PARTS,)),
        ],
        compiler_params=ALL_VMEM,
        name="send_bricks",
    )(owner, feats, w_stride)


def brick_order():
    row = iota((4 * SZ, 4 * SZ), 0)
    col = iota((4 * SZ, 4 * SZ), 1)
    z = row % SZ
    return (col == (z // 2) * 8 + (row // SZ) * 2 + z % 2).astype(BF)


def land_kernel(index, arrived, order, code, slab, first, last, held):
    held[...] = jnp.zeros_like(held)

    def put(j, c):
        held[index[j]] = arrived[j]
        return c

    lax.fori_loop(0, index.shape[0], put, 0, unroll=8)
    for big_x in range(SX // 2):
        for big_y in range(SY // 2):
            start = (big_x * (SY // 2) + big_y) * (SZ // 2)
            block = held[start : start + SZ // 2].astype(F32).reshape(4 * SZ, CH).astype(BF)
            moved = matmul(order[...], block).astype(BF)
            for i in range(2):
                for l in range(2):
                    piece = moved[(2 * i + l) * SZ : (2 * i + l + 1) * SZ]
                    row = (2 * big_y + l) * SZ
                    slab[2 * big_x + i, row : row + SZ, :] = piece
    slab[:, ROWS:, :] = code[...]
    first[...] = slab[:2]
    last[...] = slab[SX - 2 :]


def land(arrived, index, order, code):
    shapes = ((SX, ROWS + CODE, CH), (2, ROWS + CODE, CH), (2, ROWS + CODE, CH))
    return pl.pallas_call(
        land_kernel,
        out_shape=tuple(jax.ShapeDtypeStruct(s, BF) for s in shapes),
        in_specs=[smem(), whole(arrived.shape), whole(order.shape), whole(code.shape)],
        out_specs=tuple(whole(s) for s in shapes),
        scratch_shapes=[pltpu.VMEM((BRICKS + 8, CELLS, CH), BF)],
        compiler_params=ALL_VMEM,
        name="land_bricks",
    )(index, arrived, order, code)


def sides_kernel(slab, before, after, inside, up, down):
    row = iota((CODE // 2, CH), 0)
    none = jnp.zeros((CODE // 2, CH), F32)
    for x in range(FX):
        if x < 2:
            ref, at = before, x
        elif x < 2 + SX:
            ref, at = slab, x - 2
        else:
            ref, at = after, x - 2 - SX
        up[x, :SIDE, :] = ref[at, ROWS - SIDE : ROWS, :]
        down[x, :SIDE, :] = ref[at, :SIDE, :]
        codes = ref[at, ROWS:, :].astype(F32)
        upper = jnp.where(row < 2, codes[8:], 0.0)
        lower = jnp.where((row == 2) | (row == 3), codes[:8], 0.0)
        up[x, SIDE:, :] = jnp.concatenate([upper, none], axis=0).astype(BF)
        down[x, SIDE:, :] = jnp.concatenate([none, lower], axis=0).astype(BF)


def sides(slab, before, after, inside):
    shape = (FX, SIDE + CODE, CH)
    return pl.pallas_call(
        sides_kernel,
        out_shape=(jax.ShapeDtypeStruct(shape, BF),) * 2,
        in_specs=[whole(slab.shape), whole(before.shape), whole(after.shape), anywhere()],
        out_specs=(whole(shape),) * 2,
        compiler_params=VMEM,
        name="y_sides",
    )(slab, before, after, inside)


def shifted(vals, z, by):
    rows = vals.shape[0]
    turned = pltpu.roll(vals, by % rows, 0)
    return jnp.where(z == (0 if by == 1 else SZ - 1), 0.0, turned)


def spread_codes(blocks):
    eye = (iota((SZ, CH), 0) == iota((SZ, CH), 1)).astype(F32)
    return jnp.concatenate([eye * block for block in blocks], axis=0).astype(BF)


def convolve(columns, w_side, w_mid):
    sides = [
        jnp.concatenate([columns[i + e][f] for e in range(3) for f in range(3)], axis=1)
        for i in range(2)
    ]
    outer = matmul(jnp.concatenate(sides, axis=0), w_side)
    middle = matmul(jnp.concatenate([part for four in columns for part in four], axis=1), w_mid)
    middle = jnp.concatenate([middle[:, :CH], middle[:, CH:]], axis=0)
    return outer[:, :CH], middle, outer[:, CH:]


def front(columns, spread, w_side, w_mid, head, head_t):
    rows = spread.shape[0]
    lane = iota((rows, CH), 1)
    z = iota((rows // SZ, SZ, CH), 1).reshape(rows, CH)
    below, middle, above = convolve(columns, w_side, w_mid)
    pre = shifted(below, z, 1) + middle + shifted(above, z, -1)
    code = matmul(spread, jnp.ones((CH, CH), BF))
    mask = code > 0.5
    pre = jnp.where(mask, pre, 0.0)
    gate = jax.nn.sigmoid(pre)
    logits = matmul((pre * gate).astype(BF), head)
    target = (code - 1.0 == (lane % 8).astype(F32)).astype(F32)
    grad_logits = jnp.where(mask, jax.nn.sigmoid(logits) - target, 0.0)
    high = grad_logits.astype(BF).astype(F32)
    terms = jnp.where(lane < 8, high, jnp.where(lane < 16, grad_logits - high, 0.0))
    grad_act = matmul(terms.astype(BF), head_t)
    return (grad_act * gate * (1.0 + pre * (1.0 - gate))).astype(BF)


INNER = (SY - 2) * SZ


def front_cost(slabs):
    flops = 2 * 9 * 3 * CH * CH * INNER * slabs
    return pl.CostEstimate(flops=flops, bytes_accessed=4 * 2**20, transcendentals=0)


def inner_kernel(slab, w_side, w_mid, head, head_t, grad):
    def step(pair, carry):
        x = 2 * pair
        columns = [[slab[x + i, f * SZ : f * SZ + INNER, :] for f in range(3)] for i in range(4)]
        blocks = []
        for i in range(2):
            codes = slab[x + i + 1, ROWS:, :].astype(F32)
            blocks += [codes[y : y + 1] for y in range(3, SY + 1)]
        vals = front(
            columns, spread_codes(blocks), w_side[...], w_mid[...], head[...], head_t[...]
        )
        for i in range(2):
            grad[x + i] = vals[i * INNER : (i + 1) * INNER]
        return carry

    lax.fori_loop(0, SX // 2 - 1, step, 0, unroll=SX // 2 - 1)


def inner(slab, weights):
    arrays = (slab,) + weights
    shape = (SX - 2, INNER, CH)
    return pl.pallas_call(
        inner_kernel,
        out_shape=jax.ShapeDtypeStruct(shape, BF),
        in_specs=[whole(a.shape) for a in arrays],
        out_specs=whole(shape),
        compiler_params=VMEM,
        cost_estimate=front_cost(SX - 2),
        name="grad_pre_inside",
    )(*arrays)


def x_sides_kernel(slab, before, after, w_side, w_mid, head, head_t, grad):
    def source(x):
        if x < 2:
            return before, x
        return (slab, x - 2) if x < SX + 2 else (after, x - SX - 2)

    for pair, x in enumerate((0, SX)):
        slabs = [source(x + i) for i in range(4)]
        columns = [
            [ref[at, f * SZ : f * SZ + INNER, :] for f in range(3)] for ref, at in slabs
        ]
        blocks = []
        for ref, at in slabs[1:3]:
            codes = ref[at, ROWS:, :].astype(F32)
            blocks += [codes[y : y + 1] for y in range(3, SY + 1)]
        vals = front(
            columns, spread_codes(blocks), w_side[...], w_mid[...], head[...], head_t[...]
        )
        for i in range(2):
            grad[2 * pair + i] = vals[i * INNER : (i + 1) * INNER]


def x_sides(slab, before, after, weights):
    arrays = (slab, before, after) + weights
    shape = (4, INNER, CH)
    return pl.pallas_call(
        x_sides_kernel,
        out_shape=jax.ShapeDtypeStruct(shape, BF),
        in_specs=[whole(a.shape) for a in arrays],
        out_specs=whole(shape),
        compiler_params=VMEM,
        cost_estimate=front_cost(4),
        name="grad_pre_x_sides",
    )(*arrays)


def core_kernel(
    index, slab, before, after, left, right, inside, at_x,
    w_side, w_mid, head, head_t, w_side_t, w_mid_t, order_t,
    back_hbm, kept_hbm, low, high, codes, grad, coarse, held, back, sems,
):
    middle = pl.ds(SIDE, ROWS)
    pairs = (
        (slab.at[:, pl.ds(0, ROWS)], kept_hbm.at[pl.ds(2, SX), middle]),
        (before.at[:, pl.ds(0, ROWS)], kept_hbm.at[pl.ds(0, 2), middle]),
        (after.at[:, pl.ds(0, ROWS)], kept_hbm.at[pl.ds(2 + SX, 2), middle]),
        (left.at[:, pl.ds(0, SIDE)], kept_hbm.at[pl.ds(0, FX), pl.ds(0, SIDE)]),
        (right.at[:, pl.ds(0, SIDE)], kept_hbm.at[pl.ds(0, FX), pl.ds(SIDE + ROWS, SIDE)]),
    )
    copies = [pltpu.make_async_copy(a, b, sems.at[i]) for i, (a, b) in enumerate(pairs)]
    for copy in copies:
        copy.start()
    for at, ref in ((0, before), (2, slab), (2 + SX, after)):
        many = ref.shape[0]
        low[at : at + many, SIDE:, :] = ref[:, :SIDE, :]
        high[at : at + many, :SIDE, :] = ref[:, ROWS - SIDE : ROWS, :]
        codes[at : at + many] = ref[:, ROWS:, :].astype(F32)
    low[:, :SIDE, :] = left[:, :SIDE, :]
    high[:, SIDE:, :] = right[:, :SIDE, :]
    codes[...] += left[:, SIDE:, :].astype(F32) + right[:, SIDE:, :].astype(F32)
    grad[:2, SIDE : SIDE + INNER, :] = at_x[:2]
    grad[2:SX, SIDE : SIDE + INNER, :] = inside[...]
    grad[SX:, SIDE : SIDE + INNER, :] = at_x[2:]

    z_own = iota((2 * SY, SZ, CH), 1).reshape(2 * ROWS, CH)

    def forward(pair, carry):
        x = 2 * pair
        columns = [
            [
                jnp.concatenate(
                    [ref[x + i, f * SZ : f * SZ + SIDE, :] for ref in (low, high)], axis=0
                )
                for f in range(3)
            ]
            for i in range(4)
        ]
        blocks = []
        for i in range(2):
            here = codes[x + i + 1]
            blocks += [here[y : y + 1] for y in (1, 2, SY + 1, SY + 2)]
        vals = front(
            columns, spread_codes(blocks), w_side[...], w_mid[...], head[...], head_t[...]
        )
        for i in range(2):
            grad[x + i, :SIDE, :] = vals[2 * i * SIDE : (2 * i + 1) * SIDE]
            grad[x + i, SIDE + INNER :, :] = vals[(2 * i + 1) * SIDE : (2 * i + 2) * SIDE]
        return carry

    lax.fori_loop(0, SX // 2 + 1, forward, 0, unroll=5)
    out = pltpu.make_async_copy(
        grad.at[pl.ds(1, SX), pl.ds(SZ, ROWS)],
        kept_hbm.at[pl.ds(FX, SX), pl.ds(0, ROWS)],
        sems.at[len(pairs)],
    )
    out.start()
    copies.append(out)

    def backward(pair, carry):
        x = 2 * pair
        columns = [[grad[x + i, f * SZ : f * SZ + ROWS, :] for f in range(3)] for i in range(4)]
        below, middle, above = convolve(columns, w_side_t[...], w_mid_t[...])
        vals = (shifted(below, z_own, -1) + middle + shifted(above, z_own, 1)).astype(BF)
        for i in range(2):
            coarse[x + i] = vals[i * ROWS : (i + 1) * ROWS]
        return carry

    lax.fori_loop(0, SX // 2, backward, 0, unroll=2)

    for big_x in range(SX // 2):
        for big_y in range(SY // 2):
            block = jnp.concatenate(
                [
                    coarse[2 * big_x + i, (2 * big_y + l) * SZ : (2 * big_y + l + 1) * SZ, :]
                    for i in range(2)
                    for l in range(2)
                ],
                axis=0,
            )
            start = (big_x * (SY // 2) + big_y) * (SZ // 2)
            moved = matmul(order_t[...], block).reshape(SZ // 2, CELLS, CH)
            held[start : start + SZ // 2] = moved.astype(BF)

    def put(j, carry):
        back[j] = held[index[j]]
        return carry

    part = index.shape[0] // PARTS
    for i in range(PARTS):
        lax.fori_loop(i * part, (i + 1) * part, put, 0, unroll=8)
        rows = pl.ds(i * part, part)
        copy = pltpu.make_async_copy(back.at[rows], back_hbm.at[rows], sems.at[6 + i])
        copy.start()
        copies.append(copy)
    for copy in copies:
        copy.wait()


def core(
    index, slab, before, after, left, right, inside, at_x, weights, weights_t, order_t
):
    arrays = (slab, before, after, left, right, inside, at_x) + weights + weights_t + (order_t,)
    shapes = ((index.shape[0], CELLS, CH), (KEPT, FY * SZ, CH))
    return pl.pallas_call(
        core_kernel,
        out_shape=tuple(jax.ShapeDtypeStruct(s, BF) for s in shapes),
        in_specs=[smem()] + [whole(a.shape) for a in arrays],
        out_specs=(hbm(),) * 2,
        scratch_shapes=[
            pltpu.VMEM((FX, 2 * SIDE, CH), BF),
            pltpu.VMEM((FX, 2 * SIDE, CH), BF),
            pltpu.VMEM((FX, CODE, CH), F32),
            pltpu.VMEM((SX + 2, ROWS + SIDE, CH), BF),
            pltpu.VMEM((SX, ROWS, CH), BF),
            pltpu.VMEM((BRICKS, CELLS, CH), BF),
            pltpu.VMEM((index.shape[0], CELLS, CH), BF),
            pltpu.SemaphoreType.DMA((6 + PARTS,)),
        ],
        compiler_params=MOST_VMEM,
        name="conv_both_ways",
    )(index, *arrays)


def weights_kernel(half, kept_hbm, keep, give, kept, total, taps_out, sem):
    copy = pltpu.make_async_copy(kept_hbm.at[pl.ds(0, FX + SX)], kept, sem)
    copy.start()
    copy.wait()
    z_own = iota((SY, SZ, CH), 1).reshape(ROWS, CH)
    total[...] = jnp.zeros_like(total)

    def add(x, carry):
        here = kept[FX + x, :ROWS, :]
        mid = here.astype(F32)
        grads = jnp.concatenate(
            [shifted(mid, z_own, -1).astype(BF), here, shifted(mid, z_own, 1).astype(BF)],
            axis=1,
        )
        for e in range(3):
            taps = jnp.concatenate(
                [kept[x + 1 + e, (1 + f) * SZ : (1 + f) * SZ + ROWS, :] for f in range(3)], axis=1
            )
            total[e] += lax.dot_general(
                taps, grads, (((0,), (0,)), ((), ())), preferred_element_type=F32
            )
        return carry

    lax.fori_loop(0, SX, add, 0, unroll=2)
    for tap in range(27):
        e, f, g = tap // 9, tap // 3 % 3, tap % 3
        taps_out[tap] = total[e, f * CH : (f + 1) * CH, g * CH : (g + 1) * CH]
    taps_out[27:] = jnp.zeros((5, CH, CH), F32)
    mine = half[0]
    keep[...] = taps_out[pl.ds(16 * mine, 16)]
    give[...] = taps_out[pl.ds(16 * (1 - mine), 16)].astype(BF)


def weights(half, kept):
    shape = (16, CH, CH)
    return pl.pallas_call(
        weights_kernel,
        out_shape=(jax.ShapeDtypeStruct(shape, F32), jax.ShapeDtypeStruct(shape, BF)),
        in_specs=[smem(), hbm()],
        out_specs=(whole(shape),) * 2,
        scratch_shapes=[
            pltpu.VMEM((FX + SX, FY * SZ, CH), BF),
            pltpu.VMEM((3, 3 * CH, 3 * CH), F32),
            pltpu.VMEM((32, CH, CH), F32),
            pltpu.SemaphoreType.DMA,
        ],
        compiler_params=ALL_VMEM,
        cost_estimate=pl.CostEstimate(
            flops=2 * 27 * CH * CH * SX * ROWS, bytes_accessed=6 * 2**20, transcendentals=0
        ),
        name="conv_weight_grad",
    )(half, kept)


def pair_kernel(me, keep, got, *outs):
    both = keep[...] + got[...].astype(F32).reshape(keep.shape)
    for by, out in enumerate(outs):
        y = lax.rem(me[0] + by, len(outs))
        part = jnp.where(y < 2, both[:, :, 0], both[:, :, 1])
        low = jnp.concatenate([part[:, 0, :4], part[:, 1, :4]], axis=1)
        high = jnp.concatenate([part[:, 0, 4:], part[:, 1, 4:]], axis=1)
        out[...] = jnp.where(y % 2 == 0, low, high).astype(out.dtype)


def add_pair(y, keep, got, ring, devs):
    shape = (devs // 2, 8, CH)
    kinds = (F32,) + (BF,) * (ring - 1)
    keep = keep.reshape(devs // 2, 2, 2, 8, CH)
    got = got.reshape(devs, 16, CH)
    return pl.pallas_call(
        pair_kernel,
        out_shape=tuple(jax.ShapeDtypeStruct(shape, kind) for kind in kinds),
        in_specs=[smem(), whole(keep.shape), whole(got.shape)],
        out_specs=(whole(shape),) * ring,
        compiler_params=ALL_VMEM,
        name="add_pair",
    )(y, keep, got)


def sum_over_gy(keep, give, devs):
    me = lax.axis_index("gy")
    y = me // 2
    peers = lax.axis_size("gy")
    ring = peers // 2
    got = lax.ppermute(give, "gy", [(i, i ^ 1) for i in range(peers)])
    parts = add_pair(y.astype(jnp.int32).reshape(1), keep, got, ring, devs)
    perms = [[(i, (i + 2 * by) % peers) for i in range(peers)] for by in range(ring)]
    return parts[:1] + tuple(
        lax.ppermute(part, "gy", perm) for part, perm in zip(parts[1:], perms[1:])
    )


def last_kernel(place, came, feats, mine, stride, rows):
    per_dev = place.shape[0]

    def take(i, carry):
        rows[i] = came[place[i]]
        return carry

    lax.fori_loop(0, per_dev, take, 0, unroll=8)
    vals = rows[...].astype(F32).reshape(per_dev * CELLS, CH).astype(BF)
    mine[...] = vals
    stride[...] = lax.dot_general(
        feats[...], vals, (((0,), (0,)), ((), ())), preferred_element_type=F32
    ).astype(BF)


def last(came, place, feats):
    shapes = ((feats.shape[0], CH), (feats.shape[1], CH))
    return pl.pallas_call(
        last_kernel,
        out_shape=tuple(jax.ShapeDtypeStruct(s, BF) for s in shapes),
        in_specs=[smem(), whole(came.shape), whole(feats.shape)],
        out_specs=tuple(whole(s) for s in shapes),
        scratch_shapes=[pltpu.VMEM((place.shape[0], CELLS, CH), BF)],
        compiler_params=ALL_VMEM,
        name="stride_term",
    )(place, came, feats)


def terms_kernel(stride, *refs):
    terms, out = refs[:-1], refs[-1]
    conv = sum(term[...].astype(F32) for term in terms)
    both = stride[...].astype(F32)
    out[:, 0] = jnp.concatenate([conv[:, :4], both[:, :4]], axis=1).astype(BF)
    out[:, 1] = jnp.concatenate([conv[:, 4:], both[:, 4:]], axis=1).astype(BF)


def put_together(stride, terms):
    shape = terms[0].shape
    arrays = (stride.reshape(shape),) + tuple(terms)
    return pl.pallas_call(
        terms_kernel,
        out_shape=jax.ShapeDtypeStruct((shape[0], 2) + shape[1:], BF),
        in_specs=[whole(shape) for a in arrays],
        out_specs=whole((shape[0], 2) + shape[1:]),
        compiler_params=VMEM,
        name="put_together",
    )(*arrays)


def to_all(buffer):
    return lax.all_to_all(buffer, ("gx", "gy"), split_axis=0, concat_axis=0, tiled=True)


def both_ways(first, last_part, axis):
    peers = lax.axis_size(axis)
    up = [(i, i + 1) for i in range(peers - 1)]
    down = [(i + 1, i) for i in range(peers - 1)]
    return lax.ppermute(last_part, axis, up), lax.ppermute(first, axis, down)


def label_codes(arrival_slot, labels):
    bricks = BX * BY * SZ // BR
    filled = jnp.any(
        (arrival_slot >> 3)[None, :] == jnp.arange(bricks, dtype=jnp.int32)[:, None], axis=1
    ).reshape(BX, 1, BY, 1, SZ // BR, 1)
    cells = labels.reshape(BX, BR, BY, BR, SZ // BR, BR)
    codes = jnp.where(filled, cells + 1, 0).reshape(SX, SY, SZ).astype(BF)
    return jnp.pad(codes, ((0, 0), (2, CODE - 2 - SY), (0, CH - SZ)))


def arrange(taps):
    side = taps[:, :, ::2].transpose(0, 1, 3, 2, 4).reshape(9 * CH, 2 * CH)
    middle = taps[:, :, 1]
    rest = ((0, 0),) * 3
    middle = jnp.stack(
        [jnp.pad(middle, ((0, 1),) + rest), jnp.pad(middle, ((1, 0),) + rest)], axis=3
    )
    return side, middle.reshape(12 * CH, 2 * CH)


def per_device(fine_feats, owner_of, arrival_slot, w_stride, w_conv, w_head, labels):
    devs = lax.axis_size("gx") * lax.axis_size("gy")
    per_dev, cells, in_width = fine_feats.shape
    cap = arrival_slot.shape[0] // devs
    feats = fine_feats.reshape(per_dev * cells, in_width)
    buffer, place = send(feats, owner_of, w_stride, devs, cap)

    brick, octant = arrival_slot >> 3, arrival_slot & 7
    deep = SZ // BR
    big_x = 2 * (brick // (BY * deep)) + (octant >> 2)
    big_y = 2 * (brick // deep % BY) + ((octant >> 1) & 1)
    big_z = 2 * (brick % deep) + (octant & 1)
    index = jnp.where(arrival_slot >= 0, (big_x * (SY // 2) + big_y) * (SZ // 2) + big_z, BRICKS)
    code = label_codes(arrival_slot, labels)
    order = brick_order()
    place, w_conv = lax.optimization_barrier((place, w_conv))
    taps = w_conv.reshape(3, 3, 3, CH, CH)
    w_fwd = arrange(taps)
    w_bwd = arrange(taps[::-1, ::-1].swapaxes(3, 4))
    head = jnp.pad(jnp.concatenate([w_head, w_head], axis=1), ((0, 0), (0, CH - 16)))

    arrived, w_fwd, w_bwd = lax.optimization_barrier((to_all(buffer), w_fwd, w_bwd))
    slab, first, last_part = land(arrived, index, order, code)
    before, after = both_ways(first, last_part, "gx")
    weights_fwd = w_fwd + (head, head.T)
    inside = inner(slab, weights_fwd)
    up, down = sides(slab, before, after, inside)
    left, right = both_ways(down, up, "gy")
    at_x = x_sides(slab, before, after, weights_fwd)
    returned, kept = core(
        jnp.minimum(index, BRICKS - 1),
        slab,
        before,
        after,
        left,
        right,
        inside,
        at_x,
        weights_fwd,
        w_bwd,
        order.T,
    )
    came = to_all(returned)
    half = (lax.axis_index("gy") % 2).astype(jnp.int32).reshape(1)
    terms = sum_over_gy(*weights(half, kept), devs)
    mine, stride = last(came, place, feats)
    terms, stride = lax.optimization_barrier((terms, stride))
    share = rows = 4
    terms = to_all(put_together(stride, terms).reshape(devs, rows + share, CH))
    grad_fine = lax.dot_general(
        mine, w_stride, (((1,), (1,)), ((), ())), preferred_element_type=F32
    ).astype(BF)
    terms = terms.astype(F32).reshape(lax.axis_size("gx"), -1, 2, rows + share, CH)
    by_part = jnp.sum(terms, axis=0)
    conv_sum = by_part[:, :, :rows].transpose(1, 0, 2, 3).reshape(2, -1, CH)
    stride_sum = jnp.sum(by_part[:, :, rows:], axis=(0, 1))
    block = jnp.concatenate(
        [conv_sum, jnp.broadcast_to(stride_sum, (2,) + stride_sum.shape)], axis=1
    ).astype(BF)
    block, grad_fine = lax.optimization_barrier((block, grad_fine))
    sums = to_all(jnp.broadcast_to(block, (devs // 2,) + block.shape).reshape(devs, -1, CH))
    scale = 1.0 / math.sqrt(per_dev * devs * cells)
    mine = sums[:, :-share].reshape(-1, CH)
    swap = [(i, i ^ 1) for i in range(lax.axis_size("gy"))]
    other = lax.ppermute(mine, "gy", swap)
    first_core = half[0] == 0
    grad_conv = jnp.concatenate(
        [
            jnp.where(first_core, mine, other),
            jnp.where(first_core, other, mine)[: 27 * CH - mine.shape[0]],
        ],
        axis=0,
    ).astype(F32).reshape(27, CH, CH) * scale
    grad_stride = sums[:, -share:].reshape(in_width, CH).astype(F32) * scale
    return (
        grad_fine.reshape(per_dev, cells, in_width),
        grad_stride,
        grad_conv,
    )


def solution(mesh):
    return jax.shard_map(
        per_device,
        mesh=mesh,
        in_specs=(
            P(("gx", "gy"), None, None),
            P(("gx", "gy")),
            P(("gx", "gy")),
            P(),
            P(),
            P(),
            P("gx", "gy", None),
        ),
        out_specs=(P(("gx", "gy"), None, None), P(), P()),
        check_vma=False,
    )
```

```python
import functools
import math

import jax
import jax.numpy as jnp
from jax import lax
from jax.experimental import pallas as pl
from jax.experimental.pallas import tpu as pltpu
from jax.sharding import PartitionSpec as P

BX = 2
BY = 2
BR = 4
SX = 8
SY = 8
SZ = 48
CH = 128
CELLS = 8
FX = SX + 4
FY = SY + 4
ROWS = SY * SZ
CODE = 16
SIDE = 2 * SZ
BRICKS = 384
KEPT = 84
PARTS = 4
VMEM = pltpu.CompilerParams(vmem_limit_bytes=24 * 1024 * 1024)
MOST_VMEM = pltpu.CompilerParams(vmem_limit_bytes=48 * 1024 * 1024)
ALL_VMEM = pltpu.CompilerParams(vmem_limit_bytes=63 * 1024 * 1024)
BF = jnp.bfloat16
F32 = jnp.float32


def whole(shape):
    return pl.BlockSpec(shape, lambda: (0,) * len(shape))


def anywhere():
    return pl.BlockSpec(memory_space=pl.ANY)


def smem():
    return pl.BlockSpec(memory_space=pltpu.SMEM)


def matmul(a, b):
    return jnp.dot(a, b, preferred_element_type=F32)


def iota(shape, dim):
    return lax.broadcasted_iota(jnp.int32, shape, dim)


def send_kernel(
    cap, owner_hbm, feats_hbm, w_hbm, buf_hbm, place, owner, feats, w_stride, rows, buf, count, sems
):
    per_dev = owner.shape[0]
    devs = count.shape[0]
    part = feats.shape[0] // PARTS
    copies = [
        pltpu.make_async_copy(owner_hbm, owner, sems.at[0]),
        pltpu.make_async_copy(w_hbm, w_stride, sems.at[1]),
    ] + [
        pltpu.make_async_copy(
            feats_hbm.at[pl.ds(i * part, part)], feats.at[pl.ds(i * part, part)], sems.at[2 + i]
        )
        for i in range(PARTS)
    ]
    for copy in copies:
        copy.start()

    def clear(i, c):
        count[i] = 0
        return c

    lax.fori_loop(0, devs, clear, 0, unroll=8)
    buf[...] = jnp.zeros_like(buf)
    copies[0].wait()

    def find(i):
        who = owner[i]
        pos = count[who]
        count[who] = pos + 1
        place[i] = who * cap + pos

    def put(i):
        buf[place[i]] = rows[i]

    copies[1].wait()
    bricks = per_dev // PARTS
    for i in range(PARTS + 1):
        if i < PARTS:
            copies[2 + i].wait()
            vals = matmul(feats[i * part : (i + 1) * part, :], w_stride[...])
            rows[i * bricks : (i + 1) * bricks] = vals.reshape(bricks, CELLS, CH).astype(BF)
            for j in range(i * bricks, (i + 1) * bricks):
                find(j)
        if i > 0:
            for j in range((i - 1) * bricks, i * bricks):
                put(j)
    out = pltpu.make_async_copy(buf, buf_hbm, sems.at[0])
    out.start()
    out.wait()


def hbm():
    return pl.BlockSpec(memory_space=pltpu.HBM)


def send(feats, owner, w_stride, devs, cap):
    per_dev = owner.shape[0]
    return pl.pallas_call(
        functools.partial(send_kernel, cap),
        out_shape=(
            jax.ShapeDtypeStruct((devs * cap, CELLS, CH), BF),
            jax.ShapeDtypeStruct((per_dev,), jnp.int32),
        ),
        in_specs=[hbm(), hbm(), hbm()],
        out_specs=(hbm(), smem()),
        scratch_shapes=[
            pltpu.SMEM((per_dev,), jnp.int32),
            pltpu.VMEM(feats.shape, BF),
            pltpu.VMEM(w_stride.shape, BF),
            pltpu.VMEM((per_dev, CELLS, CH), BF),
            pltpu.VMEM((devs * cap, CELLS, CH), BF),
            pltpu.SMEM((devs,), jnp.int32),
            pltpu.SemaphoreType.DMA((2 + PARTS,)),
        ],
        compiler_params=ALL_VMEM,
        name="send_bricks",
    )(owner, feats, w_stride)


def brick_order():
    row = iota((4 * SZ, 4 * SZ), 0)
    col = iota((4 * SZ, 4 * SZ), 1)
    z = row % SZ
    return (col == (z // 2) * 8 + (row // SZ) * 2 + z % 2).astype(BF)


def land_kernel(index, arrived, order, code, slab, first, last, held):
    held[...] = jnp.zeros_like(held)

    for j in range(index.shape[0]):
        held[index[j]] = arrived[j]
    for big_x in range(SX // 2):
        for big_y in range(SY // 2):
            start = (big_x * (SY // 2) + big_y) * (SZ // 2)
            block = held[start : start + SZ // 2].astype(F32).reshape(4 * SZ, CH).astype(BF)
            moved = matmul(order[...], block).astype(BF)
            for i in range(2):
                for l in range(2):
                    piece = moved[(2 * i + l) * SZ : (2 * i + l + 1) * SZ]
                    row = (2 * big_y + l) * SZ
                    slab[2 * big_x + i, row : row + SZ, :] = piece
    slab[:, ROWS:, :] = code[...]
    first[...] = slab[:2]
    last[...] = slab[SX - 2 :]


def land(arrived, index, order, code):
    shapes = ((SX, ROWS + CODE, CH), (2, ROWS + CODE, CH), (2, ROWS + CODE, CH))
    return pl.pallas_call(
        land_kernel,
        out_shape=tuple(jax.ShapeDtypeStruct(s, BF) for s in shapes),
        in_specs=[smem(), whole(arrived.shape), whole(order.shape), whole(code.shape)],
        out_specs=tuple(whole(s) for s in shapes),
        scratch_shapes=[pltpu.VMEM((BRICKS + 8, CELLS, CH), BF)],
        compiler_params=ALL_VMEM,
        name="land_bricks",
    )(index, arrived, order, code)


def sides_kernel(slab, before, after, inside, up, down):
    row = iota((CODE // 2, CH), 0)
    none = jnp.zeros((CODE // 2, CH), F32)
    for x in range(FX):
        if x < 2:
            ref, at = before, x
        elif x < 2 + SX:
            ref, at = slab, x - 2
        else:
            ref, at = after, x - 2 - SX
        up[x, :SIDE, :] = ref[at, ROWS - SIDE : ROWS, :]
        down[x, :SIDE, :] = ref[at, :SIDE, :]
        codes = ref[at, ROWS:, :].astype(F32)
        upper = jnp.where(row < 2, codes[8:], 0.0)
        lower = jnp.where((row == 2) | (row == 3), codes[:8], 0.0)
        up[x, SIDE:, :] = jnp.concatenate([upper, none], axis=0).astype(BF)
        down[x, SIDE:, :] = jnp.concatenate([none, lower], axis=0).astype(BF)


def sides(slab, before, after, inside):
    shape = (FX, SIDE + CODE, CH)
    return pl.pallas_call(
        sides_kernel,
        out_shape=(jax.ShapeDtypeStruct(shape, BF),) * 2,
        in_specs=[whole(slab.shape), whole(before.shape), whole(after.shape), anywhere()],
        out_specs=(whole(shape),) * 2,
        compiler_params=VMEM,
        name="y_sides",
    )(slab, before, after, inside)


def shifted(vals, z, by):
    rows = vals.shape[0]
    turned = pltpu.roll(vals, by % rows, 0)
    return jnp.where(z == (0 if by == 1 else SZ - 1), 0.0, turned)


def spread_codes(blocks):
    eye = (iota((SZ, CH), 0) == iota((SZ, CH), 1)).astype(F32)
    return jnp.concatenate([eye * block for block in blocks], axis=0).astype(BF)


def convolve(columns, w_side, w_mid):
    sides = [
        jnp.concatenate([columns[i + e][f] for e in range(3) for f in range(3)], axis=1)
        for i in range(2)
    ]
    outer = matmul(jnp.concatenate(sides, axis=0), w_side)
    middle = matmul(jnp.concatenate([part for four in columns for part in four], axis=1), w_mid)
    middle = jnp.concatenate([middle[:, :CH], middle[:, CH:]], axis=0)
    return outer[:, :CH], middle, outer[:, CH:]


def front(columns, spread, w_side, w_mid, head, head_t):
    rows = spread.shape[0]
    lane = iota((rows, CH), 1)
    z = iota((rows // SZ, SZ, CH), 1).reshape(rows, CH)
    below, middle, above = convolve(columns, w_side, w_mid)
    pre = shifted(below, z, 1) + middle + shifted(above, z, -1)
    code = matmul(spread, jnp.ones((CH, CH), BF))
    mask = code > 0.5
    pre = jnp.where(mask, pre, 0.0)
    gate = jax.nn.sigmoid(pre)
    logits = matmul((pre * gate).astype(BF), head)
    target = (code - 1.0 == (lane % 8).astype(F32)).astype(F32)
    grad_logits = jnp.where(mask, jax.nn.sigmoid(logits) - target, 0.0)
    high = grad_logits.astype(BF).astype(F32)
    terms = jnp.where(lane < 8, high, jnp.where(lane < 16, grad_logits - high, 0.0))
    grad_act = matmul(terms.astype(BF), head_t)
    return (grad_act * gate * (1.0 + pre * (1.0 - gate))).astype(BF)


INNER = (SY - 2) * SZ


def front_cost(slabs):
    flops = 2 * 9 * 3 * CH * CH * INNER * slabs
    return pl.CostEstimate(flops=flops, bytes_accessed=4 * 2**20, transcendentals=0)


def inner_kernel(slab, w_side, w_mid, head, head_t, grad):
    def step(pair, carry):
        x = 2 * pair
        columns = [[slab[x + i, f * SZ : f * SZ + INNER, :] for f in range(3)] for i in range(4)]
        blocks = []
        for i in range(2):
            codes = slab[x + i + 1, ROWS:, :].astype(F32)
            blocks += [codes[y : y + 1] for y in range(3, SY + 1)]
        vals = front(
            columns, spread_codes(blocks), w_side[...], w_mid[...], head[...], head_t[...]
        )
        for i in range(2):
            grad[x + i] = vals[i * INNER : (i + 1) * INNER]
        return carry

    lax.fori_loop(0, SX // 2 - 1, step, 0, unroll=SX // 2 - 1)


def inner(slab, weights):
    arrays = (slab,) + weights
    shape = (SX - 2, INNER, CH)
    return pl.pallas_call(
        inner_kernel,
        out_shape=jax.ShapeDtypeStruct(shape, BF),
        in_specs=[whole(a.shape) for a in arrays],
        out_specs=whole(shape),
        compiler_params=VMEM,
        cost_estimate=front_cost(SX - 2),
        name="grad_pre_inside",
    )(*arrays)


def x_sides_kernel(slab, before, after, w_side, w_mid, head, head_t, grad):
    def source(x):
        if x < 2:
            return before, x
        return (slab, x - 2) if x < SX + 2 else (after, x - SX - 2)

    for pair, x in enumerate((0, SX)):
        slabs = [source(x + i) for i in range(4)]
        columns = [
            [ref[at, f * SZ : f * SZ + INNER, :] for f in range(3)] for ref, at in slabs
        ]
        blocks = []
        for ref, at in slabs[1:3]:
            codes = ref[at, ROWS:, :].astype(F32)
            blocks += [codes[y : y + 1] for y in range(3, SY + 1)]
        vals = front(
            columns, spread_codes(blocks), w_side[...], w_mid[...], head[...], head_t[...]
        )
        for i in range(2):
            grad[2 * pair + i] = vals[i * INNER : (i + 1) * INNER]


def x_sides(slab, before, after, weights):
    arrays = (slab, before, after) + weights
    shape = (4, INNER, CH)
    return pl.pallas_call(
        x_sides_kernel,
        out_shape=jax.ShapeDtypeStruct(shape, BF),
        in_specs=[whole(a.shape) for a in arrays],
        out_specs=whole(shape),
        compiler_params=VMEM,
        cost_estimate=front_cost(4),
        name="grad_pre_x_sides",
    )(*arrays)


def core_kernel(
    index, slab, before, after, left, right, inside, at_x,
    w_side, w_mid, head, head_t, w_side_t, w_mid_t, order_t,
    back_hbm, kept_hbm, low, high, codes, grad, coarse, held, back, sems,
):
    middle = pl.ds(SIDE, ROWS)
    pairs = (
        (slab.at[:, pl.ds(0, ROWS)], kept_hbm.at[pl.ds(2, SX), middle]),
        (before.at[:, pl.ds(0, ROWS)], kept_hbm.at[pl.ds(0, 2), middle]),
        (after.at[:, pl.ds(0, ROWS)], kept_hbm.at[pl.ds(2 + SX, 2), middle]),
        (left.at[:, pl.ds(0, SIDE)], kept_hbm.at[pl.ds(0, FX), pl.ds(0, SIDE)]),
        (right.at[:, pl.ds(0, SIDE)], kept_hbm.at[pl.ds(0, FX), pl.ds(SIDE + ROWS, SIDE)]),
    )
    copies = [pltpu.make_async_copy(a, b, sems.at[i]) for i, (a, b) in enumerate(pairs)]
    for copy in copies:
        copy.start()
    for at, ref in ((0, before), (2, slab), (2 + SX, after)):
        many = ref.shape[0]
        low[at : at + many, SIDE:, :] = ref[:, :SIDE, :]
        high[at : at + many, :SIDE, :] = ref[:, ROWS - SIDE : ROWS, :]
        codes[at : at + many] = ref[:, ROWS:, :].astype(F32)
    low[:, :SIDE, :] = left[:, :SIDE, :]
    high[:, SIDE:, :] = right[:, :SIDE, :]
    codes[...] += left[:, SIDE:, :].astype(F32) + right[:, SIDE:, :].astype(F32)
    grad[:2, SIDE : SIDE + INNER, :] = at_x[:2]
    grad[2:SX, SIDE : SIDE + INNER, :] = inside[...]
    grad[SX:, SIDE : SIDE + INNER, :] = at_x[2:]

    z_own = iota((2 * SY, SZ, CH), 1).reshape(2 * ROWS, CH)

    def forward(pair, carry):
        x = 2 * pair
        columns = [
            [
                jnp.concatenate(
                    [ref[x + i, f * SZ : f * SZ + SIDE, :] for ref in (low, high)], axis=0
                )
                for f in range(3)
            ]
            for i in range(4)
        ]
        blocks = []
        for i in range(2):
            here = codes[x + i + 1]
            blocks += [here[y : y + 1] for y in (1, 2, SY + 1, SY + 2)]
        vals = front(
            columns, spread_codes(blocks), w_side[...], w_mid[...], head[...], head_t[...]
        )
        for i in range(2):
            grad[x + i, :SIDE, :] = vals[2 * i * SIDE : (2 * i + 1) * SIDE]
            grad[x + i, SIDE + INNER :, :] = vals[(2 * i + 1) * SIDE : (2 * i + 2) * SIDE]
        return carry

    lax.fori_loop(0, SX // 2 + 1, forward, 0, unroll=5)
    out = pltpu.make_async_copy(
        grad.at[pl.ds(1, SX), pl.ds(SZ, ROWS)],
        kept_hbm.at[pl.ds(FX, SX), pl.ds(0, ROWS)],
        sems.at[len(pairs)],
    )
    out.start()
    copies.append(out)

    def backward(pair, carry):
        x = 2 * pair
        columns = [[grad[x + i, f * SZ : f * SZ + ROWS, :] for f in range(3)] for i in range(4)]
        below, middle, above = convolve(columns, w_side_t[...], w_mid_t[...])
        vals = (shifted(below, z_own, -1) + middle + shifted(above, z_own, 1)).astype(BF)
        for i in range(2):
            coarse[x + i] = vals[i * ROWS : (i + 1) * ROWS]
        return carry

    lax.fori_loop(0, SX // 2, backward, 0, unroll=4)

    for big_x in range(SX // 2):
        for big_y in range(SY // 2):
            block = jnp.concatenate(
                [
                    coarse[2 * big_x + i, (2 * big_y + l) * SZ : (2 * big_y + l + 1) * SZ, :]
                    for i in range(2)
                    for l in range(2)
                ],
                axis=0,
            )
            start = (big_x * (SY // 2) + big_y) * (SZ // 2)
            moved = matmul(order_t[...], block).reshape(SZ // 2, CELLS, CH)
            held[start : start + SZ // 2] = moved.astype(BF)

    part = index.shape[0] // PARTS
    for i in range(PARTS):
        for j in range(i * part, (i + 1) * part):
            back[j] = held[index[j]]
        rows = pl.ds(i * part, part)
        copy = pltpu.make_async_copy(back.at[rows], back_hbm.at[rows], sems.at[6 + i])
        copy.start()
        copies.append(copy)
    for copy in copies:
        copy.wait()


def core(
    index, slab, before, after, left, right, inside, at_x, weights, weights_t, order_t
):
    arrays = (slab, before, after, left, right, inside, at_x) + weights + weights_t + (order_t,)
    shapes = ((index.shape[0], CELLS, CH), (KEPT, FY * SZ, CH))
    return pl.pallas_call(
        core_kernel,
        out_shape=tuple(jax.ShapeDtypeStruct(s, BF) for s in shapes),
        in_specs=[smem()] + [whole(a.shape) for a in arrays],
        out_specs=(hbm(),) * 2,
        scratch_shapes=[
            pltpu.VMEM((FX, 2 * SIDE, CH), BF),
            pltpu.VMEM((FX, 2 * SIDE, CH), BF),
            pltpu.VMEM((FX, CODE, CH), F32),
            pltpu.VMEM((SX + 2, ROWS + SIDE, CH), BF),
            pltpu.VMEM((SX, ROWS, CH), BF),
            pltpu.VMEM((BRICKS, CELLS, CH), BF),
            pltpu.VMEM((index.shape[0], CELLS, CH), BF),
            pltpu.SemaphoreType.DMA((6 + PARTS,)),
        ],
        compiler_params=MOST_VMEM,
        name="conv_both_ways",
    )(index, *arrays)


def weights_kernel(half, kept_hbm, keep, give, kept, total, taps_out, sem):
    copy = pltpu.make_async_copy(kept_hbm.at[pl.ds(0, FX + SX)], kept, sem)
    copy.start()
    copy.wait()
    z_own = iota((SY, SZ, CH), 1).reshape(ROWS, CH)
    total[...] = jnp.zeros_like(total)

    def add(x, carry):
        here = kept[FX + x, :ROWS, :]
        mid = here.astype(F32)
        grads = jnp.concatenate(
            [shifted(mid, z_own, -1).astype(BF), here, shifted(mid, z_own, 1).astype(BF)],
            axis=1,
        )
        for e in range(3):
            taps = jnp.concatenate(
                [kept[x + 1 + e, (1 + f) * SZ : (1 + f) * SZ + ROWS, :] for f in range(3)], axis=1
            )
            total[e] += lax.dot_general(
                taps, grads, (((0,), (0,)), ((), ())), preferred_element_type=F32
            )
        return carry

    lax.fori_loop(0, SX, add, 0, unroll=2)
    for tap in range(27):
        e, f, g = tap // 9, tap // 3 % 3, tap % 3
        taps_out[tap] = total[e, f * CH : (f + 1) * CH, g * CH : (g + 1) * CH]
    taps_out[27:] = jnp.zeros((5, CH, CH), F32)
    mine = half[0]
    keep[...] = taps_out[pl.ds(16 * mine, 16)]
    give[...] = taps_out[pl.ds(16 * (1 - mine), 16)].astype(BF)


def weights(half, kept):
    shape = (16, CH, CH)
    return pl.pallas_call(
        weights_kernel,
        out_shape=(jax.ShapeDtypeStruct(shape, F32), jax.ShapeDtypeStruct(shape, BF)),
        in_specs=[smem(), hbm()],
        out_specs=(whole(shape),) * 2,
        scratch_shapes=[
            pltpu.VMEM((FX + SX, FY * SZ, CH), BF),
            pltpu.VMEM((3, 3 * CH, 3 * CH), F32),
            pltpu.VMEM((32, CH, CH), F32),
            pltpu.SemaphoreType.DMA,
        ],
        compiler_params=ALL_VMEM,
        cost_estimate=pl.CostEstimate(
            flops=2 * 27 * CH * CH * SX * ROWS, bytes_accessed=6 * 2**20, transcendentals=0
        ),
        name="conv_weight_grad",
    )(half, kept)


def pair_kernel(me, keep, got, *outs):
    both = keep[...] + got[...].astype(F32).reshape(keep.shape)
    for by, out in enumerate(outs):
        y = lax.rem(me[0] + by, len(outs))
        part = jnp.where(y < 2, both[:, :, 0], both[:, :, 1])
        low = jnp.concatenate([part[:, 0, :4], part[:, 1, :4]], axis=1)
        high = jnp.concatenate([part[:, 0, 4:], part[:, 1, 4:]], axis=1)
        out[...] = jnp.where(y % 2 == 0, low, high).astype(out.dtype)


def add_pair(y, keep, got, ring, devs):
    shape = (devs // 2, 8, CH)
    kinds = (F32,) + (BF,) * (ring - 1)
    keep = keep.reshape(devs // 2, 2, 2, 8, CH)
    got = got.reshape(devs, 16, CH)
    return pl.pallas_call(
        pair_kernel,
        out_shape=tuple(jax.ShapeDtypeStruct(shape, kind) for kind in kinds),
        in_specs=[smem(), whole(keep.shape), whole(got.shape)],
        out_specs=(whole(shape),) * ring,
        compiler_params=ALL_VMEM,
        name="add_pair",
    )(y, keep, got)


def sum_over_gy(keep, give, devs):
    me = lax.axis_index("gy")
    y = me // 2
    peers = lax.axis_size("gy")
    ring = peers // 2
    got = lax.ppermute(give, "gy", [(i, i ^ 1) for i in range(peers)])
    parts = add_pair(y.astype(jnp.int32).reshape(1), keep, got, ring, devs)
    perms = [[(i, (i + 2 * by) % peers) for i in range(peers)] for by in range(ring)]
    return parts[:1] + tuple(
        lax.ppermute(part, "gy", perm) for part, perm in zip(parts[1:], perms[1:])
    )


def last_kernel(place, came, feats, mine, stride, rows):
    per_dev = place.shape[0]

    for i in range(per_dev):
        rows[i] = came[place[i]]
    vals = rows[...].astype(F32).reshape(per_dev * CELLS, CH).astype(BF)
    mine[...] = vals
    stride[...] = lax.dot_general(
        feats[...], vals, (((0,), (0,)), ((), ())), preferred_element_type=F32
    ).astype(BF)


def last(came, place, feats):
    shapes = ((feats.shape[0], CH), (feats.shape[1], CH))
    return pl.pallas_call(
        last_kernel,
        out_shape=tuple(jax.ShapeDtypeStruct(s, BF) for s in shapes),
        in_specs=[smem(), whole(came.shape), whole(feats.shape)],
        out_specs=tuple(whole(s) for s in shapes),
        scratch_shapes=[pltpu.VMEM((place.shape[0], CELLS, CH), BF)],
        compiler_params=VMEM,
        name="stride_term",
    )(place, came, feats)


def terms_kernel(stride, *refs):
    terms, out = refs[:-1], refs[-1]
    conv = sum(term[...].astype(F32) for term in terms)
    both = stride[...].astype(F32)
    out[:, 0] = jnp.concatenate([conv[:, :4], both[:, :4]], axis=1).astype(BF)
    out[:, 1] = jnp.concatenate([conv[:, 4:], both[:, 4:]], axis=1).astype(BF)


def put_together(stride, terms):
    shape = terms[0].shape
    arrays = (stride.reshape(shape),) + tuple(terms)
    return pl.pallas_call(
        terms_kernel,
        out_shape=jax.ShapeDtypeStruct((shape[0], 2) + shape[1:], BF),
        in_specs=[whole(shape) for a in arrays],
        out_specs=whole((shape[0], 2) + shape[1:]),
        compiler_params=VMEM,
        name="put_together",
    )(*arrays)


def to_all(buffer):
    return lax.all_to_all(buffer, ("gx", "gy"), split_axis=0, concat_axis=0, tiled=True)


def both_ways(first, last_part, axis):
    peers = lax.axis_size(axis)
    up = [(i, i + 1) for i in range(peers - 1)]
    down = [(i + 1, i) for i in range(peers - 1)]
    return lax.ppermute(last_part, axis, up), lax.ppermute(first, axis, down)


def label_codes(arrival_slot, labels):
    bricks = BX * BY * SZ // BR
    filled = jnp.any(
        (arrival_slot >> 3)[None, :] == jnp.arange(bricks, dtype=jnp.int32)[:, None], axis=1
    ).reshape(BX, 1, BY, 1, SZ // BR, 1)
    cells = labels.reshape(BX, BR, BY, BR, SZ // BR, BR)
    codes = jnp.where(filled, cells + 1, 0).reshape(SX, SY, SZ).astype(BF)
    return jnp.pad(codes, ((0, 0), (2, CODE - 2 - SY), (0, CH - SZ)))


def arrange(taps):
    side = taps[:, :, ::2].transpose(0, 1, 3, 2, 4).reshape(9 * CH, 2 * CH)
    middle = taps[:, :, 1]
    rest = ((0, 0),) * 3
    middle = jnp.stack(
        [jnp.pad(middle, ((0, 1),) + rest), jnp.pad(middle, ((1, 0),) + rest)], axis=3
    )
    return side, middle.reshape(12 * CH, 2 * CH)


def per_device(fine_feats, owner_of, arrival_slot, w_stride, w_conv, w_head, labels):
    devs = lax.axis_size("gx") * lax.axis_size("gy")
    per_dev, cells, in_width = fine_feats.shape
    cap = arrival_slot.shape[0] // devs
    feats = fine_feats.reshape(per_dev * cells, in_width)
    buffer, place = send(feats, owner_of, w_stride, devs, cap)

    brick, octant = arrival_slot >> 3, arrival_slot & 7
    deep = SZ // BR
    big_x = 2 * (brick // (BY * deep)) + (octant >> 2)
    big_y = 2 * (brick // deep % BY) + ((octant >> 1) & 1)
    big_z = 2 * (brick % deep) + (octant & 1)
    index = jnp.where(arrival_slot >= 0, (big_x * (SY // 2) + big_y) * (SZ // 2) + big_z, BRICKS)
    code = label_codes(arrival_slot, labels)
    order = brick_order()
    place, w_conv = lax.optimization_barrier((place, w_conv))
    taps = w_conv.reshape(3, 3, 3, CH, CH)
    w_fwd = arrange(taps)
    w_bwd = arrange(taps[::-1, ::-1].swapaxes(3, 4))
    head = jnp.pad(jnp.concatenate([w_head, w_head], axis=1), ((0, 0), (0, CH - 16)))

    arrived, w_fwd, w_bwd = lax.optimization_barrier((to_all(buffer), w_fwd, w_bwd))
    slab, first, last_part = land(arrived, index, order, code)
    before, after = both_ways(first, last_part, "gx")
    weights_fwd = w_fwd + (head, head.T)
    inside = inner(slab, weights_fwd)
    up, down = sides(slab, before, after, inside)
    left, right = both_ways(down, up, "gy")
    at_x = x_sides(slab, before, after, weights_fwd)
    returned, kept = core(
        jnp.minimum(index, BRICKS - 1),
        slab,
        before,
        after,
        left,
        right,
        inside,
        at_x,
        weights_fwd,
        w_bwd,
        order.T,
    )
    came = to_all(returned)
    half = (lax.axis_index("gy") % 2).astype(jnp.int32).reshape(1)
    terms = sum_over_gy(*weights(half, kept), devs)
    mine, stride = last(came, place, feats)
    terms, stride = lax.optimization_barrier((terms, stride))
    share = rows = 4
    terms = to_all(put_together(stride, terms).reshape(devs, rows + share, CH))
    grad_fine = lax.dot_general(
        mine, w_stride, (((1,), (1,)), ((), ())), preferred_element_type=F32
    ).astype(BF)
    terms = terms.astype(F32).reshape(lax.axis_size("gx"), -1, 2, rows + share, CH)
    by_part = jnp.sum(terms, axis=0)
    conv_sum = by_part[:, :, :rows].transpose(1, 0, 2, 3).reshape(2, -1, CH)
    stride_sum = jnp.sum(by_part[:, :, rows:], axis=(0, 1))
    block = jnp.concatenate(
        [conv_sum, jnp.broadcast_to(stride_sum, (2,) + stride_sum.shape)], axis=1
    ).astype(BF)
    block, grad_fine = lax.optimization_barrier((block, grad_fine))
    sums = to_all(jnp.broadcast_to(block, (devs // 2,) + block.shape).reshape(devs, -1, CH))
    scale = 1.0 / math.sqrt(per_dev * devs * cells)
    mine = sums[:, :-share].reshape(-1, CH)
    swap = [(i, i ^ 1) for i in range(lax.axis_size("gy"))]
    other = lax.ppermute(mine, "gy", swap)
    first_core = half[0] == 0
    grad_conv = jnp.concatenate(
        [
            jnp.where(first_core, mine, other),
            jnp.where(first_core, other, mine)[: 27 * CH - mine.shape[0]],
        ],
        axis=0,
    ).astype(F32).reshape(27, CH, CH) * scale
    grad_stride = sums[:, -share:].reshape(in_width, CH).astype(F32) * scale
    return (
        grad_fine.reshape(per_dev, cells, in_width),
        grad_stride,
        grad_conv,
    )


def solution(mesh):
    return jax.shard_map(
        per_device,
        mesh=mesh,
        in_specs=(
            P(("gx", "gy"), None, None),
            P(("gx", "gy")),
            P(("gx", "gy")),
            P(),
            P(),
            P(),
            P("gx", "gy", None),
        ),
        out_specs=(P(("gx", "gy"), None, None), P(), P()),
        check_vma=False,
    )
```

```python
import functools
import math

import jax
import jax.numpy as jnp
from jax import lax
from jax.experimental import pallas as pl
from jax.experimental.pallas import tpu as pltpu
from jax.sharding import PartitionSpec as P

BX = 2
BY = 2
BR = 4
SX = 8
SY = 8
SZ = 48
CH = 128
CELLS = 8
FX = SX + 4
FY = SY + 4
ROWS = SY * SZ
CODE = 16
SIDE = 2 * SZ
BRICKS = 384
KEPT = 84
PARTS = 4
VMEM = pltpu.CompilerParams(vmem_limit_bytes=24 * 1024 * 1024)
MOST_VMEM = pltpu.CompilerParams(vmem_limit_bytes=48 * 1024 * 1024)
ALL_VMEM = pltpu.CompilerParams(vmem_limit_bytes=63 * 1024 * 1024)
BF = jnp.bfloat16
F32 = jnp.float32


def whole(shape):
    return pl.BlockSpec(shape, lambda: (0,) * len(shape))


def anywhere():
    return pl.BlockSpec(memory_space=pl.ANY)


def smem():
    return pl.BlockSpec(memory_space=pltpu.SMEM)


def matmul(a, b):
    return jnp.dot(a, b, preferred_element_type=F32)


def iota(shape, dim):
    return lax.broadcasted_iota(jnp.int32, shape, dim)


def send_kernel(
    cap, owner_hbm, feats_hbm, w_hbm, buf_hbm, place, owner, feats, w_stride, rows, buf, count, sems
):
    per_dev = owner.shape[0]
    devs = count.shape[0]
    part = feats.shape[0] // PARTS
    copies = [
        pltpu.make_async_copy(owner_hbm, owner, sems.at[0]),
        pltpu.make_async_copy(w_hbm, w_stride, sems.at[1]),
    ] + [
        pltpu.make_async_copy(
            feats_hbm.at[pl.ds(i * part, part)], feats.at[pl.ds(i * part, part)], sems.at[2 + i]
        )
        for i in range(PARTS)
    ]
    for copy in copies:
        copy.start()

    def clear(i, c):
        count[i] = 0
        return c

    lax.fori_loop(0, devs, clear, 0, unroll=8)
    buf[...] = jnp.zeros_like(buf)
    copies[0].wait()

    def find(i):
        who = owner[i]
        pos = count[who]
        count[who] = pos + 1
        place[i] = who * cap + pos

    def put(i):
        buf[place[i]] = rows[i]

    copies[1].wait()
    bricks = per_dev // PARTS
    for i in range(PARTS + 1):
        if i < PARTS:
            copies[2 + i].wait()
            vals = matmul(feats[i * part : (i + 1) * part, :], w_stride[...])
            rows[i * bricks : (i + 1) * bricks] = vals.reshape(bricks, CELLS, CH).astype(BF)
            for j in range(i * bricks, (i + 1) * bricks):
                find(j)
        if i > 0:
            for j in range((i - 1) * bricks, i * bricks):
                put(j)
    out = pltpu.make_async_copy(buf, buf_hbm, sems.at[0])
    out.start()
    out.wait()


def hbm():
    return pl.BlockSpec(memory_space=pltpu.HBM)


def send(feats, owner, w_stride, devs, cap):
    per_dev = owner.shape[0]
    return pl.pallas_call(
        functools.partial(send_kernel, cap),
        out_shape=(
            jax.ShapeDtypeStruct((devs * cap, CELLS, CH), BF),
            jax.ShapeDtypeStruct((per_dev,), jnp.int32),
        ),
        in_specs=[hbm(), hbm(), hbm()],
        out_specs=(hbm(), smem()),
        scratch_shapes=[
            pltpu.SMEM((per_dev,), jnp.int32),
            pltpu.VMEM(feats.shape, BF),
            pltpu.VMEM(w_stride.shape, BF),
            pltpu.VMEM((per_dev, CELLS, CH), BF),
            pltpu.VMEM((devs * cap, CELLS, CH), BF),
            pltpu.SMEM((devs,), jnp.int32),
            pltpu.SemaphoreType.DMA((2 + PARTS,)),
        ],
        compiler_params=ALL_VMEM,
        name="send_bricks",
    )(owner, feats, w_stride)


def brick_order():
    row = iota((4 * SZ, 4 * SZ), 0)
    col = iota((4 * SZ, 4 * SZ), 1)
    z = row % SZ
    return (col == (z // 2) * 8 + (row // SZ) * 2 + z % 2).astype(BF)


def land_kernel(index, arrived, order, code, slab, first, last, held):
    held[...] = jnp.zeros_like(held)

    for j in range(index.shape[0]):
        held[index[j]] = arrived[j]
    deep = SZ // 2
    for big_x in range(SX // 2):
        for half in range(SY // 4):
            start = (big_x * (SY // 2) + 2 * half) * deep
            block = jnp.concatenate(
                [
                    held[at : at + deep].astype(F32).reshape(4 * SZ, CH)
                    for at in (start, start + deep)
                ],
                axis=1,
            ).astype(BF)
            moved = matmul(order[...], block).astype(BF)
            for i in range(2):
                for l in range(2):
                    piece = moved[(2 * i + l) * SZ : (2 * i + l + 1) * SZ]
                    for j in range(2):
                        row = (4 * half + 2 * j + l) * SZ
                        slab[2 * big_x + i, row : row + SZ, :] = piece[:, j * CH : (j + 1) * CH]
    slab[:, ROWS:, :] = code[...]
    first[...] = slab[:2]
    last[...] = slab[SX - 2 :]


def land(arrived, index, order, code):
    shapes = ((SX, ROWS + CODE, CH), (2, ROWS + CODE, CH), (2, ROWS + CODE, CH))
    return pl.pallas_call(
        land_kernel,
        out_shape=tuple(jax.ShapeDtypeStruct(s, BF) for s in shapes),
        in_specs=[smem(), whole(arrived.shape), whole(order.shape), whole(code.shape)],
        out_specs=tuple(whole(s) for s in shapes),
        scratch_shapes=[pltpu.VMEM((BRICKS + 8, CELLS, CH), BF)],
        compiler_params=ALL_VMEM,
        name="land_bricks",
    )(index, arrived, order, code)


def sides_kernel(slab, before, after, inside, up, down):
    row = iota((CODE // 2, CH), 0)
    none = jnp.zeros((CODE // 2, CH), F32)
    for x in range(FX):
        if x < 2:
            ref, at = before, x
        elif x < 2 + SX:
            ref, at = slab, x - 2
        else:
            ref, at = after, x - 2 - SX
        up[x, :SIDE, :] = ref[at, ROWS - SIDE : ROWS, :]
        down[x, :SIDE, :] = ref[at, :SIDE, :]
        codes = ref[at, ROWS:, :].astype(F32)
        upper = jnp.where(row < 2, codes[8:], 0.0)
        lower = jnp.where((row == 2) | (row == 3), codes[:8], 0.0)
        up[x, SIDE:, :] = jnp.concatenate([upper, none], axis=0).astype(BF)
        down[x, SIDE:, :] = jnp.concatenate([none, lower], axis=0).astype(BF)


def sides(slab, before, after, inside):
    shape = (FX, SIDE + CODE, CH)
    return pl.pallas_call(
        sides_kernel,
        out_shape=(jax.ShapeDtypeStruct(shape, BF),) * 2,
        in_specs=[whole(slab.shape), whole(before.shape), whole(after.shape), anywhere()],
        out_specs=(whole(shape),) * 2,
        compiler_params=VMEM,
        name="y_sides",
    )(slab, before, after, inside)


def shifted(vals, z, by):
    rows = vals.shape[0]
    turned = pltpu.roll(vals, by % rows, 0)
    return jnp.where(z == (0 if by == 1 else SZ - 1), 0.0, turned)


def spread_codes(blocks):
    eye = (iota((SZ, CH), 0) == iota((SZ, CH), 1)).astype(F32)
    return jnp.concatenate([eye * block for block in blocks], axis=0)


def convolve(columns, w_side, w_mid):
    sides = [
        jnp.concatenate([columns[i + e][f] for e in range(3) for f in range(3)], axis=1)
        for i in range(2)
    ]
    outer = matmul(jnp.concatenate(sides, axis=0), w_side)
    middle = matmul(jnp.concatenate([part for four in columns for part in four], axis=1), w_mid)
    middle = jnp.concatenate([middle[:, :CH], middle[:, CH:]], axis=0)
    return outer[:, :CH], middle, outer[:, CH:]


def front(columns, spread, w_side, w_mid, head, head_t):
    rows = spread.shape[0]
    lane = iota((rows, CH), 1)
    z = iota((rows // SZ, SZ, CH), 1).reshape(rows, CH)
    below, middle, above = convolve(columns, w_side, w_mid)
    pre = shifted(below, z, 1) + middle + shifted(above, z, -1)
    code = jnp.sum(spread, axis=1, keepdims=True)
    mask = code > 0.5
    pre = jnp.where(mask, pre, 0.0)
    gate = jax.nn.sigmoid(pre)
    logits = matmul((pre * gate).astype(BF), head)
    target = (code - 1.0 == (lane % 8).astype(F32)).astype(F32)
    grad_logits = jnp.where(mask, jax.nn.sigmoid(logits) - target, 0.0)
    high = grad_logits.astype(BF).astype(F32)
    terms = jnp.where(lane < 8, high, jnp.where(lane < 16, grad_logits - high, 0.0))
    grad_act = matmul(terms.astype(BF), head_t)
    return (grad_act * gate * (1.0 + pre * (1.0 - gate))).astype(BF)


INNER = (SY - 2) * SZ


def front_cost(slabs):
    flops = 2 * 9 * 3 * CH * CH * INNER * slabs
    return pl.CostEstimate(flops=flops, bytes_accessed=4 * 2**20, transcendentals=0)


def inner_kernel(slab, w_side, w_mid, head, head_t, grad):
    def step(pair, carry):
        x = 2 * pair
        columns = [[slab[x + i, f * SZ : f * SZ + INNER, :] for f in range(3)] for i in range(4)]
        blocks = []
        for i in range(2):
            codes = slab[x + i + 1, ROWS:, :].astype(F32)
            blocks += [codes[y : y + 1] for y in range(3, SY + 1)]
        vals = front(
            columns, spread_codes(blocks), w_side[...], w_mid[...], head[...], head_t[...]
        )
        for i in range(2):
            grad[x + i] = vals[i * INNER : (i + 1) * INNER]
        return carry

    lax.fori_loop(0, SX // 2 - 1, step, 0, unroll=SX // 2 - 1)


def inner(slab, weights):
    arrays = (slab,) + weights
    shape = (SX - 2, INNER, CH)
    return pl.pallas_call(
        inner_kernel,
        out_shape=jax.ShapeDtypeStruct(shape, BF),
        in_specs=[whole(a.shape) for a in arrays],
        out_specs=whole(shape),
        compiler_params=VMEM,
        cost_estimate=front_cost(SX - 2),
        name="grad_pre_inside",
    )(*arrays)


def x_sides_kernel(slab, before, after, w_side, w_mid, head, head_t, grad):
    def source(x):
        if x < 2:
            return before, x
        return (slab, x - 2) if x < SX + 2 else (after, x - SX - 2)

    for pair, x in enumerate((0, SX)):
        slabs = [source(x + i) for i in range(4)]
        columns = [
            [ref[at, f * SZ : f * SZ + INNER, :] for f in range(3)] for ref, at in slabs
        ]
        blocks = []
        for ref, at in slabs[1:3]:
            codes = ref[at, ROWS:, :].astype(F32)
            blocks += [codes[y : y + 1] for y in range(3, SY + 1)]
        vals = front(
            columns, spread_codes(blocks), w_side[...], w_mid[...], head[...], head_t[...]
        )
        for i in range(2):
            grad[2 * pair + i] = vals[i * INNER : (i + 1) * INNER]


def x_sides(slab, before, after, weights):
    arrays = (slab, before, after) + weights
    shape = (4, INNER, CH)
    return pl.pallas_call(
        x_sides_kernel,
        out_shape=jax.ShapeDtypeStruct(shape, BF),
        in_specs=[whole(a.shape) for a in arrays],
        out_specs=whole(shape),
        compiler_params=VMEM,
        cost_estimate=front_cost(4),
        name="grad_pre_x_sides",
    )(*arrays)


def core_kernel(
    index, slab, before, after, left, right, inside, at_x,
    w_side, w_mid, head, head_t, w_side_t, w_mid_t, order_t,
    back_hbm, kept_hbm, low, high, codes, grad, coarse, held, back, sems,
):
    middle = pl.ds(SIDE, ROWS)
    pairs = (
        (slab.at[:, pl.ds(0, ROWS)], kept_hbm.at[pl.ds(2, SX), middle]),
        (before.at[:, pl.ds(0, ROWS)], kept_hbm.at[pl.ds(0, 2), middle]),
        (after.at[:, pl.ds(0, ROWS)], kept_hbm.at[pl.ds(2 + SX, 2), middle]),
        (left.at[:, pl.ds(0, SIDE)], kept_hbm.at[pl.ds(0, FX), pl.ds(0, SIDE)]),
        (right.at[:, pl.ds(0, SIDE)], kept_hbm.at[pl.ds(0, FX), pl.ds(SIDE + ROWS, SIDE)]),
    )
    copies = [pltpu.make_async_copy(a, b, sems.at[i]) for i, (a, b) in enumerate(pairs)]
    for copy in copies:
        copy.start()
    for at, ref in ((0, before), (2, slab), (2 + SX, after)):
        many = ref.shape[0]
        low[at : at + many, SIDE:, :] = ref[:, :SIDE, :]
        high[at : at + many, :SIDE, :] = ref[:, ROWS - SIDE : ROWS, :]
        codes[at : at + many] = ref[:, ROWS:, :].astype(F32)
    low[:, :SIDE, :] = left[:, :SIDE, :]
    high[:, SIDE:, :] = right[:, :SIDE, :]
    codes[...] += left[:, SIDE:, :].astype(F32) + right[:, SIDE:, :].astype(F32)
    grad[:2, SIDE : SIDE + INNER, :] = at_x[:2]
    grad[2:SX, SIDE : SIDE + INNER, :] = inside[...]
    grad[SX:, SIDE : SIDE + INNER, :] = at_x[2:]

    z_own = iota((2 * SY, SZ, CH), 1).reshape(2 * ROWS, CH)

    def forward(pair, carry):
        x = 2 * pair
        columns = [
            [
                jnp.concatenate(
                    [ref[x + i, f * SZ : f * SZ + SIDE, :] for ref in (low, high)], axis=0
                )
                for f in range(3)
            ]
            for i in range(4)
        ]
        blocks = []
        for i in range(2):
            here = codes[x + i + 1]
            blocks += [here[y : y + 1] for y in (1, 2, SY + 1, SY + 2)]
        vals = front(
            columns, spread_codes(blocks), w_side[...], w_mid[...], head[...], head_t[...]
        )
        for i in range(2):
            grad[x + i, :SIDE, :] = vals[2 * i * SIDE : (2 * i + 1) * SIDE]
            grad[x + i, SIDE + INNER :, :] = vals[(2 * i + 1) * SIDE : (2 * i + 2) * SIDE]
        return carry

    lax.fori_loop(0, SX // 2 + 1, forward, 0, unroll=5)
    out = pltpu.make_async_copy(
        grad.at[pl.ds(1, SX), pl.ds(SZ, ROWS)],
        kept_hbm.at[pl.ds(FX, SX), pl.ds(0, ROWS)],
        sems.at[len(pairs)],
    )
    out.start()
    copies.append(out)

    def backward(pair, carry):
        x = 2 * pair
        columns = [[grad[x + i, f * SZ : f * SZ + ROWS, :] for f in range(3)] for i in range(4)]
        below, middle, above = convolve(columns, w_side_t[...], w_mid_t[...])
        vals = (shifted(below, z_own, -1) + middle + shifted(above, z_own, 1)).astype(BF)
        for i in range(2):
            coarse[x + i] = vals[i * ROWS : (i + 1) * ROWS]
        return carry

    lax.fori_loop(0, SX // 2, backward, 0, unroll=4)

    deep = SZ // 2
    for big_x in range(SX // 2):
        for half in range(SY // 4):
            block = jnp.concatenate(
                [
                    jnp.concatenate(
                        [
                            coarse[2 * big_x + i, (2 * big_y + l) * SZ : (2 * big_y + l + 1) * SZ, :]
                            for i in range(2)
                            for l in range(2)
                        ],
                        axis=0,
                    )
                    for big_y in (2 * half, 2 * half + 1)
                ],
                axis=1,
            )
            moved = matmul(order_t[...], block)
            for j in range(2):
                start = (big_x * (SY // 2) + 2 * half + j) * deep
                one = moved[:, j * CH : (j + 1) * CH].reshape(deep, CELLS, CH)
                held[start : start + deep] = one.astype(BF)

    part = index.shape[0] // PARTS
    for i in range(PARTS):
        for j in range(i * part, (i + 1) * part):
            back[j] = held[index[j]]
        rows = pl.ds(i * part, part)
        copy = pltpu.make_async_copy(back.at[rows], back_hbm.at[rows], sems.at[6 + i])
        copy.start()
        copies.append(copy)
    for copy in copies:
        copy.wait()


def core(
    index, slab, before, after, left, right, inside, at_x, weights, weights_t, order_t
):
    arrays = (slab, before, after, left, right, inside, at_x) + weights + weights_t + (order_t,)
    shapes = ((index.shape[0], CELLS, CH), (KEPT, FY * SZ, CH))
    return pl.pallas_call(
        core_kernel,
        out_shape=tuple(jax.ShapeDtypeStruct(s, BF) for s in shapes),
        in_specs=[smem()] + [whole(a.shape) for a in arrays],
        out_specs=(hbm(),) * 2,
        scratch_shapes=[
            pltpu.VMEM((FX, 2 * SIDE, CH), BF),
            pltpu.VMEM((FX, 2 * SIDE, CH), BF),
            pltpu.VMEM((FX, CODE, CH), F32),
            pltpu.VMEM((SX + 2, ROWS + SIDE, CH), BF),
            pltpu.VMEM((SX, ROWS, CH), BF),
            pltpu.VMEM((BRICKS, CELLS, CH), BF),
            pltpu.VMEM((index.shape[0], CELLS, CH), BF),
            pltpu.SemaphoreType.DMA((6 + PARTS,)),
        ],
        compiler_params=MOST_VMEM,
        name="conv_both_ways",
    )(index, *arrays)


def weights_kernel(half, kept_hbm, keep, give, kept, total, taps_out, sems):
    half_x = SX // 2
    copies = []
    for i, (at, many) in enumerate(
        ((0, half_x + 3), (FX, half_x), (half_x + 3, FX - half_x - 3), (FX + half_x, half_x))
    ):
        slabs = pl.ds(at, many)
        copies.append(pltpu.make_async_copy(kept_hbm.at[slabs], kept.at[slabs], sems.at[i]))
        copies[-1].start()
    z_own = iota((SY, SZ, CH), 1).reshape(ROWS, CH)
    total[...] = jnp.zeros_like(total)

    def add(x, carry):
        here = kept[FX + x, :ROWS, :]
        mid = here.astype(F32)
        grads = jnp.concatenate(
            [shifted(mid, z_own, -1).astype(BF), here, shifted(mid, z_own, 1).astype(BF)],
            axis=1,
        )
        for e in range(3):
            taps = jnp.concatenate(
                [kept[x + 1 + e, (1 + f) * SZ : (1 + f) * SZ + ROWS, :] for f in range(3)], axis=1
            )
            total[e] += lax.dot_general(
                taps, grads, (((0,), (0,)), ((), ())), preferred_element_type=F32
            )
        return carry

    for part in range(2):
        copies[2 * part].wait()
        copies[2 * part + 1].wait()
        lax.fori_loop(half_x * part, half_x * (part + 1), add, 0, unroll=2)
    for tap in range(27):
        e, f, g = tap // 9, tap // 3 % 3, tap % 3
        taps_out[tap] = total[e, f * CH : (f + 1) * CH, g * CH : (g + 1) * CH]
    taps_out[27:] = jnp.zeros((5, CH, CH), F32)
    mine = half[0]
    keep[...] = taps_out[pl.ds(16 * mine, 16)]
    give[...] = taps_out[pl.ds(16 * (1 - mine), 16)].astype(BF)


def weights(half, kept):
    shape = (16, CH, CH)
    return pl.pallas_call(
        weights_kernel,
        out_shape=(jax.ShapeDtypeStruct(shape, F32), jax.ShapeDtypeStruct(shape, BF)),
        in_specs=[smem(), hbm()],
        out_specs=(whole(shape),) * 2,
        scratch_shapes=[
            pltpu.VMEM((FX + SX, FY * SZ, CH), BF),
            pltpu.VMEM((3, 3 * CH, 3 * CH), F32),
            pltpu.VMEM((32, CH, CH), F32),
            pltpu.SemaphoreType.DMA((4,)),
        ],
        compiler_params=ALL_VMEM,
        cost_estimate=pl.CostEstimate(
            flops=2 * 27 * CH * CH * SX * ROWS, bytes_accessed=6 * 2**20, transcendentals=0
        ),
        name="conv_weight_grad",
    )(half, kept)


def pair_kernel(me, keep, got, *outs):
    both = keep[...] + got[...].astype(F32).reshape(keep.shape)
    for by, out in enumerate(outs):
        y = lax.rem(me[0] + by, len(outs))
        part = jnp.where(y < 2, both[:, :, 0], both[:, :, 1])
        low = jnp.concatenate([part[:, 0, :4], part[:, 1, :4]], axis=1)
        high = jnp.concatenate([part[:, 0, 4:], part[:, 1, 4:]], axis=1)
        out[...] = jnp.where(y % 2 == 0, low, high).astype(out.dtype)


def add_pair(y, keep, got, ring, devs):
    shape = (devs // 2, 8, CH)
    kinds = (F32,) + (BF,) * (ring - 1)
    keep = keep.reshape(devs // 2, 2, 2, 8, CH)
    got = got.reshape(devs, 16, CH)
    return pl.pallas_call(
        pair_kernel,
        out_shape=tuple(jax.ShapeDtypeStruct(shape, kind) for kind in kinds),
        in_specs=[smem(), whole(keep.shape), whole(got.shape)],
        out_specs=(whole(shape),) * ring,
        compiler_params=ALL_VMEM,
        name="add_pair",
    )(y, keep, got)


def sum_over_gy(keep, give, devs):
    me = lax.axis_index("gy")
    y = me // 2
    peers = lax.axis_size("gy")
    ring = peers // 2
    got = lax.ppermute(give, "gy", [(i, i ^ 1) for i in range(peers)])
    parts = add_pair(y.astype(jnp.int32).reshape(1), keep, got, ring, devs)
    perms = [[(i, (i + 2 * by) % peers) for i in range(peers)] for by in range(ring)]
    return parts[:1] + tuple(
        lax.ppermute(part, "gy", perm) for part, perm in zip(parts[1:], perms[1:])
    )


def last_kernel(place, came, feats, mine, stride, rows):
    per_dev = place.shape[0]

    for i in range(per_dev):
        rows[i] = came[place[i]]
    vals = rows[...].astype(F32).reshape(per_dev * CELLS, CH).astype(BF)
    mine[...] = vals
    stride[...] = lax.dot_general(
        feats[...], vals, (((0,), (0,)), ((), ())), preferred_element_type=F32
    ).astype(BF)


def fetch_kernel(source, out, sem):
    copy = pltpu.make_async_copy(source, out, sem)
    copy.start()
    copy.wait()


def fetch(feats):
    return pl.pallas_call(
        fetch_kernel,
        out_shape=jax.ShapeDtypeStruct(feats.shape, BF),
        in_specs=[hbm()],
        out_specs=whole(feats.shape),
        scratch_shapes=[pltpu.SemaphoreType.DMA],
        compiler_params=VMEM,
        name="fetch_feats",
    )(feats)


def last(came, place, feats):
    shapes = ((feats.shape[0], CH), (feats.shape[1], CH))
    return pl.pallas_call(
        last_kernel,
        out_shape=tuple(jax.ShapeDtypeStruct(s, BF) for s in shapes),
        in_specs=[smem(), whole(came.shape), whole(feats.shape)],
        out_specs=tuple(whole(s) for s in shapes),
        scratch_shapes=[pltpu.VMEM((place.shape[0], CELLS, CH), BF)],
        compiler_params=VMEM,
        name="stride_term",
    )(place, came, feats)


def terms_kernel(stride, *refs):
    terms, out = refs[:-1], refs[-1]
    conv = sum(term[...].astype(F32) for term in terms)
    both = stride[...].astype(F32)
    out[:, 0] = jnp.concatenate([conv[:, :4], both[:, :4]], axis=1).astype(BF)
    out[:, 1] = jnp.concatenate([conv[:, 4:], both[:, 4:]], axis=1).astype(BF)


def put_together(stride, terms):
    shape = terms[0].shape
    arrays = (stride.reshape(shape),) + tuple(terms)
    return pl.pallas_call(
        terms_kernel,
        out_shape=jax.ShapeDtypeStruct((shape[0], 2) + shape[1:], BF),
        in_specs=[whole(shape) for a in arrays],
        out_specs=whole((shape[0], 2) + shape[1:]),
        compiler_params=VMEM,
        name="put_together",
    )(*arrays)


def to_all(buffer):
    return lax.all_to_all(buffer, ("gx", "gy"), split_axis=0, concat_axis=0, tiled=True)


def both_ways(first, last_part, axis):
    peers = lax.axis_size(axis)
    up = [(i, i + 1) for i in range(peers - 1)]
    down = [(i + 1, i) for i in range(peers - 1)]
    return lax.ppermute(last_part, axis, up), lax.ppermute(first, axis, down)


def label_codes(arrival_slot, labels):
    bricks = BX * BY * SZ // BR
    filled = jnp.any(
        (arrival_slot >> 3)[None, :] == jnp.arange(bricks, dtype=jnp.int32)[:, None], axis=1
    ).reshape(BX, 1, BY, 1, SZ // BR, 1)
    cells = labels.reshape(BX, BR, BY, BR, SZ // BR, BR)
    codes = jnp.where(filled, cells + 1, 0).reshape(SX, SY, SZ).astype(BF)
    return jnp.pad(codes, ((0, 0), (2, CODE - 2 - SY), (0, CH - SZ)))


def arrange(taps):
    side = taps[:, :, ::2].transpose(0, 1, 3, 2, 4).reshape(9 * CH, 2 * CH)
    middle = taps[:, :, 1]
    rest = ((0, 0),) * 3
    middle = jnp.stack(
        [jnp.pad(middle, ((0, 1),) + rest), jnp.pad(middle, ((1, 0),) + rest)], axis=3
    )
    return side, middle.reshape(12 * CH, 2 * CH)


def per_device(fine_feats, owner_of, arrival_slot, w_stride, w_conv, w_head, labels):
    devs = lax.axis_size("gx") * lax.axis_size("gy")
    per_dev, cells, in_width = fine_feats.shape
    cap = arrival_slot.shape[0] // devs
    feats = fine_feats.reshape(per_dev * cells, in_width)
    buffer, place = send(feats, owner_of, w_stride, devs, cap)

    brick, octant = arrival_slot >> 3, arrival_slot & 7
    deep = SZ // BR
    big_x = 2 * (brick // (BY * deep)) + (octant >> 2)
    big_y = 2 * (brick // deep % BY) + ((octant >> 1) & 1)
    big_z = 2 * (brick % deep) + (octant & 1)
    index = jnp.where(arrival_slot >= 0, (big_x * (SY // 2) + big_y) * (SZ // 2) + big_z, BRICKS)
    code = label_codes(arrival_slot, labels)
    order = brick_order()
    place, w_conv = lax.optimization_barrier((place, w_conv))
    taps = w_conv.reshape(3, 3, 3, CH, CH)
    w_fwd = arrange(taps)
    w_bwd = arrange(taps[::-1, ::-1].swapaxes(3, 4))
    head = jnp.pad(jnp.concatenate([w_head, w_head], axis=1), ((0, 0), (0, CH - 16)))

    arrived, w_fwd, w_bwd = lax.optimization_barrier((to_all(buffer), w_fwd, w_bwd))
    slab, first, last_part = land(arrived, index, order, code)
    before, after = both_ways(first, last_part, "gx")
    weights_fwd = w_fwd + (head, head.T)
    inside = inner(slab, weights_fwd)
    up, down = sides(slab, before, after, inside)
    left, right = both_ways(down, up, "gy")
    at_x = x_sides(slab, before, after, weights_fwd)
    returned, kept = core(
        jnp.minimum(index, BRICKS - 1),
        slab,
        before,
        after,
        left,
        right,
        inside,
        at_x,
        weights_fwd,
        w_bwd,
        order.T,
    )
    came = to_all(returned)
    half = (lax.axis_index("gy") % 2).astype(jnp.int32).reshape(1)
    terms = sum_over_gy(*weights(half, kept), devs)
    feats, first_term = lax.optimization_barrier((feats, terms[0]))
    terms = (first_term,) + tuple(terms[1:])
    feats = fetch(feats)
    came, feats = lax.optimization_barrier((came, feats))
    mine, stride = last(came, place, feats)
    terms, stride = lax.optimization_barrier((terms, stride))
    share = rows = 4
    terms = to_all(put_together(stride, terms).reshape(devs, rows + share, CH))
    grad_fine = lax.dot_general(
        mine, w_stride, (((1,), (1,)), ((), ())), preferred_element_type=F32
    ).astype(BF)
    terms = terms.astype(F32).reshape(lax.axis_size("gx"), -1, 2, rows + share, CH)
    by_part = jnp.sum(terms, axis=0)
    conv_sum = by_part[:, :, :rows].transpose(1, 0, 2, 3).reshape(2, -1, CH)
    stride_sum = jnp.sum(by_part[:, :, rows:], axis=(0, 1))
    block = jnp.concatenate(
        [conv_sum, jnp.broadcast_to(stride_sum, (2,) + stride_sum.shape)], axis=1
    ).astype(BF)
    block, grad_fine = lax.optimization_barrier((block, grad_fine))
    sums = to_all(jnp.broadcast_to(block, (devs // 2,) + block.shape).reshape(devs, -1, CH))
    scale = 1.0 / math.sqrt(per_dev * devs * cells)
    mine = sums[:, :-share].reshape(-1, CH)
    swap = [(i, i ^ 1) for i in range(lax.axis_size("gy"))]
    other = lax.ppermute(mine, "gy", swap)
    first_core = half[0] == 0
    grad_conv = jnp.concatenate(
        [
            jnp.where(first_core, mine, other),
            jnp.where(first_core, other, mine)[: 27 * CH - mine.shape[0]],
        ],
        axis=0,
    ).astype(F32).reshape(27, CH, CH) * scale
    grad_stride = sums[:, -share:].reshape(in_width, CH).astype(F32) * scale
    return (
        grad_fine.reshape(per_dev, cells, in_width),
        grad_stride,
        grad_conv,
    )


def solution(mesh):
    return jax.shard_map(
        per_device,
        mesh=mesh,
        in_specs=(
            P(("gx", "gy"), None, None),
            P(("gx", "gy")),
            P(("gx", "gy")),
            P(),
            P(),
            P(),
            P("gx", "gy", None),
        ),
        out_specs=(P(("gx", "gy"), None, None), P(), P()),
        check_vma=False,
    )
```

```python
import functools
import math

import jax
import jax.numpy as jnp
from jax import lax
from jax.experimental import pallas as pl
from jax.experimental.pallas import tpu as pltpu
from jax.sharding import PartitionSpec as P

BX = 2
BY = 2
BR = 4
SX = 8
SY = 8
SZ = 48
CH = 128
CELLS = 8
FX = SX + 4
FY = SY + 4
ROWS = SY * SZ
CODE = 16
SIDE = 2 * SZ
BRICKS = 384
KEPT = 84
PARTS = 8
VMEM = pltpu.CompilerParams(vmem_limit_bytes=24 * 1024 * 1024)
MOST_VMEM = pltpu.CompilerParams(vmem_limit_bytes=48 * 1024 * 1024)
ALL_VMEM = pltpu.CompilerParams(vmem_limit_bytes=63 * 1024 * 1024)
BF = jnp.bfloat16
F32 = jnp.float32


def whole(shape):
    return pl.BlockSpec(shape, lambda: (0,) * len(shape))


def anywhere():
    return pl.BlockSpec(memory_space=pl.ANY)


def smem():
    return pl.BlockSpec(memory_space=pltpu.SMEM)


def matmul(a, b):
    return jnp.dot(a, b, preferred_element_type=F32)


def iota(shape, dim):
    return lax.broadcasted_iota(jnp.int32, shape, dim)


def send_kernel(
    cap, owner_hbm, feats_hbm, w_hbm, buf_hbm, place, owner, feats, w_stride, rows, buf, count, sems
):
    per_dev = owner.shape[0]
    devs = count.shape[0]
    part = feats.shape[0] // PARTS
    copies = [
        pltpu.make_async_copy(owner_hbm, owner, sems.at[0]),
        pltpu.make_async_copy(w_hbm, w_stride, sems.at[1]),
    ] + [
        pltpu.make_async_copy(
            feats_hbm.at[pl.ds(i * part, part)], feats.at[pl.ds(i * part, part)], sems.at[2 + i]
        )
        for i in range(PARTS)
    ]
    for copy in copies:
        copy.start()

    for i in range(devs):
        count[i] = 0
    buf[...] = jnp.zeros_like(buf)
    copies[0].wait()

    def find(i):
        who = owner[i]
        pos = count[who]
        count[who] = pos + 1
        place[i] = who * cap + pos

    def put(i):
        buf[place[i]] = rows[i]

    copies[1].wait()
    bricks = per_dev // PARTS
    for i in range(PARTS + 1):
        if i < PARTS:
            copies[2 + i].wait()
            vals = matmul(feats[i * part : (i + 1) * part, :], w_stride[...])
            rows[i * bricks : (i + 1) * bricks] = vals.reshape(bricks, CELLS, CH).astype(BF)
            for j in range(i * bricks, (i + 1) * bricks):
                find(j)
        if i > 0:
            for j in range((i - 1) * bricks, i * bricks):
                put(j)
    out = pltpu.make_async_copy(buf, buf_hbm, sems.at[0])
    out.start()
    out.wait()


def hbm():
    return pl.BlockSpec(memory_space=pltpu.HBM)


def send(feats, owner, w_stride, devs, cap):
    per_dev = owner.shape[0]
    return pl.pallas_call(
        functools.partial(send_kernel, cap),
        out_shape=(
            jax.ShapeDtypeStruct((devs * cap, CELLS, CH), BF),
            jax.ShapeDtypeStruct((per_dev,), jnp.int32),
        ),
        in_specs=[hbm(), hbm(), hbm()],
        out_specs=(hbm(), smem()),
        scratch_shapes=[
            pltpu.SMEM((per_dev,), jnp.int32),
            pltpu.VMEM(feats.shape, BF),
            pltpu.VMEM(w_stride.shape, BF),
            pltpu.VMEM((per_dev, CELLS, CH), BF),
            pltpu.VMEM((devs * cap, CELLS, CH), BF),
            pltpu.SMEM((devs,), jnp.int32),
            pltpu.SemaphoreType.DMA((2 + PARTS,)),
        ],
        compiler_params=ALL_VMEM,
        name="send_bricks",
    )(owner, feats, w_stride)


def brick_order():
    row = iota((4 * SZ, 4 * SZ), 0)
    col = iota((4 * SZ, 4 * SZ), 1)
    z = row % SZ
    return (col == (z // 2) * 8 + (row // SZ) * 2 + z % 2).astype(BF)


def land_kernel(index, arrived, order, code, slab, first, last, held):
    held[...] = jnp.zeros_like(held)

    for j in range(index.shape[0]):
        held[index[j]] = arrived[j]
    deep = SZ // 2
    for big_x in range(SX // 2):
        for half in range(SY // 4):
            start = (big_x * (SY // 2) + 2 * half) * deep
            block = jnp.concatenate(
                [
                    held[at : at + deep].astype(F32).reshape(4 * SZ, CH)
                    for at in (start, start + deep)
                ],
                axis=1,
            ).astype(BF)
            moved = matmul(order[...], block).astype(BF)
            for i in range(2):
                for l in range(2):
                    piece = moved[(2 * i + l) * SZ : (2 * i + l + 1) * SZ]
                    for j in range(2):
                        row = (4 * half + 2 * j + l) * SZ
                        slab[2 * big_x + i, row : row + SZ, :] = piece[:, j * CH : (j + 1) * CH]
    slab[:, ROWS:, :] = code[...]
    first[...] = slab[:2]
    last[...] = slab[SX - 2 :]


def land(arrived, index, order, code):
    shapes = ((SX, ROWS + CODE, CH), (2, ROWS + CODE, CH), (2, ROWS + CODE, CH))
    return pl.pallas_call(
        land_kernel,
        out_shape=tuple(jax.ShapeDtypeStruct(s, BF) for s in shapes),
        in_specs=[smem(), whole(arrived.shape), whole(order.shape), whole(code.shape)],
        out_specs=tuple(whole(s) for s in shapes),
        scratch_shapes=[pltpu.VMEM((BRICKS + 8, CELLS, CH), BF)],
        compiler_params=ALL_VMEM,
        name="land_bricks",
    )(index, arrived, order, code)


def sides_kernel(slab, before, after, inside, up, down):
    row = iota((CODE // 2, CH), 0)
    none = jnp.zeros((CODE // 2, CH), F32)
    for x in range(FX):
        if x < 2:
            ref, at = before, x
        elif x < 2 + SX:
            ref, at = slab, x - 2
        else:
            ref, at = after, x - 2 - SX
        up[x, :SIDE, :] = ref[at, ROWS - SIDE : ROWS, :]
        down[x, :SIDE, :] = ref[at, :SIDE, :]
        codes = ref[at, ROWS:, :].astype(F32)
        upper = jnp.where(row < 2, codes[8:], 0.0)
        lower = jnp.where((row == 2) | (row == 3), codes[:8], 0.0)
        up[x, SIDE:, :] = jnp.concatenate([upper, none], axis=0).astype(BF)
        down[x, SIDE:, :] = jnp.concatenate([none, lower], axis=0).astype(BF)


def sides(slab, before, after, inside):
    shape = (FX, SIDE + CODE, CH)
    return pl.pallas_call(
        sides_kernel,
        out_shape=(jax.ShapeDtypeStruct(shape, BF),) * 2,
        in_specs=[whole(slab.shape), whole(before.shape), whole(after.shape), anywhere()],
        out_specs=(whole(shape),) * 2,
        compiler_params=VMEM,
        name="y_sides",
    )(slab, before, after, inside)


def shifted(vals, z, by):
    rows = vals.shape[0]
    turned = pltpu.roll(vals, by % rows, 0)
    return jnp.where(z == (0 if by == 1 else SZ - 1), 0.0, turned)


def spread_codes(blocks):
    eye = (iota((SZ, CH), 0) == iota((SZ, CH), 1)).astype(F32)
    return jnp.concatenate([eye * block for block in blocks], axis=0)


def convolve(columns, w_side, w_mid):
    sides = [
        jnp.concatenate([columns[i + e][f] for e in range(3) for f in range(3)], axis=1)
        for i in range(2)
    ]
    outer = matmul(jnp.concatenate(sides, axis=0), w_side)
    middle = matmul(jnp.concatenate([part for four in columns for part in four], axis=1), w_mid)
    middle = jnp.concatenate([middle[:, :CH], middle[:, CH:]], axis=0)
    return outer[:, :CH], middle, outer[:, CH:]


def front(columns, spread, w_side, w_mid, head, head_t):
    rows = spread.shape[0]
    lane = iota((rows, CH), 1)
    z = iota((rows // SZ, SZ, CH), 1).reshape(rows, CH)
    below, middle, above = convolve(columns, w_side, w_mid)
    pre = shifted(below, z, 1) + middle + shifted(above, z, -1)
    code = jnp.sum(spread, axis=1, keepdims=True)
    mask = code > 0.5
    pre = jnp.where(mask, pre, 0.0)
    gate = jax.nn.sigmoid(pre)
    logits = matmul((pre * gate).astype(BF), head)
    target = (code - 1.0 == (lane % 8).astype(F32)).astype(F32)
    grad_logits = jnp.where(mask, jax.nn.sigmoid(logits) - target, 0.0)
    high = grad_logits.astype(BF).astype(F32)
    terms = jnp.where(lane < 8, high, jnp.where(lane < 16, grad_logits - high, 0.0))
    grad_act = matmul(terms.astype(BF), head_t)
    return (grad_act * gate * (1.0 + pre * (1.0 - gate))).astype(BF)


INNER = (SY - 2) * SZ


def front_cost(slabs):
    flops = 2 * 9 * 3 * CH * CH * INNER * slabs
    return pl.CostEstimate(flops=flops, bytes_accessed=4 * 2**20, transcendentals=0)


def inner_kernel(slab, w_side, w_mid, head, head_t, grad):
    def step(pair, carry):
        x = 2 * pair
        columns = [[slab[x + i, f * SZ : f * SZ + INNER, :] for f in range(3)] for i in range(4)]
        blocks = []
        for i in range(2):
            codes = slab[x + i + 1, ROWS:, :].astype(F32)
            blocks += [codes[y : y + 1] for y in range(3, SY + 1)]
        vals = front(
            columns, spread_codes(blocks), w_side[...], w_mid[...], head[...], head_t[...]
        )
        for i in range(2):
            grad[x + i] = vals[i * INNER : (i + 1) * INNER]
        return carry

    lax.fori_loop(0, SX // 2 - 1, step, 0, unroll=SX // 2 - 1)


def inner(slab, weights):
    arrays = (slab,) + weights
    shape = (SX - 2, INNER, CH)
    return pl.pallas_call(
        inner_kernel,
        out_shape=jax.ShapeDtypeStruct(shape, BF),
        in_specs=[whole(a.shape) for a in arrays],
        out_specs=whole(shape),
        compiler_params=VMEM,
        cost_estimate=front_cost(SX - 2),
        name="grad_pre_inside",
    )(*arrays)


def x_sides_kernel(slab, before, after, w_side, w_mid, head, head_t, grad):
    def source(x):
        if x < 2:
            return before, x
        return (slab, x - 2) if x < SX + 2 else (after, x - SX - 2)

    for pair, x in enumerate((0, SX)):
        slabs = [source(x + i) for i in range(4)]
        columns = [
            [ref[at, f * SZ : f * SZ + INNER, :] for f in range(3)] for ref, at in slabs
        ]
        blocks = []
        for ref, at in slabs[1:3]:
            codes = ref[at, ROWS:, :].astype(F32)
            blocks += [codes[y : y + 1] for y in range(3, SY + 1)]
        vals = front(
            columns, spread_codes(blocks), w_side[...], w_mid[...], head[...], head_t[...]
        )
        for i in range(2):
            grad[2 * pair + i] = vals[i * INNER : (i + 1) * INNER]


def x_sides(slab, before, after, weights):
    arrays = (slab, before, after) + weights
    shape = (4, INNER, CH)
    return pl.pallas_call(
        x_sides_kernel,
        out_shape=jax.ShapeDtypeStruct(shape, BF),
        in_specs=[whole(a.shape) for a in arrays],
        out_specs=whole(shape),
        compiler_params=VMEM,
        cost_estimate=front_cost(4),
        name="grad_pre_x_sides",
    )(*arrays)


def core_kernel(
    index, slab, before, after, left, right, inside, at_x,
    w_side, w_mid, head, head_t, w_side_t, w_mid_t, order_t,
    back_hbm, kept_hbm, low, high, codes, grad, coarse, held, back, sems,
):
    middle = pl.ds(SIDE, ROWS)
    pairs = (
        (slab.at[:, pl.ds(0, ROWS)], kept_hbm.at[pl.ds(2, SX), middle]),
        (before.at[:, pl.ds(0, ROWS)], kept_hbm.at[pl.ds(0, 2), middle]),
        (after.at[:, pl.ds(0, ROWS)], kept_hbm.at[pl.ds(2 + SX, 2), middle]),
        (left.at[:, pl.ds(0, SIDE)], kept_hbm.at[pl.ds(0, FX), pl.ds(0, SIDE)]),
        (right.at[:, pl.ds(0, SIDE)], kept_hbm.at[pl.ds(0, FX), pl.ds(SIDE + ROWS, SIDE)]),
    )
    copies = [pltpu.make_async_copy(a, b, sems.at[i]) for i, (a, b) in enumerate(pairs)]
    for copy in copies:
        copy.start()
    for at, ref in ((0, before), (2, slab), (2 + SX, after)):
        many = ref.shape[0]
        low[at : at + many, SIDE:, :] = ref[:, :SIDE, :]
        high[at : at + many, :SIDE, :] = ref[:, ROWS - SIDE : ROWS, :]
        codes[at : at + many] = ref[:, ROWS:, :].astype(F32)
    low[:, :SIDE, :] = left[:, :SIDE, :]
    high[:, SIDE:, :] = right[:, :SIDE, :]
    codes[...] += left[:, SIDE:, :].astype(F32) + right[:, SIDE:, :].astype(F32)
    grad[:2, SIDE : SIDE + INNER, :] = at_x[:2]
    grad[2:SX, SIDE : SIDE + INNER, :] = inside[...]
    grad[SX:, SIDE : SIDE + INNER, :] = at_x[2:]

    z_own = iota((2 * SY, SZ, CH), 1).reshape(2 * ROWS, CH)

    def forward(pair, carry):
        x = 2 * pair
        columns = [
            [
                jnp.concatenate(
                    [ref[x + i, f * SZ : f * SZ + SIDE, :] for ref in (low, high)], axis=0
                )
                for f in range(3)
            ]
            for i in range(4)
        ]
        blocks = []
        for i in range(2):
            here = codes[x + i + 1]
            blocks += [here[y : y + 1] for y in (1, 2, SY + 1, SY + 2)]
        vals = front(
            columns, spread_codes(blocks), w_side[...], w_mid[...], head[...], head_t[...]
        )
        for i in range(2):
            grad[x + i, :SIDE, :] = vals[2 * i * SIDE : (2 * i + 1) * SIDE]
            grad[x + i, SIDE + INNER :, :] = vals[(2 * i + 1) * SIDE : (2 * i + 2) * SIDE]
        return carry

    lax.fori_loop(0, SX // 2 + 1, forward, 0, unroll=5)
    out = pltpu.make_async_copy(
        grad.at[pl.ds(1, SX), pl.ds(SZ, ROWS)],
        kept_hbm.at[pl.ds(FX, SX), pl.ds(0, ROWS)],
        sems.at[len(pairs)],
    )
    out.start()
    copies.append(out)

    def backward(pair, carry):
        x = 2 * pair
        columns = [[grad[x + i, f * SZ : f * SZ + ROWS, :] for f in range(3)] for i in range(4)]
        below, middle, above = convolve(columns, w_side_t[...], w_mid_t[...])
        vals = (shifted(below, z_own, -1) + middle + shifted(above, z_own, 1)).astype(BF)
        for i in range(2):
            coarse[x + i] = vals[i * ROWS : (i + 1) * ROWS]
        return carry

    lax.fori_loop(0, SX // 2, backward, 0, unroll=4)

    deep = SZ // 2
    for big_x in range(SX // 2):
        for half in range(SY // 4):
            block = jnp.concatenate(
                [
                    jnp.concatenate(
                        [
                            coarse[2 * big_x + i, (2 * big_y + l) * SZ : (2 * big_y + l + 1) * SZ, :]
                            for i in range(2)
                            for l in range(2)
                        ],
                        axis=0,
                    )
                    for big_y in (2 * half, 2 * half + 1)
                ],
                axis=1,
            )
            moved = matmul(order_t[...], block)
            for j in range(2):
                start = (big_x * (SY // 2) + 2 * half + j) * deep
                one = moved[:, j * CH : (j + 1) * CH].reshape(deep, CELLS, CH)
                held[start : start + deep] = one.astype(BF)

    part = index.shape[0] // PARTS
    for i in range(PARTS):
        for j in range(i * part, (i + 1) * part):
            back[j] = held[index[j]]
        rows = pl.ds(i * part, part)
        copy = pltpu.make_async_copy(back.at[rows], back_hbm.at[rows], sems.at[6 + i])
        copy.start()
        copies.append(copy)
    for copy in copies:
        copy.wait()


def core(
    index, slab, before, after, left, right, inside, at_x, weights, weights_t, order_t
):
    arrays = (slab, before, after, left, right, inside, at_x) + weights + weights_t + (order_t,)
    shapes = ((index.shape[0], CELLS, CH), (KEPT, FY * SZ, CH))
    return pl.pallas_call(
        core_kernel,
        out_shape=tuple(jax.ShapeDtypeStruct(s, BF) for s in shapes),
        in_specs=[smem()] + [whole(a.shape) for a in arrays],
        out_specs=(hbm(),) * 2,
        scratch_shapes=[
            pltpu.VMEM((FX, 2 * SIDE, CH), BF),
            pltpu.VMEM((FX, 2 * SIDE, CH), BF),
            pltpu.VMEM((FX, CODE, CH), F32),
            pltpu.VMEM((SX + 2, ROWS + SIDE, CH), BF),
            pltpu.VMEM((SX, ROWS, CH), BF),
            pltpu.VMEM((BRICKS, CELLS, CH), BF),
            pltpu.VMEM((index.shape[0], CELLS, CH), BF),
            pltpu.SemaphoreType.DMA((6 + PARTS,)),
        ],
        compiler_params=MOST_VMEM,
        name="conv_both_ways",
    )(index, *arrays)


def weights_kernel(half, kept_hbm, keep, give, kept, total, taps_out, sems):
    half_x = SX // 2
    copies = []
    for i, (at, many) in enumerate(
        ((0, half_x + 3), (FX, half_x), (half_x + 3, FX - half_x - 3), (FX + half_x, half_x))
    ):
        slabs = pl.ds(at, many)
        copies.append(pltpu.make_async_copy(kept_hbm.at[slabs], kept.at[slabs], sems.at[i]))
        copies[-1].start()
    z_own = iota((SY, SZ, CH), 1).reshape(ROWS, CH)
    total[...] = jnp.zeros_like(total)

    def add(x, carry):
        here = kept[FX + x, :ROWS, :]
        mid = here.astype(F32)
        grads = jnp.concatenate(
            [shifted(mid, z_own, -1).astype(BF), here, shifted(mid, z_own, 1).astype(BF)],
            axis=1,
        )
        for e in range(3):
            taps = jnp.concatenate(
                [kept[x + 1 + e, (1 + f) * SZ : (1 + f) * SZ + ROWS, :] for f in range(3)], axis=1
            )
            total[e] += lax.dot_general(
                taps, grads, (((0,), (0,)), ((), ())), preferred_element_type=F32
            )
        return carry

    for part in range(2):
        copies[2 * part].wait()
        copies[2 * part + 1].wait()
        lax.fori_loop(half_x * part, half_x * (part + 1), add, 0, unroll=2)
    for tap in range(27):
        e, f, g = tap // 9, tap // 3 % 3, tap % 3
        taps_out[tap] = total[e, f * CH : (f + 1) * CH, g * CH : (g + 1) * CH]
    taps_out[27:] = jnp.zeros((5, CH, CH), F32)
    mine = half[0]
    keep[...] = taps_out[pl.ds(16 * mine, 16)]
    give[...] = taps_out[pl.ds(16 * (1 - mine), 16)].astype(BF)


def weights(half, kept):
    shape = (16, CH, CH)
    return pl.pallas_call(
        weights_kernel,
        out_shape=(jax.ShapeDtypeStruct(shape, F32), jax.ShapeDtypeStruct(shape, BF)),
        in_specs=[smem(), hbm()],
        out_specs=(whole(shape),) * 2,
        scratch_shapes=[
            pltpu.VMEM((FX + SX, FY * SZ, CH), BF),
            pltpu.VMEM((3, 3 * CH, 3 * CH), F32),
            pltpu.VMEM((32, CH, CH), F32),
            pltpu.SemaphoreType.DMA((4,)),
        ],
        compiler_params=ALL_VMEM,
        cost_estimate=pl.CostEstimate(
            flops=2 * 27 * CH * CH * SX * ROWS, bytes_accessed=6 * 2**20, transcendentals=0
        ),
        name="conv_weight_grad",
    )(half, kept)


def pair_kernel(me, keep, got, *outs):
    both = keep[...] + got[...].astype(F32).reshape(keep.shape)
    for by, out in enumerate(outs):
        y = lax.rem(me[0] + by, len(outs))
        part = jnp.where(y < 2, both[:, :, 0], both[:, :, 1])
        low = jnp.concatenate([part[:, 0, :4], part[:, 1, :4]], axis=1)
        high = jnp.concatenate([part[:, 0, 4:], part[:, 1, 4:]], axis=1)
        out[...] = jnp.where(y % 2 == 0, low, high).astype(out.dtype)


def add_pair(y, keep, got, ring, devs):
    shape = (devs // 2, 8, CH)
    kinds = (F32,) + (BF,) * (ring - 1)
    keep = keep.reshape(devs // 2, 2, 2, 8, CH)
    got = got.reshape(devs, 16, CH)
    return pl.pallas_call(
        pair_kernel,
        out_shape=tuple(jax.ShapeDtypeStruct(shape, kind) for kind in kinds),
        in_specs=[smem(), whole(keep.shape), whole(got.shape)],
        out_specs=(whole(shape),) * ring,
        compiler_params=ALL_VMEM,
        name="add_pair",
    )(y, keep, got)


def sum_over_gy(keep, give, devs):
    me = lax.axis_index("gy")
    y = me // 2
    peers = lax.axis_size("gy")
    ring = peers // 2
    got = lax.ppermute(give, "gy", [(i, i ^ 1) for i in range(peers)])
    parts = add_pair(y.astype(jnp.int32).reshape(1), keep, got, ring, devs)
    perms = [[(i, (i + 2 * by) % peers) for i in range(peers)] for by in range(ring)]
    return parts[:1] + tuple(
        lax.ppermute(part, "gy", perm) for part, perm in zip(parts[1:], perms[1:])
    )


def last_kernel(place, came, feats, mine, stride, rows):
    per_dev = place.shape[0]

    for i in range(per_dev):
        rows[i] = came[place[i]]
    vals = rows[...].astype(F32).reshape(per_dev * CELLS, CH).astype(BF)
    mine[...] = vals
    stride[...] = lax.dot_general(
        feats[...], vals, (((0,), (0,)), ((), ())), preferred_element_type=F32
    ).astype(BF)


def fetch_kernel(source, out, sem):
    copy = pltpu.make_async_copy(source, out, sem)
    copy.start()
    copy.wait()


def fetch(feats):
    return pl.pallas_call(
        fetch_kernel,
        out_shape=jax.ShapeDtypeStruct(feats.shape, BF),
        in_specs=[hbm()],
        out_specs=whole(feats.shape),
        scratch_shapes=[pltpu.SemaphoreType.DMA],
        compiler_params=VMEM,
        name="fetch_feats",
    )(feats)


def last(came, place, feats):
    shapes = ((feats.shape[0], CH), (feats.shape[1], CH))
    return pl.pallas_call(
        last_kernel,
        out_shape=tuple(jax.ShapeDtypeStruct(s, BF) for s in shapes),
        in_specs=[smem(), whole(came.shape), whole(feats.shape)],
        out_specs=tuple(whole(s) for s in shapes),
        scratch_shapes=[pltpu.VMEM((place.shape[0], CELLS, CH), BF)],
        compiler_params=VMEM,
        name="stride_term",
    )(place, came, feats)


def terms_kernel(stride, *refs):
    terms, out = refs[:-1], refs[-1]
    conv = sum(term[...].astype(F32) for term in terms)
    both = stride[...].astype(F32)
    out[:, 0] = jnp.concatenate([conv[:, :4], both[:, :4]], axis=1).astype(BF)
    out[:, 1] = jnp.concatenate([conv[:, 4:], both[:, 4:]], axis=1).astype(BF)


def put_together(stride, terms):
    shape = terms[0].shape
    arrays = (stride.reshape(shape),) + tuple(terms)
    return pl.pallas_call(
        terms_kernel,
        out_shape=jax.ShapeDtypeStruct((shape[0], 2) + shape[1:], BF),
        in_specs=[whole(shape) for a in arrays],
        out_specs=whole((shape[0], 2) + shape[1:]),
        compiler_params=VMEM,
        name="put_together",
    )(*arrays)


def to_all(buffer):
    return lax.all_to_all(buffer, ("gx", "gy"), split_axis=0, concat_axis=0, tiled=True)


def both_ways(first, last_part, axis):
    peers = lax.axis_size(axis)
    up = [(i, i + 1) for i in range(peers - 1)]
    down = [(i + 1, i) for i in range(peers - 1)]
    return lax.ppermute(last_part, axis, up), lax.ppermute(first, axis, down)


def label_codes(arrival_slot, labels):
    bricks = BX * BY * SZ // BR
    filled = jnp.any(
        (arrival_slot >> 3)[None, :] == jnp.arange(bricks, dtype=jnp.int32)[:, None], axis=1
    ).reshape(BX, 1, BY, 1, SZ // BR, 1)
    cells = labels.reshape(BX, BR, BY, BR, SZ // BR, BR)
    codes = jnp.where(filled, cells + 1, 0).reshape(SX, SY, SZ).astype(BF)
    return jnp.pad(codes, ((0, 0), (2, CODE - 2 - SY), (0, CH - SZ)))


def arrange(taps):
    side = taps[:, :, ::2].transpose(0, 1, 3, 2, 4).reshape(9 * CH, 2 * CH)
    middle = taps[:, :, 1]
    rest = ((0, 0),) * 3
    middle = jnp.stack(
        [jnp.pad(middle, ((0, 1),) + rest), jnp.pad(middle, ((1, 0),) + rest)], axis=3
    )
    return side, middle.reshape(12 * CH, 2 * CH)


def per_device(fine_feats, owner_of, arrival_slot, w_stride, w_conv, w_head, labels):
    devs = lax.axis_size("gx") * lax.axis_size("gy")
    per_dev, cells, in_width = fine_feats.shape
    cap = arrival_slot.shape[0] // devs
    feats = fine_feats.reshape(per_dev * cells, in_width)
    buffer, place = send(feats, owner_of, w_stride, devs, cap)

    brick, octant = arrival_slot >> 3, arrival_slot & 7
    deep = SZ // BR
    big_x = 2 * (brick // (BY * deep)) + (octant >> 2)
    big_y = 2 * (brick // deep % BY) + ((octant >> 1) & 1)
    big_z = 2 * (brick % deep) + (octant & 1)
    index = jnp.where(arrival_slot >= 0, (big_x * (SY // 2) + big_y) * (SZ // 2) + big_z, BRICKS)
    code = label_codes(arrival_slot, labels)
    order = brick_order()
    place, w_conv = lax.optimization_barrier((place, w_conv))
    taps = w_conv.reshape(3, 3, 3, CH, CH)
    w_fwd = arrange(taps)
    w_bwd = arrange(taps[::-1, ::-1].swapaxes(3, 4))
    head = jnp.pad(jnp.concatenate([w_head, w_head], axis=1), ((0, 0), (0, CH - 16)))

    arrived, w_fwd, w_bwd = lax.optimization_barrier((to_all(buffer), w_fwd, w_bwd))
    slab, first, last_part = land(arrived, index, order, code)
    before, after = both_ways(first, last_part, "gx")
    weights_fwd = w_fwd + (head, head.T)
    inside = inner(slab, weights_fwd)
    up, down = sides(slab, before, after, inside)
    left, right = both_ways(down, up, "gy")
    at_x = x_sides(slab, before, after, weights_fwd)
    returned, kept = core(
        jnp.minimum(index, BRICKS - 1),
        slab,
        before,
        after,
        left,
        right,
        inside,
        at_x,
        weights_fwd,
        w_bwd,
        order.T,
    )
    came = to_all(returned)
    half = (lax.axis_index("gy") % 2).astype(jnp.int32).reshape(1)
    terms = sum_over_gy(*weights(half, kept), devs)
    feats, first_term = lax.optimization_barrier((feats, terms[0]))
    terms = (first_term,) + tuple(terms[1:])
    feats = fetch(feats)
    came, feats = lax.optimization_barrier((came, feats))
    mine, stride = last(came, place, feats)
    terms, stride = lax.optimization_barrier((terms, stride))
    share = rows = 4
    terms = to_all(put_together(stride, terms).reshape(devs, rows + share, CH))
    grad_fine = lax.dot_general(
        mine, w_stride, (((1,), (1,)), ((), ())), preferred_element_type=F32
    ).astype(BF)
    terms = terms.astype(F32).reshape(lax.axis_size("gx"), -1, 2, rows + share, CH)
    by_part = jnp.sum(terms, axis=0)
    conv_sum = by_part[:, :, :rows].transpose(1, 0, 2, 3).reshape(2, -1, CH)
    stride_sum = jnp.sum(by_part[:, :, rows:], axis=(0, 1))
    block = jnp.concatenate(
        [conv_sum, jnp.broadcast_to(stride_sum, (2,) + stride_sum.shape)], axis=1
    ).astype(BF)
    block, grad_fine = lax.optimization_barrier((block, grad_fine))
    sums = to_all(jnp.broadcast_to(block, (devs // 2,) + block.shape).reshape(devs, -1, CH))
    scale = 1.0 / math.sqrt(per_dev * devs * cells)
    mine = sums[:, :-share].reshape(-1, CH)
    swap = [(i, i ^ 1) for i in range(lax.axis_size("gy"))]
    other = lax.ppermute(mine, "gy", swap)
    first_core = half[0] == 0
    grad_conv = jnp.concatenate(
        [
            jnp.where(first_core, mine, other),
            jnp.where(first_core, other, mine)[: 27 * CH - mine.shape[0]],
        ],
        axis=0,
    ).astype(F32).reshape(27, CH, CH) * scale
    grad_stride = sums[:, -share:].reshape(in_width, CH).astype(F32) * scale
    return (
        grad_fine.reshape(per_dev, cells, in_width),
        grad_stride,
        grad_conv,
    )


def solution(mesh):
    return jax.shard_map(
        per_device,
        mesh=mesh,
        in_specs=(
            P(("gx", "gy"), None, None),
            P(("gx", "gy")),
            P(("gx", "gy")),
            P(),
            P(),
            P(),
            P("gx", "gy", None),
        ),
        out_specs=(P(("gx", "gy"), None, None), P(), P()),
        check_vma=False,
    )
```
